32 devices in a mesh: dp: 16 (over z, x, core), shard: 2 (over y).
Axes of the slice: x: 2, y: 2, z: 4, core: 2. Of those that a mesh axis runs over, the one named last changes fastest.
Arguments:
- group_grads: bfloat16 [16, 1024, 1024], P('dp', 'shard'), may hold values from -2 to 2
- moment: float32 [1024, 1024], P('shard'), may hold values from -6 to 6
- second: float32 [1024, 1024], P(None, 'shard'), may hold values from 0.5 to 4
- stat_left: float32 [1024, 1024], P('shard'), may hold values from -200 to 2000, as said below
- stat_right: float32 [1024, 1024], P('shard'), may hold values from -200 to 2000, as said below
- basis_left: float32 [1024, 1024], P('shard'), as said below
- basis_right: float32 [1024, 1024], P('shard'), as said below
Outputs:
- update: bfloat16 [1024, 1024], P('shard')
- second_new: float32 [1024, 1024], P(None, 'shard')
- left_new: float32 [1024, 1024], P('shard')
- right_new: float32 [1024, 1024], P('shard')
The draws below stay inside these ranges and needn't reach their ends.
Inputs may be any that keep to these rules, and one draw needn't show every extreme that they name: `stat_left`: each statistic is symmetric. `stat_right`: each statistic is symmetric. `basis_left`: diagonal entries near 0.9 sqrt(1024), off-diagonal entries of order one. `basis_right`: diagonal entries near 0.9 sqrt(1024), off-diagonal entries of order one.
All inputs are finite; a program needn't handle non-finite values.
Results may differ from the reference program's by a relative error of at most 0.0049.
The reference program's roundings to bfloat16 on the way count: a program that leaves them out, or rounds other values in their place, can miss the bound.
Values may be sent and summed in bfloat16 or wider, within the bound.
No kernel may reach another device: no remote copies, remote signals or barrier semaphores. Data moves between devices by JAX's collectives and lax.ppermute only.
A program may use at most 128 MiB of HBM per device.

```python
import math
import jax
import jax.numpy as jnp
from jax import lax

B = 1024
NS_ITERS = 2
N_DP = 16


def statistic_draw(key):
    key_noise, key_rough = jax.random.split(key, 2)
    position = jnp.arange(B).astype(jnp.float32)
    noise = jnp.clip(jax.random.normal(key_noise, (B, B), jnp.float32), -3.0, 3.0)
    rough = jax.random.uniform(key_rough, (B,), jnp.float32, -0.35, 0.35)
    ramp = 1.0 + 3.0 * position / B
    symmetric = (noise + noise.T) * (0.35 / math.sqrt(B))
    scales = jnp.sqrt(ramp) * jnp.exp(rough)
    identity = (position[:, None] == position[None, :]).astype(jnp.float32)
    return 100.0 * scales[:, None] * scales[None, :] * (identity + symmetric)


def basis_draw(key):
    position = jnp.arange(B).astype(jnp.float32)
    noise = jnp.clip(0.45 * jax.random.normal(key, (B, B), jnp.float32), -2.5, 2.5)
    identity = (position[:, None] == position[None, :]).astype(jnp.float32)
    return 0.9 * math.sqrt(B) * identity + noise


def draw_stat_left(key, part):
    return statistic_draw(jax.random.fold_in(key, 11))


def draw_stat_right(key, part):
    return statistic_draw(jax.random.fold_in(key, 12))


def draw_basis_left(key, part):
    return basis_draw(jax.random.fold_in(key, 21))


def draw_basis_right(key, part):
    return basis_draw(jax.random.fold_in(key, 22))


def spiked(drawn, own_key, source, target, shards_of, factor):
    owner, partner = [(jnp.arange(drawn.shape[dim]) // (drawn.shape[dim] // shards_of)).reshape([-1 if axis == dim else 1 for axis in range(drawn.ndim)]) for dim in (source, target)]
    chosen = jax.random.permutation(own_key, shards_of)[partner]
    strong = (owner == chosen) | (owner == (partner + shards_of // 2) % shards_of)
    return jnp.where(strong, factor * drawn, drawn)


def levels(key, extent, cuts, low, largest):
    factor_of, own = 1.0, jax.random.fold_in(key, 6)
    for axis_at, blocks in cuts:
        steps = jnp.exp(jax.random.uniform(jax.random.fold_in(own, axis_at), (blocks,), jnp.float32, low / len(cuts), largest / len(cuts)))
        factor_of = factor_of * jnp.repeat(steps, extent[axis_at] // blocks).reshape([-1 if axis == axis_at else 1 for axis in range(len(extent))])
    return factor_of


def centred(own_key, extent, deviation, reach, cuts=(), dtype=jnp.bfloat16):
    entries = jax.random.normal(own_key, extent, jnp.float32) * deviation
    if len(cuts) > 0:
        entries = levels(own_key, extent, cuts, -0.22, 0.18) * entries
    return jnp.clip(entries, min=-reach, max=reach).astype(dtype)


def gaussian_with(stream_key, extent, width, most, cuts, heavy, held_as=jnp.bfloat16):
    entries = width * jax.random.normal(stream_key, extent, jnp.float32)
    if cuts:
        entries = entries * levels(stream_key, extent, cuts, -0.22, 0.18)
    return jnp.clip(spiked(entries, jax.random.fold_in(stream_key, 3), *heavy), -most, most).astype(held_as)


def setup_inputs(seed: int = 0) -> dict:
    key_list = jax.random.split(jax.random.key(seed), 8)
    return {
        "group_grads": gaussian_with(key_list[0], (N_DP, B, B), N_DP ** -0.5, 2.0, ((0, 16), (1, 2)), (0, 2, 16, 2.0)),
        "moment": centred(key_list[1], (B, B), 1.0, 6.0, ((0, 2),), jnp.float32),
        "second": jnp.clip(jnp.exp(math.log(4.0) - 2.0794415 * jax.random.uniform(key_list[2], (B, B), jnp.float32) ** levels(key_list[2], (B, B), ((1, 2),), -0.2, 0.2)), 0.5, 4.0),
        "stat_left": draw_stat_left(jax.random.fold_in(key_list[7], 71), 0),
        "stat_right": draw_stat_right(jax.random.fold_in(key_list[7], 71), 0),
        "basis_left": draw_basis_left(jax.random.fold_in(key_list[7], 71), 0),
        "basis_right": draw_basis_right(jax.random.fold_in(key_list[7], 71), 0),
    }


BETA_ONE = 0.9
BETA_TWO = 0.9
BETA_STAT = 0.95
EPSILON = 1e-08
NORM_EPS = 1e-06

def orthogonalize(statistic, basis_half):
    product = jnp.dot(statistic.astype(jnp.bfloat16), basis_half, preferred_element_type=jnp.float32)
    scaled = product / jnp.sqrt(lax.optimization_barrier(jnp.mean(product * product, axis=0)) + NORM_EPS)
    current = scaled.astype(jnp.bfloat16)
    result = scaled
    for iteration in range(NS_ITERS):
        gram = (jnp.dot(current, current.T, preferred_element_type=jnp.float32) / B).astype(jnp.bfloat16)
        result = 1.5 * current.astype(jnp.float32) - 0.5 * jnp.dot(gram, current, preferred_element_type=jnp.float32)
        if iteration + 1 < NS_ITERS:
            current = result.astype(jnp.bfloat16)
    return result

def reference(group_grads, moment, second, stat_left, stat_right, basis_left, basis_right):
    summed = lax.optimization_barrier(jnp.sum(group_grads.astype(jnp.float32), axis=0))
    gradient = summed.astype(jnp.bfloat16)
    moment_half = (BETA_ONE * moment + (1.0 - BETA_ONE) * gradient.astype(jnp.float32)).astype(jnp.bfloat16)
    left_stat = BETA_STAT * stat_left + (1.0 - BETA_STAT) * jnp.dot(gradient, gradient.T, preferred_element_type=jnp.float32)
    right_stat = BETA_STAT * stat_right + (1.0 - BETA_STAT) * jnp.dot(gradient.T, gradient, preferred_element_type=jnp.float32)
    left_rot = basis_left.astype(jnp.bfloat16)
    right_rot = basis_right.astype(jnp.bfloat16)
    grad_turned = jnp.dot(gradient, right_rot, preferred_element_type=jnp.float32).astype(jnp.bfloat16)
    moment_turned = jnp.dot(moment_half, right_rot, preferred_element_type=jnp.float32).astype(jnp.bfloat16)
    grad_rot = jnp.dot(left_rot.T, grad_turned, preferred_element_type=jnp.float32) / B
    moment_rot = jnp.dot(left_rot.T, moment_turned, preferred_element_type=jnp.float32) / B
    second_new = BETA_TWO * second + (1.0 - BETA_TWO) * grad_rot * grad_rot
    scaled = (moment_rot / (jnp.sqrt(second_new) + EPSILON)).astype(jnp.bfloat16)
    turned_back = jnp.dot(left_rot, scaled, preferred_element_type=jnp.float32).astype(jnp.bfloat16)
    update = (jnp.dot(turned_back, right_rot.T, preferred_element_type=jnp.float32) / B).astype(jnp.bfloat16)
    left_new = orthogonalize(left_stat, left_rot)
    right_new = orthogonalize(right_stat, right_rot)
    return (update, second_new, left_new, right_new)
```

```python
import functools

import jax
import jax.numpy as jnp
from jax import lax
from jax.experimental import pallas as pl
from jax.experimental.pallas import tpu as pltpu
from jax.sharding import PartitionSpec as P

NS_ITERS = 2


BETA_ONE = 0.9
BETA_TWO = 0.9
BETA_STAT = 0.95
EPSILON = 1e-08
NORM_EPS = 1e-06
HALF = jnp.bfloat16
FULL = jnp.float32
VMEM = pl.BlockSpec(memory_space=pltpu.VMEM)
ANY = pl.BlockSpec(memory_space=pl.ANY)
SMEM = pl.BlockSpec(memory_space=pltpu.SMEM)


def matmul(left_mat, right_mat, left_dim=1, right_dim=0):
    return lax.dot_general(
        left_mat,
        right_mat,
        (((left_dim,), (right_dim,)), ((), ())),
        preferred_element_type=FULL,
    )


def shaped(shape, dtype):
    return jax.ShapeDtypeStruct(shape, dtype)


def tile(index, size):
    return pl.ds(pl.multiple_of(index * size, size), size)


def call(kernel, outs, operands, specs, scratch=(), flops=0, moved=0):
    return pl.pallas_call(
        kernel,
        out_shape=outs,
        in_specs=specs,
        out_specs=[VMEM] * len(outs),
        scratch_shapes=list(scratch),
        compiler_params=pltpu.CompilerParams(vmem_limit_bytes=50 * 2**20),
        cost_estimate=pl.CostEstimate(flops=flops, bytes_accessed=moved, transcendentals=0),
    )(*operands)


def state_parts_kernel(where, left, right, stat_left, stat_right, bases, stats):
    half = left.shape[0] // 2
    rows = left.shape[0]
    near = tile(where[0], rows)
    mine = tile(where[1], half)
    bases[:half] = left[mine].astype(HALF)
    bases[half:] = right[mine].astype(HALF)
    stats[:, :rows] = stat_left[mine, near]
    stats[:, rows:] = stat_right[mine, near]


def first_sum_kernel(where, group, came, kept, sent):
    size = kept.shape[0]
    core, x = where[1], where[2]
    kept[...] = group[0, tile(core * 2 + x, size)].astype(FULL) + came[tile(x, size)].astype(FULL)
    sent[...] = group[0, tile(core * 2 + 1 - x, size)].astype(FULL) + came[
        tile(1 - x, size)
    ].astype(FULL)


def second_sum_kernel(where, kept, came, own, *sent):
    size = own.shape[0]
    z = where[3]
    own[...] = kept[tile(z, size)] + came[tile(z, size)]
    for k, out in enumerate(sent):
        there = tile(z ^ (k + 1), size)
        out[...] = kept[there] + came[there]


def third_sum_kernel(own, one, two, three, out):
    out[...] = ((own[...] + one[...]) + (two[...] + three[...])).astype(HALF)


def joined_kernel(where, *refs):
    out = refs[-1]
    z = where[3]
    size = refs[0].shape[0]
    for k, part in enumerate(refs[:-1]):
        out[tile(z ^ k, size)] = part[...]


def place_basis(where, out, own, mine, theirs, begin, natural):
    rows = own.shape[0]
    half = rows // 2
    position, core = where[0], where[1]
    first = position if natural else 0
    out[tile(first, rows)] = own[...].astype(HALF)
    other = (1 - first) * 2
    out[tile(other + core, half)] = mine[begin : begin + half]
    out[tile(other + 1 - core, half)] = theirs[begin : begin + half]


def place_stat(where, out, own, mine, theirs, begin, natural):
    rows = own.shape[0]
    half = rows // 2
    position, core = where[0], where[1]
    first = position if natural else 0
    here, there = tile(first, rows), tile(1 - first, rows)
    out[here, here] = own[:, tile(position, rows)]
    cross = own[:, tile(1 - position, rows)]
    out[here, there] = cross
    out[there, here] = cross.T
    other = (1 - first) * 2
    out[tile(other + core, half), there] = mine[:, begin : begin + rows]
    out[tile(other + 1 - core, half), there] = theirs[:, begin : begin + rows]


def left_state_kernel(where, basis, bmine, btheirs, stat, smine, stheirs, rot, turned, full):
    place_basis(where, rot, basis, bmine, btheirs, 0, False)
    place_stat(where, full, stat, smine, stheirs, 0, False)
    turned[...] = rot[...].T


def right_state_kernel(where, basis, bmine, btheirs, stat, smine, stheirs, rot, near, full):
    rows = basis.shape[0]
    place_basis(where, rot, basis, bmine, btheirs, rows // 2, True)
    place_stat(where, full, stat, smine, stheirs, rows, True)
    near[:, :rows] = rot[:, tile(where[0], rows)]
    near[:, rows:] = rot[:, tile(1 - where[0], rows)]


def moment_kernel(where, moment, near, *refs):
    parts, (gradient, ours, others, sem) = refs[:-4], refs[-4:]
    core, x = where[1], where[2]
    size = parts[0].shape[0]
    rows = moment.shape[0]
    copies = []
    for place, part in enumerate(parts):
        block = (
            (place // 4) * 4 + (core ^ (place % 4 // 2)) * 2 + (x ^ (place % 2))
        )
        copies.append(
            pltpu.make_async_copy(part, gradient.at[tile(block, size)], sem.at[place])
        )
    for copy in copies:
        copy.start()
    for copy in copies:
        copy.wait()
    step = rows // 2

    @pl.loop(0, 2)
    def _(i):
        here = tile(i, step)
        half = (
            BETA_ONE * moment[here] + (1.0 - BETA_ONE) * gradient[here].astype(FULL)
        ).astype(HALF)
        ours[here] = matmul(half, near[:, :rows]).astype(HALF)
        others[here] = matmul(half, near[:, rows:]).astype(HALF)


def adam_kernel(gradient, near, rot, turned, mine, came, second, new, kept, sent, block, scaled):
    width = gradient.shape[0]
    rows = mine.shape[0]
    step = width // 4

    @pl.loop(0, 4)
    def _(i):
        here = tile(i, step)
        block[here] = matmul(gradient[here], near[:, :rows]).astype(HALF)

    @pl.loop(0, 4)
    def _(i):
        here = tile(i, step)
        grad_rot = matmul(turned[here], block[...]) * (1.0 / width)
        moment_rot = (
            matmul(turned[here, :rows], mine[...]) + matmul(turned[here, rows:], came[...])
        ) * (1.0 / width)
        value = BETA_TWO * second[here] + (1.0 - BETA_TWO) * grad_rot * grad_rot
        new[here] = value
        scaled[here] = (moment_rot / (jnp.sqrt(value) + EPSILON)).astype(HALF)

    @pl.loop(0, rows // step)
    def _(i):
        here = tile(i, step)
        kept[here] = matmul(rot[here], scaled[...]).astype(HALF)
        sent[here] = matmul(rot[tile(i + rows // step, step)], scaled[...]).astype(HALF)


def update_kernel(mine, came, near, out):
    rows, width = out.shape
    step = rows // 2

    @pl.loop(0, 2)
    def _(i):
        here = tile(i, step)
        total = matmul(mine[here], near[:, :rows], 1, 1) + matmul(
            came[here], near[:, rows:], 1, 1
        )
        out[here] = (total * (1.0 / width)).astype(HALF)


def refresh_kernel(natural, where, gradient, rot, stat, out, stat_in, turned, half, product, sem):
    width = gradient.shape[0]
    rows = out.shape[0]
    steps = 4
    step = width // steps
    copies = [
        pltpu.make_async_copy(stat.at[tile(i, step)], stat_in.at[tile(i, step)], sem.at[i])
        for i in range(steps)
    ]
    for copy in copies:
        copy.start()
    if natural:

        @pl.loop(0, steps)
        def _(i):
            turned[:, tile(i, step)] = gradient[tile(i, step)].T

        source, dim = turned, 0
    else:
        source, dim = gradient, 1
    for copy in copies:
        copy.wait()

    @pl.loop(0, steps)
    def _(i):
        here = tile(i, step)
        grads = matmul(source[here], gradient[...], 1, dim)
        half[here] = (BETA_STAT * stat_in[here] + (1.0 - BETA_STAT) * grads).astype(HALF)

    def power(i, total):
        here = tile(i, step)
        value = matmul(half[here], rot[...])
        product[here] = value
        return total + jnp.sum(value * value, axis=0, keepdims=True)

    total = lax.fori_loop(0, steps, power, jnp.zeros((1, width), FULL))
    scale = lax.rsqrt(total * (1.0 / width) + NORM_EPS)

    @pl.loop(0, steps)
    def _(i):
        here = tile(i, step)
        half[here] = (product[here] * scale).astype(HALF)

    def improved(current, here):
        gram = (matmul(current[here], current[...], 1, 1) * (1.0 / width)).astype(HALF)
        return 1.5 * current[here].astype(FULL) - 0.5 * matmul(gram, current[...])

    current, following = half, turned
    for _ in range(NS_ITERS - 1):

        @pl.loop(0, steps)
        def _(i):
            here = tile(i, step)
            following[here] = improved(current, here).astype(HALF)

        current, following = following, current

    first = where[0] * (rows // step) if natural else 0

    @pl.loop(0, rows // step)
    def _(i):
        out[tile(i, step)] = improved(current, tile(first + i, step))


def fast_body(group_grads, moment, second, stat_left, stat_right, basis_left, basis_right):
    position = lax.axis_index("shard")
    member = lax.axis_index("dp")
    rows, width = moment.shape
    half = rows // 2
    quarter = rows // 4
    chunk = rows // 16
    core, x, z = member & 1, (member >> 1) & 1, member >> 2
    where = jnp.stack([position, core, x, z]).astype(jnp.int32)
    unit = 2 * width**3

    def dp_swap(value, distance):
        return lax.ppermute(value, "dp", [(i, i ^ distance) for i in range(16)])

    def shard_swap(value):
        return lax.ppermute(value, "shard", [(0, 1), (1, 0)])

    def cross_swap(value):
        pairs = [(i, i ^ 5) for i in range(32)]
        return lax.ppermute(value, ("dp", "shard"), pairs)

    bases_sent, stats_sent = call(
        state_parts_kernel,
        [shaped((rows, width), HALF), shaped((half, width), FULL)],
        (where, basis_left, basis_right, stat_left, stat_right),
        [SMEM] + [VMEM] * 4,
        moved=2**23,
    )
    bases_mine = shard_swap(bases_sent)
    stats_mine = shard_swap(stats_sent)

    raw = lax.dynamic_slice_in_dim(group_grads[0], (1 - core) * half, half, 0)
    came = dp_swap(raw, 1)
    kept, sent = call(
        first_sum_kernel,
        [shaped((quarter, width), FULL)] * 2,
        (where, group_grads, came),
        [SMEM, VMEM, VMEM],
        moved=2**21,
    )
    came = dp_swap(sent, 2)
    own, *sent = call(
        second_sum_kernel,
        [shaped((chunk, width), FULL)] * 4,
        (where, kept, came),
        [SMEM, VMEM, VMEM],
        moved=2**20,
    )
    pieces = [dp_swap(value, 4 * (k + 1)) for k, value in enumerate(sent)]
    (piece,) = call(
        third_sum_kernel, [shaped((chunk, width), HALF)], (own, *pieces), [VMEM] * 4, moved=2**19
    )
    pieces = [piece] + [dp_swap(piece, 4 * k) for k in (1, 2, 3)]
    (part,) = call(
        joined_kernel, [shaped((quarter, width), HALF)], (where, *pieces), [SMEM] + [VMEM] * 4,
        moved=2**19,
    )
    parts = [part, dp_swap(part, 2), shard_swap(part), cross_swap(part)]
    swapped = [dp_swap(value, 1) for value in parts]

    bases_theirs = dp_swap(bases_mine, 1)
    stats_theirs = dp_swap(stats_mine, 1)
    bases = (bases_mine, bases_theirs)
    stats = (stats_mine, stats_theirs)
    state_outs = [
        shaped((width, width), HALF),
        shaped((width, width), HALF),
        shaped((width, width), FULL),
    ]
    left_rot, left_turned, left_stat = call(
        left_state_kernel,
        state_outs,
        (where, basis_left, *bases, stat_left, *stats),
        [SMEM] + [VMEM] * 6,
        moved=2**24,
    )
    right_rot, right_near, right_stat = call(
        right_state_kernel,
        state_outs,
        (where, basis_right, *bases, stat_right, *stats),
        [SMEM] + [VMEM] * 6,
        moved=2**24,
    )

    ordered = [parts[0], parts[1], swapped[0], swapped[1], parts[2], parts[3], swapped[2], swapped[3]]
    gradient, moment_mine, moment_sent = call(
        moment_kernel,
        [shaped((width, width), HALF)] + [shaped((rows, rows), HALF)] * 2,
        (where, moment, right_near, *ordered),
        [SMEM, VMEM, VMEM] + [ANY] * 8,
        [pltpu.SemaphoreType.DMA((8,))],
        flops=unit // 2,
        moved=2**23,
    )
    moment_came = shard_swap(moment_sent)

    def refreshed(natural, rot, stat):
        (out,) = call(
            functools.partial(refresh_kernel, natural),
            [shaped((rows, width), FULL)],
            (where, gradient, rot, stat),
            [SMEM, VMEM, VMEM, ANY],
            [
                pltpu.VMEM((width, width), FULL),
                pltpu.VMEM((width, width), HALF),
                pltpu.VMEM((width, width), HALF),
                pltpu.VMEM((width, width), FULL),
                pltpu.SemaphoreType.DMA((4,)),
            ],
            flops=5 * unit,
            moved=2**23,
        )
        return out

    left_new = refreshed(False, left_rot, left_stat)
    second_new, back_mine, back_sent = call(
        adam_kernel,
        [shaped((width, rows), FULL)] + [shaped((rows, rows), HALF)] * 2,
        (gradient, right_near, left_rot, left_turned, moment_mine, moment_came, second),
        [VMEM] * 7,
        [pltpu.VMEM((width, rows), HALF)] * 2,
        flops=2 * unit,
        moved=2**23,
    )
    back_came = shard_swap(back_sent)
    right_new = refreshed(True, right_rot, right_stat)
    (update,) = call(
        update_kernel,
        [shaped((rows, width), HALF)],
        (back_mine, back_came, right_near),
        [VMEM] * 3,
        flops=unit // 2,
        moved=2**22,
    )
    return (update, second_new, left_new, right_new)


def make_plain_body(n_dp, n_shard):
    def swap(value, axis, distance):
        size = n_dp if axis == "dp" else n_shard
        return lax.ppermute(value, axis, [(i, i ^ distance) for i in range(size)])

    dp_bits = []
    bit = 1
    while bit < n_dp:
        dp_bits.append(bit)
        bit *= 2

    def ordered(first_is_low, own, other, dim):
        return jnp.where(
            first_is_low,
            jnp.concatenate([own, other], dim),
            jnp.concatenate([other, own], dim),
        )

    def body(group_grads, moment, second, stat_left, stat_right, basis_left, basis_right):
        position = lax.axis_index("shard")
        member = lax.axis_index("dp")
        rows, width = moment.shape
        core = member & 1
        half = rows // 2

        def near_columns(value):
            blocks = [
                lax.dynamic_slice_in_dim(value, (position ^ k) * rows, rows, 1)
                for k in range(n_shard)
            ]
            return jnp.concatenate(blocks, 1)

        def fetch(value, distance):
            size = value.shape[0] // 2
            part = lax.dynamic_slice_in_dim(value, core * size, size, 0)
            part = swap(part, "shard", distance)
            other = swap(part, "dp", 1)
            return ordered(core == 0, part, other, 0)

        left_own = basis_left.astype(jnp.bfloat16)
        right_own = basis_right.astype(jnp.bfloat16)
        left_rot = jnp.concatenate([left_own] + [fetch(left_own, k) for k in range(1, n_shard)], 0)
        right_rot = jnp.concatenate(
            [right_own] + [fetch(right_own, k) for k in range(1, n_shard)], 0
        )

        def whole_stat(stat):
            own = near_columns(stat)
            blocks = [own[:, b * rows : (b + 1) * rows] for b in range(n_shard)]
            bands = [own]
            for k in range(1, n_shard):
                others = [b for b in range(n_shard) if b != k]
                sent = jnp.concatenate([blocks[b] for b in others], 1).astype(jnp.bfloat16)
                came = fetch(sent, k).astype(jnp.float32)
                band = [None] * n_shard
                band[0] = blocks[k].T
                for place, b in enumerate(others):
                    band[k ^ b] = came[:, place * rows : (place + 1) * rows]
                bands.append(jnp.concatenate(band, 1))
            return jnp.concatenate(bands, 0)

        stat_left_full = whole_stat(stat_left)
        stat_right_full = whole_stat(stat_right)

        part = group_grads[0]
        for bit in dp_bits:
            size = part.shape[0] // 2
            high = (member & bit) // bit
            kept = lax.dynamic_slice_in_dim(part, high * size, size, 0)
            sent = lax.dynamic_slice_in_dim(part, (1 - high) * size, size, 0)
            part = kept.astype(jnp.float32) + swap(sent, "dp", bit).astype(jnp.float32)
        chunk = part.astype(jnp.bfloat16)[None]
        chunk = jnp.concatenate([chunk] + [swap(chunk, "shard", k) for k in range(1, n_shard)], 0)
        for bit in reversed(dp_bits):
            chunk = ordered((member & bit) == 0, chunk, swap(chunk, "dp", bit), 1)
        gradient = near_columns(chunk.reshape(width, width))

        grad_rows = gradient[:rows].astype(jnp.float32)
        moment_half = (
            BETA_ONE * near_columns(moment) + (1.0 - BETA_ONE) * grad_rows
        ).astype(jnp.bfloat16)
        near_rot = near_columns(right_rot)
        moment_turned = matmul(moment_half, near_rot).astype(jnp.bfloat16)
        moment_block = jnp.concatenate(
            [moment_turned[:, :rows]]
            + [
                swap(moment_turned[:, k * rows : (k + 1) * rows], "shard", k)
                for k in range(1, n_shard)
            ],
            0,
        )
        grad_block = matmul(gradient, near_rot[:, :rows]).astype(jnp.bfloat16)
        grad_rot = matmul(left_rot, grad_block, 0) / width
        moment_rot = matmul(left_rot, moment_block, 0) / width
        second_new = BETA_TWO * second + (1.0 - BETA_TWO) * grad_rot * grad_rot
        scaled = (moment_rot / (jnp.sqrt(second_new) + EPSILON)).astype(jnp.bfloat16)
        turned_back = matmul(left_rot, scaled).astype(jnp.bfloat16)
        back_rows = jnp.concatenate(
            [turned_back[:rows]]
            + [
                swap(turned_back[k * rows : (k + 1) * rows], "shard", k)
                for k in range(1, n_shard)
            ],
            1,
        )
        update = (near_columns(matmul(back_rows, near_rot, 1, 1)) / width).astype(jnp.bfloat16)

        def refreshed(stat, product_of_grads, rot):
            stat_new = BETA_STAT * stat + (1.0 - BETA_STAT) * product_of_grads
            product = matmul(stat_new.astype(jnp.bfloat16), rot)
            start = product / jnp.sqrt(jnp.sum(product * product, axis=0) / width + NORM_EPS)
            current = start.astype(jnp.bfloat16)
            for iteration in range(NS_ITERS):
                kept = width if iteration + 1 < NS_ITERS else rows
                gram = (matmul(current[:kept], current, 1, 1) / width).astype(jnp.bfloat16)
                result = 1.5 * current[:kept].astype(jnp.float32) - 0.5 * matmul(gram, current)
                current = result.astype(jnp.bfloat16)
            return result

        left_new = refreshed(stat_left_full, matmul(gradient, gradient, 1, 1), left_rot)
        right_new = refreshed(stat_right_full, matmul(gradient, gradient, 0, 0), right_rot)
        return (update, second_new, left_new, right_new)

    return body


def solution(mesh):
    n_dp, n_shard = mesh.shape["dp"], mesh.shape["shard"]
    body = fast_body if (n_dp, n_shard) == (16, 2) else make_plain_body(n_dp, n_shard)
    return jax.shard_map(
        body,
        mesh=mesh,
        in_specs=(
            P("dp", "shard", None),
            P("shard", None),
            P(None, "shard"),
            P("shard", None),
            P("shard", None),
            P("shard", None),
            P("shard", None),
        ),
        out_specs=(P("shard", None), P(None, "shard"), P("shard", None), P("shard", None)),
        check_vma=False,
    )
```

```python
import functools

import jax
import jax.numpy as jnp
from jax import lax
from jax.experimental import pallas as pl
from jax.experimental.pallas import tpu as pltpu
from jax.sharding import PartitionSpec as P

NS_ITERS = 2


BETA_ONE = 0.9
BETA_TWO = 0.9
BETA_STAT = 0.95
EPSILON = 1e-08
NORM_EPS = 1e-06
HALF = jnp.bfloat16
FULL = jnp.float32
VMEM = pl.BlockSpec(memory_space=pltpu.VMEM)
ANY = pl.BlockSpec(memory_space=pl.ANY)
SMEM = pl.BlockSpec(memory_space=pltpu.SMEM)


def matmul(left_mat, right_mat, left_dim=1, right_dim=0):
    return lax.dot_general(
        left_mat,
        right_mat,
        (((left_dim,), (right_dim,)), ((), ())),
        preferred_element_type=FULL,
    )


def shaped(shape, dtype):
    return jax.ShapeDtypeStruct(shape, dtype)


def tile(index, size):
    return pl.ds(pl.multiple_of(index * size, size), size)


def call(kernel, outs, operands, specs, scratch=(), flops=0, moved=0, limit=24):
    return pl.pallas_call(
        kernel,
        out_shape=outs,
        in_specs=specs,
        out_specs=[VMEM] * len(outs),
        scratch_shapes=list(scratch),
        compiler_params=pltpu.CompilerParams(vmem_limit_bytes=limit * 2**20),
        cost_estimate=pl.CostEstimate(flops=flops, bytes_accessed=moved, transcendentals=0),
    )(*operands)


def state_parts_kernel(where, left, right, stat_left, stat_right, bases, stats):
    half = left.shape[0]
    rows = stat_left.shape[1]
    bases[:half] = left[...].astype(HALF)
    bases[half:] = right[...].astype(HALF)
    stats[:, :rows] = stat_left[...]
    stats[:, rows:] = stat_right[...]


def first_sum_kernel(where, group, came, kept, sent):
    size = kept.shape[0]
    core, x = where[1], where[2]
    kept[...] = group[0, tile(core * 2 + x, size)].astype(FULL) + came[tile(x, size)].astype(FULL)
    sent[...] = group[0, tile(core * 2 + 1 - x, size)].astype(FULL) + came[
        tile(1 - x, size)
    ].astype(FULL)


def second_sum_kernel(where, kept, came, own, *sent):
    size = own.shape[0]
    z = where[3]
    own[...] = kept[tile(z, size)] + came[tile(z, size)]
    for k, out in enumerate(sent):
        there = tile(z ^ (k + 1), size)
        out[...] = kept[there] + came[there]


def third_sum_kernel(own, one, two, three, out):
    out[...] = ((own[...] + one[...]) + (two[...] + three[...])).astype(HALF)


def joined_kernel(where, *refs):
    out = refs[-1]
    z = where[3]
    size = refs[0].shape[0]
    for k, part in enumerate(refs[:-1]):
        out[tile(z ^ k, size)] = part[...]


def place_basis(where, out, own, mine, theirs, begin, natural):
    rows = own.shape[0]
    half = rows // 2
    position, core = where[0], where[1]
    first = position if natural else 0
    out[tile(first, rows)] = own[...].astype(HALF)
    other = (1 - first) * 2
    out[tile(other + core, half)] = mine[begin : begin + half]
    out[tile(other + 1 - core, half)] = theirs[begin : begin + half]


def place_stat(where, out, own, mine, theirs, begin, natural):
    rows = own.shape[0]
    half = rows // 2
    position, core = where[0], where[1]
    first = position if natural else 0
    here, there = tile(first, rows), tile(1 - first, rows)
    out[here, here] = own[:, tile(position, rows)]
    cross = own[:, tile(1 - position, rows)]
    out[here, there] = cross
    out[there, here] = cross.T
    other = (1 - first) * 2
    out[tile(other + core, half), there] = mine[:, begin : begin + rows]
    out[tile(other + 1 - core, half), there] = theirs[:, begin : begin + rows]


def left_state_kernel(where, basis, bmine, btheirs, stat, smine, stheirs, rot, turned, full):
    place_basis(where, rot, basis, bmine, btheirs, 0, False)
    place_stat(where, full, stat, smine, stheirs, 0, False)
    turned[...] = rot[...].T


def right_state_kernel(where, basis, bmine, btheirs, stat, smine, stheirs, rot, near, full):
    rows = basis.shape[0]
    place_basis(where, rot, basis, bmine, btheirs, rows // 2, True)
    place_stat(where, full, stat, smine, stheirs, rows, True)
    near[:, :rows] = rot[:, tile(where[0], rows)]
    near[:, rows:] = rot[:, tile(1 - where[0], rows)]


def moment_kernel(where, moment, near, *refs):
    parts, (gradient, ours, others, sem) = refs[:-4], refs[-4:]
    core, x = where[1], where[2]
    size = parts[0].shape[0]
    rows = moment.shape[0]
    copies = []
    for place, part in enumerate(parts):
        block = (
            (place // 4) * 4 + (core ^ (place % 4 // 2)) * 2 + (x ^ (place % 2))
        )
        copies.append(
            pltpu.make_async_copy(part, gradient.at[tile(block, size)], sem.at[place])
        )
    for copy in copies:
        copy.start()
    for copy in copies:
        copy.wait()
    half = (
        BETA_ONE * moment[...] + (1.0 - BETA_ONE) * gradient[:rows].astype(FULL)
    ).astype(HALF)
    step = rows // 2
    for i in range(2):
        here = slice(i * step, (i + 1) * step)
        others[:, here] = matmul(half, near[:, rows + i * step : rows + (i + 1) * step]).astype(HALF)
        ours[:, here] = matmul(half, near[:, here]).astype(HALF)


def adam_kernel(gradient, near, rot, turned, mine, came, second, new, kept, sent, block, scaled):
    width = gradient.shape[0]
    rows = mine.shape[0]
    step = rows // 2
    columns = [slice(i * step, (i + 1) * step) for i in range(2)]
    for here in columns:
        block[:, here] = matmul(gradient[...], near[:, here]).astype(HALF)
    for here in columns:
        grad_rot = matmul(turned[...], block[:, here]) * (1.0 / width)
        moment_rot = (
            matmul(turned[:, :rows], mine[:, here]) + matmul(turned[:, rows:], came[:, here])
        ) * (1.0 / width)
        value = BETA_TWO * second[:, here] + (1.0 - BETA_TWO) * grad_rot * grad_rot
        new[:, here] = value
        scaled[:, here] = (moment_rot / (jnp.sqrt(value) + EPSILON)).astype(HALF)
    for here in columns:
        sent[:, here] = matmul(rot[rows:], scaled[:, here]).astype(HALF)
        kept[:, here] = matmul(rot[:rows], scaled[:, here]).astype(HALF)


def update_kernel(mine, came, near, out):
    rows, width = out.shape
    step = width // 4
    for here in [slice(i * step, (i + 1) * step) for i in range(4)]:
        total = matmul(mine[...], near[here, :rows], 1, 1) + matmul(
            came[...], near[here, rows:], 1, 1
        )
        out[:, here] = (total * (1.0 / width)).astype(HALF)


def refresh_kernel(natural, where, gradient, rot, stat, out, stat_in, turned, half, gram, sem):
    width = gradient.shape[0]
    rows = out.shape[0]
    step = width // 4
    columns = [slice(i * step, (i + 1) * step) for i in range(4)]
    copies = [
        pltpu.make_async_copy(stat.at[:, here], stat_in.at[:, here], sem.at[i])
        for i, here in enumerate(columns)
    ]
    for copy in copies:
        copy.start()
    if natural:
        for here in columns:
            turned[:, here] = gradient[here].T
    for here, copy in zip(columns, copies):
        if natural:
            grads = matmul(turned[...], gradient[:, here])
        else:
            grads = matmul(gradient[...], gradient[here], 1, 1)
        copy.wait()
        half[:, here] = (BETA_STAT * stat_in[:, here] + (1.0 - BETA_STAT) * grads).astype(HALF)
    for here in columns:
        product = matmul(half[...], rot[:, here])
        square = jnp.sum(product * product, axis=0, keepdims=True) * (1.0 / width)
        turned[:, here] = (product * lax.rsqrt(square + NORM_EPS)).astype(HALF)

    def improved(current, kept, result, dtype):
        size = result.shape[0]
        for here in columns:
            gram[:size, here] = (
                matmul(current[kept], current[here], 1, 1) * (1.0 / width)
            ).astype(HALF)
        for here in columns:
            result[:, here] = (
                1.5 * current[kept, here].astype(FULL)
                - 0.5 * matmul(gram[:size], current[:, here])
            ).astype(dtype)

    current, following = turned, half
    for _ in range(NS_ITERS - 1):
        improved(current, slice(0, width), following, HALF)
        current, following = following, current
    improved(current, tile(where[0], rows) if natural else slice(0, rows), out, FULL)


def fast_body(group_grads, moment, second, stat_left, stat_right, basis_left, basis_right):
    position = lax.axis_index("shard")
    member = lax.axis_index("dp")
    rows, width = moment.shape
    half = rows // 2
    quarter = rows // 4
    chunk = rows // 16
    core, x, z = member & 1, (member >> 1) & 1, member >> 2
    where = jnp.stack([position, core, x, z]).astype(jnp.int32)
    unit = 2 * width**3

    def dp_swap(value, distance):
        return lax.ppermute(value, "dp", [(i, i ^ distance) for i in range(16)])

    def shard_swap(value):
        return lax.ppermute(value, "shard", [(0, 1), (1, 0)])

    def cross_swap(value):
        pairs = [(i, i ^ 5) for i in range(32)]
        return lax.ppermute(value, ("dp", "shard"), pairs)

    bases_sent, stats_sent = pl.pallas_call(
        state_parts_kernel,
        out_shape=[shaped((rows, width), HALF), shaped((half, width), FULL)],
        grid_spec=pltpu.PrefetchScalarGridSpec(
            num_scalar_prefetch=1,
            grid=(1,),
            in_specs=[pl.BlockSpec((half, width), lambda i, where: (where[1], 0))] * 2
            + [pl.BlockSpec((half, rows), lambda i, where: (where[1], where[0]))] * 2,
            out_specs=[
                pl.BlockSpec((rows, width), lambda i, where: (0, 0)),
                pl.BlockSpec((half, width), lambda i, where: (0, 0)),
            ],
        ),
        compiler_params=pltpu.CompilerParams(vmem_limit_bytes=56 * 2**20),
        cost_estimate=pl.CostEstimate(flops=0, bytes_accessed=2**22, transcendentals=0),
    )(where, basis_left, basis_right, stat_left, stat_right)
    bases_mine = shard_swap(bases_sent)
    stats_mine = shard_swap(stats_sent)

    raw = lax.dynamic_slice_in_dim(group_grads[0], (1 - core) * half, half, 0)
    came = dp_swap(raw, 1)
    kept, sent = call(
        first_sum_kernel,
        [shaped((quarter, width), FULL)] * 2,
        (where, group_grads, came),
        [SMEM, VMEM, VMEM],
        moved=2**21,
    )
    came = dp_swap(sent, 2)
    own, *sent = call(
        second_sum_kernel,
        [shaped((chunk, width), FULL)] * 4,
        (where, kept, came),
        [SMEM, VMEM, VMEM],
        moved=2**20,
    )
    pieces = [dp_swap(value, 4 * (k + 1)) for k, value in enumerate(sent)]
    (piece,) = call(
        third_sum_kernel, [shaped((chunk, width), HALF)], (own, *pieces), [VMEM] * 4, moved=2**19
    )
    pieces = [piece] + [dp_swap(piece, 4 * k) for k in (1, 2, 3)]
    (part,) = call(
        joined_kernel, [shaped((quarter, width), HALF)], (where, *pieces), [SMEM] + [VMEM] * 4,
        moved=2**19,
    )
    part, bases_mine, stats_mine = lax.optimization_barrier((part, bases_mine, stats_mine))
    parts = [part, dp_swap(part, 2), shard_swap(part), cross_swap(part)]
    swapped = [dp_swap(value, 1) for value in parts]

    bases_theirs = dp_swap(bases_mine, 1)
    stats_theirs = dp_swap(stats_mine, 1)
    bases = (bases_mine, bases_theirs)
    stats = (stats_mine, stats_theirs)
    state_outs = [
        shaped((width, width), HALF),
        shaped((width, width), HALF),
        shaped((width, width), FULL),
    ]
    left_rot, left_turned, left_stat = call(
        left_state_kernel,
        state_outs,
        (where, basis_left, *bases, stat_left, *stats),
        [SMEM] + [VMEM] * 6,
        moved=2**24,
    )
    right_rot, right_near, right_stat = call(
        right_state_kernel,
        state_outs,
        (where, basis_right, *bases, stat_right, *stats),
        [SMEM] + [VMEM] * 6,
        moved=2**24,
    )

    ordered = [parts[0], parts[1], swapped[0], swapped[1], parts[2], parts[3], swapped[2], swapped[3]]
    gradient, moment_mine, moment_sent = call(
        moment_kernel,
        [shaped((width, width), HALF)] + [shaped((rows, rows), HALF)] * 2,
        (where, moment, right_near, *ordered),
        [SMEM, VMEM, VMEM] + [ANY] * 8,
        [pltpu.SemaphoreType.DMA((8,))],
        flops=unit // 2,
        moved=2**23,
    )
    moment_came = shard_swap(moment_sent)

    def refreshed(natural, rot, stat):
        (out,) = call(
            functools.partial(refresh_kernel, natural),
            [shaped((rows, width), FULL)],
            (where, gradient, rot, stat),
            [SMEM, VMEM, VMEM, ANY],
            [
                pltpu.VMEM((width, width), FULL),
                pltpu.VMEM((width, width), HALF),
                pltpu.VMEM((width, width), HALF),
                pltpu.VMEM((width, width), HALF),
                pltpu.SemaphoreType.DMA((4,)),
            ],
            flops=5 * unit,
            moved=2**23,
        )
        return out

    left_new = refreshed(False, left_rot, left_stat)
    second_new, back_mine, back_sent = call(
        adam_kernel,
        [shaped((width, rows), FULL)] + [shaped((rows, rows), HALF)] * 2,
        (gradient, right_near, left_rot, left_turned, moment_mine, moment_came, second),
        [VMEM] * 7,
        [pltpu.VMEM((width, rows), HALF)] * 2,
        flops=2 * unit,
        moved=2**23,
    )
    back_came = shard_swap(back_sent)
    right_new = refreshed(True, right_rot, right_stat)
    (update,) = call(
        update_kernel,
        [shaped((rows, width), HALF)],
        (back_mine, back_came, right_near),
        [VMEM] * 3,
        flops=unit // 2,
        moved=2**22,
    )
    return (update, second_new, left_new, right_new)


def make_plain_body(n_dp, n_shard):
    def swap(value, axis, distance):
        size = n_dp if axis == "dp" else n_shard
        return lax.ppermute(value, axis, [(i, i ^ distance) for i in range(size)])

    dp_bits = []
    bit = 1
    while bit < n_dp:
        dp_bits.append(bit)
        bit *= 2

    def ordered(first_is_low, own, other, dim):
        return jnp.where(
            first_is_low,
            jnp.concatenate([own, other], dim),
            jnp.concatenate([other, own], dim),
        )

    def body(group_grads, moment, second, stat_left, stat_right, basis_left, basis_right):
        position = lax.axis_index("shard")
        member = lax.axis_index("dp")
        rows, width = moment.shape
        core = member & 1
        half = rows // 2

        def near_columns(value):
            blocks = [
                lax.dynamic_slice_in_dim(value, (position ^ k) * rows, rows, 1)
                for k in range(n_shard)
            ]
            return jnp.concatenate(blocks, 1)

        def fetch(value, distance):
            size = value.shape[0] // 2
            part = lax.dynamic_slice_in_dim(value, core * size, size, 0)
            part = swap(part, "shard", distance)
            other = swap(part, "dp", 1)
            return ordered(core == 0, part, other, 0)

        left_own = basis_left.astype(jnp.bfloat16)
        right_own = basis_right.astype(jnp.bfloat16)
        left_rot = jnp.concatenate([left_own] + [fetch(left_own, k) for k in range(1, n_shard)], 0)
        right_rot = jnp.concatenate(
            [right_own] + [fetch(right_own, k) for k in range(1, n_shard)], 0
        )

        def whole_stat(stat):
            own = near_columns(stat)
            blocks = [own[:, b * rows : (b + 1) * rows] for b in range(n_shard)]
            bands = [own]
            for k in range(1, n_shard):
                others = [b for b in range(n_shard) if b != k]
                sent = jnp.concatenate([blocks[b] for b in others], 1).astype(jnp.bfloat16)
                came = fetch(sent, k).astype(jnp.float32)
                band = [None] * n_shard
                band[0] = blocks[k].T
                for place, b in enumerate(others):
                    band[k ^ b] = came[:, place * rows : (place + 1) * rows]
                bands.append(jnp.concatenate(band, 1))
            return jnp.concatenate(bands, 0)

        stat_left_full = whole_stat(stat_left)
        stat_right_full = whole_stat(stat_right)

        part = group_grads[0]
        for bit in dp_bits:
            size = part.shape[0] // 2
            high = (member & bit) // bit
            kept = lax.dynamic_slice_in_dim(part, high * size, size, 0)
            sent = lax.dynamic_slice_in_dim(part, (1 - high) * size, size, 0)
            part = kept.astype(jnp.float32) + swap(sent, "dp", bit).astype(jnp.float32)
        chunk = part.astype(jnp.bfloat16)[None]
        chunk = jnp.concatenate([chunk] + [swap(chunk, "shard", k) for k in range(1, n_shard)], 0)
        for bit in reversed(dp_bits):
            chunk = ordered((member & bit) == 0, chunk, swap(chunk, "dp", bit), 1)
        gradient = near_columns(chunk.reshape(width, width))

        grad_rows = gradient[:rows].astype(jnp.float32)
        moment_half = (
            BETA_ONE * near_columns(moment) + (1.0 - BETA_ONE) * grad_rows
        ).astype(jnp.bfloat16)
        near_rot = near_columns(right_rot)
        moment_turned = matmul(moment_half, near_rot).astype(jnp.bfloat16)
        moment_block = jnp.concatenate(
            [moment_turned[:, :rows]]
            + [
                swap(moment_turned[:, k * rows : (k + 1) * rows], "shard", k)
                for k in range(1, n_shard)
            ],
            0,
        )
        grad_block = matmul(gradient, near_rot[:, :rows]).astype(jnp.bfloat16)
        grad_rot = matmul(left_rot, grad_block, 0) / width
        moment_rot = matmul(left_rot, moment_block, 0) / width
        second_new = BETA_TWO * second + (1.0 - BETA_TWO) * grad_rot * grad_rot
        scaled = (moment_rot / (jnp.sqrt(second_new) + EPSILON)).astype(jnp.bfloat16)
        turned_back = matmul(left_rot, scaled).astype(jnp.bfloat16)
        back_rows = jnp.concatenate(
            [turned_back[:rows]]
            + [
                swap(turned_back[k * rows : (k + 1) * rows], "shard", k)
                for k in range(1, n_shard)
            ],
            1,
        )
        update = (near_columns(matmul(back_rows, near_rot, 1, 1)) / width).astype(jnp.bfloat16)

        def refreshed(stat, product_of_grads, rot):
            stat_new = BETA_STAT * stat + (1.0 - BETA_STAT) * product_of_grads
            product = matmul(stat_new.astype(jnp.bfloat16), rot)
            start = product / jnp.sqrt(jnp.sum(product * product, axis=0) / width + NORM_EPS)
            current = start.astype(jnp.bfloat16)
            for iteration in range(NS_ITERS):
                kept = width if iteration + 1 < NS_ITERS else rows
                gram = (matmul(current[:kept], current, 1, 1) / width).astype(jnp.bfloat16)
                result = 1.5 * current[:kept].astype(jnp.float32) - 0.5 * matmul(gram, current)
                current = result.astype(jnp.bfloat16)
            return result

        left_new = refreshed(stat_left_full, matmul(gradient, gradient, 1, 1), left_rot)
        right_new = refreshed(stat_right_full, matmul(gradient, gradient, 0, 0), right_rot)
        return (update, second_new, left_new, right_new)

    return body


def solution(mesh):
    n_dp, n_shard = mesh.shape["dp"], mesh.shape["shard"]
    body = fast_body if (n_dp, n_shard) == (16, 2) else make_plain_body(n_dp, n_shard)
    return jax.shard_map(
        body,
        mesh=mesh,
        in_specs=(
            P("dp", "shard", None),
            P("shard", None),
            P(None, "shard"),
            P("shard", None),
            P("shard", None),
            P("shard", None),
            P("shard", None),
        ),
        out_specs=(P("shard", None), P(None, "shard"), P("shard", None), P("shard", None)),
        check_vma=False,
    )
```

```python
import functools

import jax
import jax.numpy as jnp
from jax import lax
from jax.experimental import pallas as pl
from jax.experimental.pallas import tpu as pltpu
from jax.sharding import PartitionSpec as P

NS_ITERS = 2


BETA_ONE = 0.9
BETA_TWO = 0.9
BETA_STAT = 0.95
EPSILON = 1e-08
NORM_EPS = 1e-06
HALF = jnp.bfloat16
FULL = jnp.float32
VMEM = pl.BlockSpec(memory_space=pltpu.VMEM)
ANY = pl.BlockSpec(memory_space=pl.ANY)
SMEM = pl.BlockSpec(memory_space=pltpu.SMEM)


def matmul(left_mat, right_mat, left_dim=1, right_dim=0):
    return lax.dot_general(
        left_mat,
        right_mat,
        (((left_dim,), (right_dim,)), ((), ())),
        preferred_element_type=FULL,
    )


def shaped(shape, dtype):
    return jax.ShapeDtypeStruct(shape, dtype)


def tile(index, size):
    return pl.ds(pl.multiple_of(index * size, size), size)


def call(kernel, outs, operands, specs, scratch=(), flops=0, moved=0, limit=24):
    return pl.pallas_call(
        kernel,
        out_shape=outs,
        in_specs=specs,
        out_specs=[VMEM] * len(outs),
        scratch_shapes=list(scratch),
        compiler_params=pltpu.CompilerParams(vmem_limit_bytes=limit * 2**20),
        cost_estimate=pl.CostEstimate(flops=flops, bytes_accessed=moved, transcendentals=0),
    )(*operands)


TILES = 4
UPPER = [(i, j) for i in range(TILES) for j in range(i, TILES)]


def bases_kernel(where, left, right, out):
    out[0] = left[...].astype(HALF)
    out[1] = right[...].astype(HALF)


def stats_kernel(where, left, right, out):
    size = left.shape[0] // TILES
    count = len(UPPER) // 2
    for core in range(2):

        @pl.when(where[1] == core)
        def _():
            for place, (i, j) in enumerate(UPPER[core * count : (core + 1) * count]):
                for side, stat in enumerate((left, right)):
                    out[side, :, place * size : (place + 1) * size] = stat[
                        i * size : (i + 1) * size, j * size : (j + 1) * size
                    ]


def first_sum_kernel(where, group, came, kept, sent):
    size = kept.shape[0]
    core, x = where[1], where[2]
    kept[...] = group[0, tile(core * 2 + x, size)].astype(FULL) + came[tile(x, size)].astype(FULL)
    sent[...] = group[0, tile(core * 2 + 1 - x, size)].astype(FULL) + came[
        tile(1 - x, size)
    ].astype(FULL)


def second_sum_kernel(where, kept, came, own, *sent):
    size = own.shape[0]
    z = where[3]
    own[...] = kept[tile(z, size)] + came[tile(z, size)]
    for k, out in enumerate(sent):
        there = tile(z ^ (k + 1), size)
        out[...] = kept[there] + came[there]


def third_sum_kernel(own, one, two, three, out):
    out[...] = ((own[...] + one[...]) + (two[...] + three[...])).astype(HALF)


def joined_kernel(where, *refs):
    out = refs[-1]
    z = where[3]
    size = refs[0].shape[0]
    for k, part in enumerate(refs[:-1]):
        out[tile(z ^ k, size)] = part[...]


def place_basis(where, out, own, mine, theirs, side, natural):
    rows = own.shape[0]
    half = rows // 2
    position, core = where[0], where[1]
    first = position if natural else 0
    out[tile(first, rows)] = own[...].astype(HALF)
    other = (1 - first) * 2
    out[tile(other + core, half)] = mine[side]
    out[tile(other + 1 - core, half)] = theirs[side]


def place_stat(where, out, own, mine, theirs, side, natural):
    rows = own.shape[0]
    size = rows // TILES
    count = len(UPPER) // 2
    position, core = where[0], where[1]
    first = position if natural else 0
    here, there = tile(first, rows), tile(1 - first, rows)
    out[here, here] = own[:, tile(position, rows)]
    cross = own[:, tile(1 - position, rows)]
    out[here, there] = cross
    out[there, here] = cross.T
    base = (1 - first) * TILES
    for place, (i, j) in enumerate(UPPER):
        from_mine = core == place // count
        columns = slice(place % count * size, (place % count + 1) * size)
        value = jnp.where(from_mine, mine[side, :, columns], theirs[side, :, columns])
        out[tile(base + i, size), tile(base + j, size)] = value
        if i != j:
            out[tile(base + j, size), tile(base + i, size)] = value.T


def left_state_kernel(where, basis, bmine, btheirs, stat, smine, stheirs, rot, turned, full):
    place_basis(where, rot, basis, bmine, btheirs, 0, False)
    place_stat(where, full, stat, smine, stheirs, 0, False)
    turned[...] = rot[...].T


def right_state_kernel(where, basis, bmine, btheirs, stat, smine, stheirs, rot, near, back, full):
    rows = basis.shape[0]
    place_basis(where, rot, basis, bmine, btheirs, 1, True)
    place_stat(where, full, stat, smine, stheirs, 1, True)
    near[:, :rows] = rot[:, tile(where[0], rows)]
    near[:, rows:] = rot[:, tile(1 - where[0], rows)]
    back[...] = near[...].T


def moment_kernel(where, moment, near, *refs):
    parts, (gradient, turned, ours, others, sem) = refs[:-5], refs[-5:]
    core, x = where[1], where[2]
    size = parts[0].shape[0]
    rows = moment.shape[0]
    copies = []
    for place, part in enumerate(parts):
        block = (
            (place // 4) * 4 + (core ^ (place % 4 // 2)) * 2 + (x ^ (place % 2))
        )
        copies.append(
            pltpu.make_async_copy(part, gradient.at[tile(block, size)], sem.at[place])
        )
    for copy in copies:
        copy.start()
    for copy in copies:
        copy.wait()
    half = (
        BETA_ONE * moment[...] + (1.0 - BETA_ONE) * gradient[:rows].astype(FULL)
    ).astype(HALF)
    step = rows // 2
    for i in range(2):
        here = slice(i * step, (i + 1) * step)
        others[:, here] = matmul(half, near[:, rows + i * step : rows + (i + 1) * step]).astype(HALF)
        ours[:, here] = matmul(half, near[:, here]).astype(HALF)
    step = gradient.shape[0] // 4
    for i in range(4):
        here = slice(i * step, (i + 1) * step)
        turned[:, here] = gradient[here].T


def adam_kernel(gradient, near, rot, turned, mine, came, second, new, kept, sent, block, scaled):
    width = gradient.shape[0]
    rows = mine.shape[0]
    step = rows // 2
    columns = [slice(i * step, (i + 1) * step) for i in range(2)]
    for here in columns:
        block[:, here] = matmul(gradient[...], near[:, here]).astype(HALF)
    for here in columns:
        grad_rot = matmul(turned[...], block[:, here]) * (1.0 / width)
        moment_rot = (
            matmul(turned[:, :rows], mine[:, here]) + matmul(turned[:, rows:], came[:, here])
        ) * (1.0 / width)
        value = BETA_TWO * second[:, here] + (1.0 - BETA_TWO) * grad_rot * grad_rot
        new[:, here] = value
        scaled[:, here] = (moment_rot / (jnp.sqrt(value) + EPSILON)).astype(HALF)
    for here in columns:
        sent[:, here] = matmul(rot[rows:], scaled[:, here]).astype(HALF)
        kept[:, here] = matmul(rot[:rows], scaled[:, here]).astype(HALF)


def update_kernel(mine, came, back, out):
    rows, width = out.shape
    step = width // 4
    for here in [slice(i * step, (i + 1) * step) for i in range(4)]:
        total = matmul(mine[...], back[:rows, here]) + matmul(came[...], back[rows:, here])
        out[:, here] = (total * (1.0 / width)).astype(HALF)


def refresh_kernel(natural, where, one, two, rot, stat, out, half, first, second, turned, gram):
    width = one.shape[0]
    rows = out.shape[0]
    step = width // 4
    columns = [slice(i * step, (i + 1) * step) for i in range(4)]
    for here in columns:
        grads = matmul(one[...], two[:, here])
        half[:, here] = (BETA_STAT * stat[:, here] + (1.0 - BETA_STAT) * grads).astype(HALF)
    for here in columns:
        product = matmul(half[...], rot[:, here])
        square = jnp.sum(product * product, axis=0, keepdims=True) * (1.0 / width)
        start = (product * lax.rsqrt(square + NORM_EPS)).astype(HALF)
        first[:, here] = start
        turned[here] = start.T

    def improved(current, kept, result, dtype, again):
        size = result.shape[0]
        for here in columns:
            gram[:size, here] = (matmul(current[kept], turned[:, here]) * (1.0 / width)).astype(
                HALF
            )
        for here in columns:
            value = (
                1.5 * current[kept, here].astype(FULL)
                - 0.5 * matmul(gram[:size], current[:, here])
            ).astype(dtype)
            result[:, here] = value
            if again:
                turned[here] = value.T

    current, following = first, second
    for _ in range(NS_ITERS - 1):
        improved(current, slice(0, width), following, HALF, True)
        current, following = following, current
    improved(current, tile(where[0], rows) if natural else slice(0, rows), out, FULL, False)


def fast_body(group_grads, moment, second, stat_left, stat_right, basis_left, basis_right):
    position = lax.axis_index("shard")
    member = lax.axis_index("dp")
    rows, width = moment.shape
    half = rows // 2
    quarter = rows // 4
    chunk = rows // 16
    core, x, z = member & 1, (member >> 1) & 1, member >> 2
    where = jnp.stack([position, core, x, z]).astype(jnp.int32)
    unit = 2 * width**3

    def dp_swap(value, distance):
        return lax.ppermute(value, "dp", [(i, i ^ distance) for i in range(16)])

    def shard_swap(value):
        return lax.ppermute(value, "shard", [(0, 1), (1, 0)])

    def cross_swap(value):
        pairs = [(i, i ^ 5) for i in range(32)]
        return lax.ppermute(value, ("dp", "shard"), pairs)

    step = half // 2
    (bases_sent,) = pl.pallas_call(
        bases_kernel,
        out_shape=[shaped((2, half, width), HALF)],
        grid_spec=pltpu.PrefetchScalarGridSpec(
            num_scalar_prefetch=1,
            grid=(2,),
            in_specs=[pl.BlockSpec((step, width), lambda i, where: (where[1] * 2 + i, 0))] * 2,
            out_specs=[pl.BlockSpec((2, step, width), lambda i, where: (0, i, 0))],
        ),
        compiler_params=pltpu.CompilerParams(vmem_limit_bytes=56 * 2**20),
        cost_estimate=pl.CostEstimate(flops=0, bytes_accessed=2**22, transcendentals=0),
    )(where, basis_left, basis_right)
    bases_mine = shard_swap(bases_sent)

    raw = lax.dynamic_slice_in_dim(group_grads[0], (1 - core) * half, half, 0)
    came = dp_swap(raw, 1)
    kept, sent = call(
        first_sum_kernel,
        [shaped((quarter, width), FULL)] * 2,
        (where, group_grads, came),
        [SMEM, VMEM, VMEM],
        moved=2**21,
    )
    came = dp_swap(sent, 2)
    own, *sent = call(
        second_sum_kernel,
        [shaped((chunk, width), FULL)] * 4,
        (where, kept, came),
        [SMEM, VMEM, VMEM],
        moved=2**20,
    )
    (stats_sent,) = pl.pallas_call(
        stats_kernel,
        out_shape=[shaped((2, quarter, 5 * quarter), FULL)],
        grid_spec=pltpu.PrefetchScalarGridSpec(
            num_scalar_prefetch=1,
            grid=(1,),
            in_specs=[pl.BlockSpec((rows, rows), lambda i, where: (0, where[0]))] * 2,
            out_specs=[
                pl.BlockSpec((2, quarter, 5 * quarter), lambda i, where: (0, 0, 0)),
            ],
        ),
        compiler_params=pltpu.CompilerParams(vmem_limit_bytes=56 * 2**20),
        cost_estimate=pl.CostEstimate(flops=0, bytes_accessed=2**22, transcendentals=0),
    )(where, stat_left, stat_right)
    stats_mine = shard_swap(stats_sent)
    pieces = [dp_swap(value, 4 * (k + 1)) for k, value in enumerate(sent)]
    (piece,) = call(
        third_sum_kernel, [shaped((chunk, width), HALF)], (own, *pieces), [VMEM] * 4, moved=2**19
    )
    pieces = [piece] + [dp_swap(piece, 4 * k) for k in (1, 2, 3)]
    (part,) = call(
        joined_kernel, [shaped((quarter, width), HALF)], (where, *pieces), [SMEM] + [VMEM] * 4,
        moved=2**19,
    )
    part, bases_mine, stats_mine = lax.optimization_barrier((part, bases_mine, stats_mine))
    parts = [part, dp_swap(part, 2), shard_swap(part), cross_swap(part)]
    swapped = [dp_swap(value, 1) for value in parts]

    bases_theirs = dp_swap(bases_mine, 1)
    stats_theirs = dp_swap(stats_mine, 1)
    bases = (bases_mine, bases_theirs)
    stats = (stats_mine, stats_theirs)
    state_outs = [
        shaped((width, width), HALF),
        shaped((width, width), HALF),
        shaped((width, width), FULL),
    ]
    left_rot, left_turned, left_stat = call(
        left_state_kernel,
        state_outs,
        (where, basis_left, *bases, stat_left, *stats),
        [SMEM] + [VMEM] * 6,
        moved=2**24,
    )
    right_rot, right_near, right_back, right_stat = call(
        right_state_kernel,
        state_outs[:1] + state_outs,
        (where, basis_right, *bases, stat_right, *stats),
        [SMEM] + [VMEM] * 6,
        moved=2**24,
    )

    ordered = [parts[0], parts[1], swapped[0], swapped[1], parts[2], parts[3], swapped[2], swapped[3]]
    gradient, gradient_turned, moment_mine, moment_sent = call(
        moment_kernel,
        [shaped((width, width), HALF)] * 2 + [shaped((rows, rows), HALF)] * 2,
        (where, moment, right_near, *ordered),
        [SMEM, VMEM, VMEM] + [ANY] * 8,
        [pltpu.SemaphoreType.DMA((8,))],
        flops=unit // 2,
        moved=2**23,
    )
    moment_came = shard_swap(moment_sent)

    def refreshed(natural, one, two, rot, stat):
        (out,) = call(
            functools.partial(refresh_kernel, natural),
            [shaped((rows, width), FULL)],
            (where, one, two, rot, stat),
            [SMEM] + [VMEM] * 4,
            [pltpu.VMEM((width, width), HALF)] * 5,
            flops=5 * unit,
            moved=2**23,
        )
        return out

    left_new = refreshed(False, gradient, gradient_turned, left_rot, left_stat)
    second_new, back_mine, back_sent = call(
        adam_kernel,
        [shaped((width, rows), FULL)] + [shaped((rows, rows), HALF)] * 2,
        (gradient, right_near, left_rot, left_turned, moment_mine, moment_came, second),
        [VMEM] * 7,
        [pltpu.VMEM((width, rows), HALF)] * 2,
        flops=2 * unit,
        moved=2**23,
    )
    back_came = shard_swap(back_sent)
    right_new = refreshed(True, gradient_turned, gradient, right_rot, right_stat)
    (update,) = call(
        update_kernel,
        [shaped((rows, width), HALF)],
        (back_mine, back_came, right_back),
        [VMEM] * 3,
        flops=unit // 2,
        moved=2**22,
    )
    return (update, second_new, left_new, right_new)


def make_plain_body(n_dp, n_shard):
    def swap(value, axis, distance):
        size = n_dp if axis == "dp" else n_shard
        return lax.ppermute(value, axis, [(i, i ^ distance) for i in range(size)])

    dp_bits = []
    bit = 1
    while bit < n_dp:
        dp_bits.append(bit)
        bit *= 2

    def ordered(first_is_low, own, other, dim):
        return jnp.where(
            first_is_low,
            jnp.concatenate([own, other], dim),
            jnp.concatenate([other, own], dim),
        )

    def body(group_grads, moment, second, stat_left, stat_right, basis_left, basis_right):
        position = lax.axis_index("shard")
        member = lax.axis_index("dp")
        rows, width = moment.shape
        core = member & 1
        half = rows // 2

        def near_columns(value):
            blocks = [
                lax.dynamic_slice_in_dim(value, (position ^ k) * rows, rows, 1)
                for k in range(n_shard)
            ]
            return jnp.concatenate(blocks, 1)

        def fetch(value, distance):
            size = value.shape[0] // 2
            part = lax.dynamic_slice_in_dim(value, core * size, size, 0)
            part = swap(part, "shard", distance)
            other = swap(part, "dp", 1)
            return ordered(core == 0, part, other, 0)

        left_own = basis_left.astype(jnp.bfloat16)
        right_own = basis_right.astype(jnp.bfloat16)
        left_rot = jnp.concatenate([left_own] + [fetch(left_own, k) for k in range(1, n_shard)], 0)
        right_rot = jnp.concatenate(
            [right_own] + [fetch(right_own, k) for k in range(1, n_shard)], 0
        )

        def whole_stat(stat):
            own = near_columns(stat)
            blocks = [own[:, b * rows : (b + 1) * rows] for b in range(n_shard)]
            bands = [own]
            for k in range(1, n_shard):
                others = [b for b in range(n_shard) if b != k]
                sent = jnp.concatenate([blocks[b] for b in others], 1).astype(jnp.bfloat16)
                came = fetch(sent, k).astype(jnp.float32)
                band = [None] * n_shard
                band[0] = blocks[k].T
                for place, b in enumerate(others):
                    band[k ^ b] = came[:, place * rows : (place + 1) * rows]
                bands.append(jnp.concatenate(band, 1))
            return jnp.concatenate(bands, 0)

        stat_left_full = whole_stat(stat_left)
        stat_right_full = whole_stat(stat_right)

        part = group_grads[0]
        for bit in dp_bits:
            size = part.shape[0] // 2
            high = (member & bit) // bit
            kept = lax.dynamic_slice_in_dim(part, high * size, size, 0)
            sent = lax.dynamic_slice_in_dim(part, (1 - high) * size, size, 0)
            part = kept.astype(jnp.float32) + swap(sent, "dp", bit).astype(jnp.float32)
        chunk = part.astype(jnp.bfloat16)[None]
        chunk = jnp.concatenate([chunk] + [swap(chunk, "shard", k) for k in range(1, n_shard)], 0)
        for bit in reversed(dp_bits):
            chunk = ordered((member & bit) == 0, chunk, swap(chunk, "dp", bit), 1)
        gradient = near_columns(chunk.reshape(width, width))

        grad_rows = gradient[:rows].astype(jnp.float32)
        moment_half = (
            BETA_ONE * near_columns(moment) + (1.0 - BETA_ONE) * grad_rows
        ).astype(jnp.bfloat16)
        near_rot = near_columns(right_rot)
        moment_turned = matmul(moment_half, near_rot).astype(jnp.bfloat16)
        moment_block = jnp.concatenate(
            [moment_turned[:, :rows]]
            + [
                swap(moment_turned[:, k * rows : (k + 1) * rows], "shard", k)
                for k in range(1, n_shard)
            ],
            0,
        )
        grad_block = matmul(gradient, near_rot[:, :rows]).astype(jnp.bfloat16)
        grad_rot = matmul(left_rot, grad_block, 0) / width
        moment_rot = matmul(left_rot, moment_block, 0) / width
        second_new = BETA_TWO * second + (1.0 - BETA_TWO) * grad_rot * grad_rot
        scaled = (moment_rot / (jnp.sqrt(second_new) + EPSILON)).astype(jnp.bfloat16)
        turned_back = matmul(left_rot, scaled).astype(jnp.bfloat16)
        back_rows = jnp.concatenate(
            [turned_back[:rows]]
            + [
                swap(turned_back[k * rows : (k + 1) * rows], "shard", k)
                for k in range(1, n_shard)
            ],
            1,
        )
        update = (near_columns(matmul(back_rows, near_rot, 1, 1)) / width).astype(jnp.bfloat16)

        def refreshed(stat, product_of_grads, rot):
            stat_new = BETA_STAT * stat + (1.0 - BETA_STAT) * product_of_grads
            product = matmul(stat_new.astype(jnp.bfloat16), rot)
            start = product / jnp.sqrt(jnp.sum(product * product, axis=0) / width + NORM_EPS)
            current = start.astype(jnp.bfloat16)
            for iteration in range(NS_ITERS):
                kept = width if iteration + 1 < NS_ITERS else rows
                gram = (matmul(current[:kept], current, 1, 1) / width).astype(jnp.bfloat16)
                result = 1.5 * current[:kept].astype(jnp.float32) - 0.5 * matmul(gram, current)
                current = result.astype(jnp.bfloat16)
            return result

        left_new = refreshed(stat_left_full, matmul(gradient, gradient, 1, 1), left_rot)
        right_new = refreshed(stat_right_full, matmul(gradient, gradient, 0, 0), right_rot)
        return (update, second_new, left_new, right_new)

    return body


def solution(mesh):
    n_dp, n_shard = mesh.shape["dp"], mesh.shape["shard"]
    body = fast_body if (n_dp, n_shard) == (16, 2) else make_plain_body(n_dp, n_shard)
    return jax.shard_map(
        body,
        mesh=mesh,
        in_specs=(
            P("dp", "shard", None),
            P("shard", None),
            P(None, "shard"),
            P("shard", None),
            P("shard", None),
            P("shard", None),
            P("shard", None),
        ),
        out_specs=(P("shard", None), P(None, "shard"), P("shard", None), P("shard", None)),
        check_vma=False,
    )
```

```python
import jax
import jax.numpy as jnp
from jax import lax
from jax.experimental import pallas as pl
from jax.experimental.pallas import tpu as pltpu
from jax.sharding import PartitionSpec as P

NS_ITERS = 2


BETA_ONE = 0.9
BETA_TWO = 0.9
BETA_STAT = 0.95
EPSILON = 1e-08
NORM_EPS = 1e-06
HALF = jnp.bfloat16
FULL = jnp.float32
VMEM = pl.BlockSpec(memory_space=pltpu.VMEM)
ANY = pl.BlockSpec(memory_space=pl.ANY)
SMEM = pl.BlockSpec(memory_space=pltpu.SMEM)


def matmul(left_mat, right_mat, left_dim=1, right_dim=0):
    return lax.dot_general(
        left_mat,
        right_mat,
        (((left_dim,), (right_dim,)), ((), ())),
        preferred_element_type=FULL,
    )


def shaped(shape, dtype):
    return jax.ShapeDtypeStruct(shape, dtype)


def tile(index, size):
    return pl.ds(pl.multiple_of(index * size, size), size)


def call(kernel, outs, operands, specs, scratch=(), flops=0, moved=0, limit=24, space=VMEM):
    return pl.pallas_call(
        kernel,
        out_shape=outs,
        in_specs=specs,
        out_specs=[space] * len(outs),
        scratch_shapes=list(scratch),
        compiler_params=pltpu.CompilerParams(vmem_limit_bytes=limit * 2**20),
        cost_estimate=pl.CostEstimate(flops=flops, bytes_accessed=moved, transcendentals=0),
    )(*operands)


def run_all(copies):
    for copy in copies:
        copy.start()
    for copy in copies:
        copy.wait()


TILES = 4
UPPER = [(i, j) for i in range(TILES) for j in range(i, TILES)]


def bases_kernel(where, left, right, out):
    out[0] = left[...].astype(HALF)
    out[1] = right[...].astype(HALF)


def stats_kernel(where, left, right, out, sem):
    size = out.shape[0]
    rows = size * TILES
    for core, stat in enumerate((left, right)):

        @pl.when(where[1] == core)
        def _():
            begin = where[0] * rows
            run_all(
                [
                    pltpu.make_async_copy(
                        stat.at[
                            i * size : (i + 1) * size,
                            pl.ds(pl.multiple_of(begin + j * size, size), size),
                        ],
                        out.at[:, place * size : (place + 1) * size],
                        sem.at[place],
                    )
                    for place, (i, j) in enumerate(UPPER)
                ]
            )


def first_sum_kernel(where, group, came, kept, sent):
    size = kept.shape[0]
    core, x = where[1], where[2]
    kept[...] = group[0, tile(core * 2 + x, size)].astype(FULL) + came[tile(x, size)].astype(FULL)
    sent[...] = group[0, tile(core * 2 + 1 - x, size)].astype(FULL) + came[
        tile(1 - x, size)
    ].astype(FULL)


def second_sum_kernel(where, kept, came, own, *sent):
    size = own.shape[0]
    z = where[3]
    own[...] = kept[tile(z, size)] + came[tile(z, size)]
    for k, out in enumerate(sent):
        there = tile(z ^ (k + 1), size)
        out[...] = kept[there] + came[there]


def third_sum_kernel(own, one, two, three, out):
    out[...] = ((own[...] + one[...]) + (two[...] + three[...])).astype(HALF)


def joined_kernel(where, *refs):
    out = refs[-1]
    z = where[3]
    size = refs[0].shape[0]
    for k, part in enumerate(refs[:-1]):
        out[tile(z ^ k, size)] = part[...]


def place_basis(where, out, own, mine, theirs, side):
    rows = own.shape[0]
    half = rows // 2
    position, core = where[0], where[1]
    out[tile(position, rows)] = own[...].astype(HALF)
    other = (1 - position) * 2
    out[tile(other + core, half)] = mine[side]
    out[tile(other + 1 - core, half)] = theirs[side]


def state_kernel(
    where, left, right, mine, theirs, stat_left, stat_right, came, bases, turned, back, full, sem
):
    rows, width = left.shape
    size = rows // TILES
    position, core = where[0], where[1]
    here, there = tile(position, rows), tile(1 - position, rows)
    for side, stat in enumerate((stat_left, stat_right)):

        @pl.when(core == side)
        def _():
            pltpu.make_async_copy(stat, full.at[here], sem).start()

    place_basis(where, bases.at[core], left, mine, theirs, 0)
    place_basis(where, bases.at[1 - core], right, mine, theirs, 1)
    turned[...] = bases[core].T
    back[...] = bases[1 - core].T
    base = (1 - position) * TILES
    for place, (i, j) in enumerate(UPPER):
        value = came[:, place * size : (place + 1) * size]
        full[tile(base + i, size), tile(base + j, size)] = value
        if i != j:
            full[tile(base + j, size), tile(base + i, size)] = value.T
    pltpu.make_async_copy(stat_left, full.at[here], sem).wait()
    full[there, here] = full[here, there].T


def moment_kernel(where, moment, bases, *refs):
    parts, (gradient, ours, others, sem) = refs[:-4], refs[-4:]
    position, core, x = where[0], where[1], where[2]
    size = parts[0].shape[0]
    rows = moment.shape[0]
    step = rows // 2
    copies = []
    for place, part in enumerate(parts):
        block = (
            (position ^ (place // 4)) * 4 + (core ^ (place % 4 // 2)) * 2 + (x ^ (place % 2))
        )
        copies.append(
            pltpu.make_async_copy(part, gradient.at[tile(block, size)], sem.at[place])
        )
    run_all(copies)
    half = (
        BETA_ONE * moment[...] + (1.0 - BETA_ONE) * gradient[tile(position, rows)].astype(FULL)
    ).astype(HALF)
    there, here = tile((1 - position) * 2 + core, step), tile(position * 2 + core, step)
    others[...] = matmul(half, bases[1 - core, :, there]).astype(HALF)
    ours[...] = matmul(half, bases[1 - core, :, here]).astype(HALF)


def adam_kernel(where, gradient, bases, turned, mine, came, second, new, kept, sent):
    width = gradient.shape[0]
    rows, step = mine.shape
    position, core = where[0], where[1]
    here, there = tile(position, rows), tile(1 - position, rows)
    block = matmul(gradient[...], bases[1 - core, :, tile(position * 2 + core, step)])
    grad_rot = matmul(turned[...], block.astype(HALF)) * (1.0 / width)
    moment_rot = (
        matmul(turned[:, here], mine[...]) + matmul(turned[:, there], came[...])
    ) * (1.0 / width)
    value = BETA_TWO * second[:, tile(core, step)] + (1.0 - BETA_TWO) * grad_rot * grad_rot
    new[...] = value
    scaled = (moment_rot / (jnp.sqrt(value) + EPSILON)).astype(HALF)
    sent[...] = matmul(bases[core, there], scaled).astype(HALF)
    kept[...] = matmul(bases[core, here], scaled).astype(HALF)


def update_kernel(
    where, kept, came, kept_next, came_next, back, new, new_next, out, second_new, rows_back, sem
):
    rows, width = out.shape
    step = kept.shape[1]
    position, core = where[0], where[1]
    copies = [
        pltpu.make_async_copy(value, second_new.at[:, tile(place, step)], sem.at[i])
        for i, (value, place) in enumerate(((new, core), (new_next, 1 - core)))
    ]
    for copy in copies:
        copy.start()
    for value, place in (
        (kept, position * 2 + core),
        (came, (1 - position) * 2 + core),
        (kept_next, position * 2 + 1 - core),
        (came_next, (1 - position) * 2 + 1 - core),
    ):
        rows_back[:, tile(place, step)] = value[...]
    for here in [slice(i * step, (i + 1) * step) for i in range(4)]:
        out[:, here] = (matmul(rows_back[...], back[:, here]) * (1.0 / width)).astype(HALF)
    for copy in copies:
        copy.wait()


def sides_kernel(where, mine, theirs, left, right, sem):
    for core, (one, two) in enumerate(((mine, theirs), (theirs, mine))):

        @pl.when(where[1] == core)
        def _():
            run_all(
                [
                    pltpu.make_async_copy(one, left, sem.at[0]),
                    pltpu.make_async_copy(two, right, sem.at[1]),
                ]
            )


def quarters(width):
    step = width // 4
    return [slice(i * step, (i + 1) * step) for i in range(4)]


def power_kernel(where, gradient, bases, stat, start, turned, pair, half):
    width = gradient.shape[0]
    core = where[1]
    for here in quarters(width):
        value = gradient[here]
        pair[core, here] = value
        pair[1 - core, :, here] = value.T
    for here in quarters(width):
        grads = matmul(pair[0], pair[1, :, here])
        half[:, here] = (BETA_STAT * stat[:, here] + (1.0 - BETA_STAT) * grads).astype(HALF)
    for here in quarters(width):
        product = matmul(half[...], bases[0, :, here])
        square = jnp.sum(product * product, axis=0, keepdims=True) * (1.0 / width)
        value = (product * lax.rsqrt(square + NORM_EPS)).astype(HALF)
        start[:, here] = value
        turned[here] = value.T


def refresh_kernel(where, start, start_turned, out, following, following_turned, gram):
    width = start.shape[0]
    rows = out.shape[0]

    def improved(current, turned, kept, result, result_turned):
        size = result.shape[0]
        for here in quarters(width):
            gram[:size, here] = (matmul(current[kept], turned[:, here]) * (1.0 / width)).astype(
                HALF
            )
        for here in quarters(width):
            value = (
                1.5 * current[kept, here].astype(FULL)
                - 0.5 * matmul(gram[:size], current[:, here])
            ).astype(result.dtype)
            result[:, here] = value
            if result_turned is not None:
                result_turned[here] = value.T

    current, turned = start, start_turned
    for iteration in range(NS_ITERS - 1):
        place = iteration % 2
        improved(current, turned, slice(0, width), following.at[place], following_turned.at[place])
        current, turned = following.at[place], following_turned.at[place]
    improved(current, turned, tile(where[0], rows), out, None)


def fast_body(group_grads, moment, second, stat_left, stat_right, basis_left, basis_right):
    position = lax.axis_index("shard")
    member = lax.axis_index("dp")
    rows, width = moment.shape
    half = rows // 2
    quarter = rows // 4
    chunk = rows // 16
    core, x, z = member & 1, (member >> 1) & 1, member >> 2
    where = jnp.stack([position, core, x, z]).astype(jnp.int32)
    unit = 2 * width**3

    def dp_swap(value, distance):
        return lax.ppermute(value, "dp", [(i, i ^ distance) for i in range(16)])

    def shard_swap(value):
        return lax.ppermute(value, "shard", [(0, 1), (1, 0)])

    def cross_swap(value):
        pairs = [(i, i ^ 5) for i in range(32)]
        return lax.ppermute(value, ("dp", "shard"), pairs)

    step = half // 2
    (bases_sent,) = pl.pallas_call(
        bases_kernel,
        out_shape=[shaped((2, half, width), HALF)],
        grid_spec=pltpu.PrefetchScalarGridSpec(
            num_scalar_prefetch=1,
            grid=(2,),
            in_specs=[pl.BlockSpec((step, width), lambda i, where: (where[1] * 2 + i, 0))] * 2,
            out_specs=[pl.BlockSpec((2, step, width), lambda i, where: (0, i, 0))],
        ),
        compiler_params=pltpu.CompilerParams(vmem_limit_bytes=56 * 2**20),
        cost_estimate=pl.CostEstimate(flops=0, bytes_accessed=2**22, transcendentals=0),
    )(where, basis_left, basis_right)
    bases_mine = shard_swap(bases_sent)

    raw = lax.dynamic_slice_in_dim(group_grads[0], (1 - core) * half, half, 0)
    came = dp_swap(raw, 1)
    kept, sent = call(
        first_sum_kernel,
        [shaped((quarter, width), FULL)] * 2,
        (where, group_grads, came),
        [SMEM, VMEM, VMEM],
        moved=2**21,
    )
    came = dp_swap(sent, 2)
    own, *sent = call(
        second_sum_kernel,
        [shaped((chunk, width), FULL)] * 4,
        (where, kept, came),
        [SMEM, VMEM, VMEM],
        moved=2**20,
    )
    (stats_sent,) = call(
        stats_kernel,
        [shaped((quarter, len(UPPER) * quarter), FULL)],
        (where, stat_left, stat_right),
        [SMEM, ANY, ANY],
        [pltpu.SemaphoreType.DMA((len(UPPER),))],
        moved=2**21,
        limit=56,
    )
    stats_mine = shard_swap(stats_sent)
    pieces = [dp_swap(value, 4 * (k + 1)) for k, value in enumerate(sent)]
    (piece,) = call(
        third_sum_kernel, [shaped((chunk, width), HALF)], (own, *pieces), [VMEM] * 4, moved=2**19
    )
    pieces = [piece] + [dp_swap(piece, 4 * k) for k in (1, 2, 3)]
    (part,) = call(
        joined_kernel, [shaped((quarter, width), HALF)], (where, *pieces), [SMEM] + [VMEM] * 4,
        moved=2**19,
    )
    part, bases_mine, stats_mine = lax.optimization_barrier((part, bases_mine, stats_mine))
    parts = [part, dp_swap(part, 2), shard_swap(part), cross_swap(part)]

    bases_theirs = dp_swap(bases_mine, 1)
    square = shaped((width, width), HALF)
    bases, left_turned, right_turned, stat = call(
        state_kernel,
        [shaped((2, width, width), HALF), square, square, shaped((width, width), FULL)],
        (
            where,
            basis_left,
            basis_right,
            bases_mine,
            bases_theirs,
            stat_left,
            stat_right,
            stats_mine,
        ),
        [SMEM] + [VMEM] * 4 + [ANY] * 2 + [VMEM],
        [pltpu.SemaphoreType.DMA(())],
        moved=2**24,
    )
    parts[2], parts[3], bases = lax.optimization_barrier((parts[2], parts[3], bases))
    swapped = [dp_swap(value, 1) for value in parts]
    ordered = [parts[0], parts[1], swapped[0], swapped[1], parts[2], parts[3], swapped[2], swapped[3]]
    gradient, moment_mine, moment_sent = call(
        moment_kernel,
        [square] + [shaped((rows, half), HALF)] * 2,
        (where, moment, bases, *ordered),
        [SMEM, VMEM, VMEM] + [ANY] * 8,
        [pltpu.SemaphoreType.DMA((8,))],
        flops=unit // 4,
        moved=2**22,
    )
    moment_came = shard_swap(moment_sent)
    start, start_turned = call(
        power_kernel,
        [square] * 2,
        (where, gradient, bases, stat),
        [SMEM] + [VMEM] * 3,
        [pltpu.VMEM((2, width, width), HALF), pltpu.VMEM((width, width), HALF)],
        flops=2 * unit,
        moved=2**23,
    )
    new, back_kept, back_sent = call(
        adam_kernel,
        [shaped((width, half), FULL)] + [shaped((rows, half), HALF)] * 2,
        (where, gradient, bases, left_turned, moment_mine, moment_came, second),
        [SMEM] + [VMEM] * 6,
        flops=unit,
        moved=2**22,
    )
    start, back_sent = lax.optimization_barrier((start, back_sent))
    back_came = shard_swap(back_sent)
    new_next = dp_swap(new, 1)
    back_kept_next = dp_swap(back_kept, 1)
    (side_new,) = call(
        refresh_kernel,
        [shaped((rows, width), FULL)],
        (where, start, start_turned),
        [SMEM] + [VMEM] * 2,
        [pltpu.VMEM((2, width, width), HALF)] * 2 + [pltpu.VMEM((width, width), HALF)],
        flops=3 * unit,
        moved=2**22,
    )
    side_next = dp_swap(side_new, 1)
    back_came_next = dp_swap(back_came, 1)
    update, second_new = pl.pallas_call(
        update_kernel,
        out_shape=[shaped((rows, width), HALF), shaped((width, rows), FULL)],
        in_specs=[SMEM] + [VMEM] * 5 + [ANY] * 2,
        out_specs=[VMEM, ANY],
        scratch_shapes=[pltpu.VMEM((rows, width), HALF), pltpu.SemaphoreType.DMA((2,))],
        compiler_params=pltpu.CompilerParams(vmem_limit_bytes=24 * 2**20),
        cost_estimate=pl.CostEstimate(
            flops=unit // 2, bytes_accessed=2**23, transcendentals=0
        ),
    )(
        where,
        back_kept,
        back_came,
        back_kept_next,
        back_came_next,
        right_turned,
        new,
        new_next,
    )
    left_new, right_new = call(
        sides_kernel,
        [shaped((rows, width), FULL)] * 2,
        (where, side_new, side_next),
        [SMEM, ANY, ANY],
        [pltpu.SemaphoreType.DMA((2,))],
        moved=2**23,
        space=ANY,
    )
    return (update, second_new, left_new, right_new)


def make_plain_body(n_dp, n_shard):
    def swap(value, axis, distance):
        size = n_dp if axis == "dp" else n_shard
        return lax.ppermute(value, axis, [(i, i ^ distance) for i in range(size)])

    dp_bits = []
    bit = 1
    while bit < n_dp:
        dp_bits.append(bit)
        bit *= 2

    def ordered(first_is_low, own, other, dim):
        return jnp.where(
            first_is_low,
            jnp.concatenate([own, other], dim),
            jnp.concatenate([other, own], dim),
        )

    def body(group_grads, moment, second, stat_left, stat_right, basis_left, basis_right):
        position = lax.axis_index("shard")
        member = lax.axis_index("dp")
        rows, width = moment.shape
        core = member & 1
        half = rows // 2

        def near_columns(value):
            blocks = [
                lax.dynamic_slice_in_dim(value, (position ^ k) * rows, rows, 1)
                for k in range(n_shard)
            ]
            return jnp.concatenate(blocks, 1)

        def fetch(value, distance):
            size = value.shape[0] // 2
            part = lax.dynamic_slice_in_dim(value, core * size, size, 0)
            part = swap(part, "shard", distance)
            other = swap(part, "dp", 1)
            return ordered(core == 0, part, other, 0)

        left_own = basis_left.astype(jnp.bfloat16)
        right_own = basis_right.astype(jnp.bfloat16)
        left_rot = jnp.concatenate([left_own] + [fetch(left_own, k) for k in range(1, n_shard)], 0)
        right_rot = jnp.concatenate(
            [right_own] + [fetch(right_own, k) for k in range(1, n_shard)], 0
        )

        def whole_stat(stat):
            own = near_columns(stat)
            blocks = [own[:, b * rows : (b + 1) * rows] for b in range(n_shard)]
            bands = [own]
            for k in range(1, n_shard):
                others = [b for b in range(n_shard) if b != k]
                sent = jnp.concatenate([blocks[b] for b in others], 1).astype(jnp.bfloat16)
                came = fetch(sent, k).astype(jnp.float32)
                band = [None] * n_shard
                band[0] = blocks[k].T
                for place, b in enumerate(others):
                    band[k ^ b] = came[:, place * rows : (place + 1) * rows]
                bands.append(jnp.concatenate(band, 1))
            return jnp.concatenate(bands, 0)

        stat_left_full = whole_stat(stat_left)
        stat_right_full = whole_stat(stat_right)

        part = group_grads[0]
        for bit in dp_bits:
            size = part.shape[0] // 2
            high = (member & bit) // bit
            kept = lax.dynamic_slice_in_dim(part, high * size, size, 0)
            sent = lax.dynamic_slice_in_dim(part, (1 - high) * size, size, 0)
            part = kept.astype(jnp.float32) + swap(sent, "dp", bit).astype(jnp.float32)
        chunk = part.astype(jnp.bfloat16)[None]
        chunk = jnp.concatenate([chunk] + [swap(chunk, "shard", k) for k in range(1, n_shard)], 0)
        for bit in reversed(dp_bits):
            chunk = ordered((member & bit) == 0, chunk, swap(chunk, "dp", bit), 1)
        gradient = near_columns(chunk.reshape(width, width))

        grad_rows = gradient[:rows].astype(jnp.float32)
        moment_half = (
            BETA_ONE * near_columns(moment) + (1.0 - BETA_ONE) * grad_rows
        ).astype(jnp.bfloat16)
        near_rot = near_columns(right_rot)
        moment_turned = matmul(moment_half, near_rot).astype(jnp.bfloat16)
        moment_block = jnp.concatenate(
            [moment_turned[:, :rows]]
            + [
                swap(moment_turned[:, k * rows : (k + 1) * rows], "shard", k)
                for k in range(1, n_shard)
            ],
            0,
        )
        grad_block = matmul(gradient, near_rot[:, :rows]).astype(jnp.bfloat16)
        grad_rot = matmul(left_rot, grad_block, 0) / width
        moment_rot = matmul(left_rot, moment_block, 0) / width
        second_new = BETA_TWO * second + (1.0 - BETA_TWO) * grad_rot * grad_rot
        scaled = (moment_rot / (jnp.sqrt(second_new) + EPSILON)).astype(jnp.bfloat16)
        turned_back = matmul(left_rot, scaled).astype(jnp.bfloat16)
        back_rows = jnp.concatenate(
            [turned_back[:rows]]
            + [
                swap(turned_back[k * rows : (k + 1) * rows], "shard", k)
                for k in range(1, n_shard)
            ],
            1,
        )
        update = (near_columns(matmul(back_rows, near_rot, 1, 1)) / width).astype(jnp.bfloat16)

        def refreshed(stat, product_of_grads, rot):
            stat_new = BETA_STAT * stat + (1.0 - BETA_STAT) * product_of_grads
            product = matmul(stat_new.astype(jnp.bfloat16), rot)
            start = product / jnp.sqrt(jnp.sum(product * product, axis=0) / width + NORM_EPS)
            current = start.astype(jnp.bfloat16)
            for iteration in range(NS_ITERS):
                kept = width if iteration + 1 < NS_ITERS else rows
                gram = (matmul(current[:kept], current, 1, 1) / width).astype(jnp.bfloat16)
                result = 1.5 * current[:kept].astype(jnp.float32) - 0.5 * matmul(gram, current)
                current = result.astype(jnp.bfloat16)
            return result

        left_new = refreshed(stat_left_full, matmul(gradient, gradient, 1, 1), left_rot)
        right_new = refreshed(stat_right_full, matmul(gradient, gradient, 0, 0), right_rot)
        return (update, second_new, left_new, right_new)

    return body


def solution(mesh):
    n_dp, n_shard = mesh.shape["dp"], mesh.shape["shard"]
    body = fast_body if (n_dp, n_shard) == (16, 2) else make_plain_body(n_dp, n_shard)
    return jax.shard_map(
        body,
        mesh=mesh,
        in_specs=(
            P("dp", "shard", None),
            P("shard", None),
            P(None, "shard"),
            P("shard", None),
            P("shard", None),
            P("shard", None),
            P("shard", None),
        ),
        out_specs=(P("shard", None), P(None, "shard"), P("shard", None), P("shard", None)),
        check_vma=False,
    )
```

```python
import jax
import jax.numpy as jnp
from jax import lax
from jax.experimental import pallas as pl
from jax.experimental.pallas import tpu as pltpu
from jax.sharding import PartitionSpec as P

NS_ITERS = 2


BETA_ONE = 0.9
BETA_TWO = 0.9
BETA_STAT = 0.95
EPSILON = 1e-08
NORM_EPS = 1e-06
HALF = jnp.bfloat16
FULL = jnp.float32
VMEM = pl.BlockSpec(memory_space=pltpu.VMEM)
ANY = pl.BlockSpec(memory_space=pl.ANY)
SMEM = pl.BlockSpec(memory_space=pltpu.SMEM)


def matmul(left_mat, right_mat, left_dim=1, right_dim=0):
    return lax.dot_general(
        left_mat,
        right_mat,
        (((left_dim,), (right_dim,)), ((), ())),
        preferred_element_type=FULL,
    )


def shaped(shape, dtype):
    return jax.ShapeDtypeStruct(shape, dtype)


def tile(index, size):
    return pl.ds(pl.multiple_of(index * size, size), size)


def call(
    kernel, outs, operands, specs, scratch=(), flops=0, moved=0, limit=24, space=VMEM, aliases=None
):
    return pl.pallas_call(
        kernel,
        out_shape=outs,
        in_specs=specs,
        out_specs=[space] * len(outs),
        scratch_shapes=list(scratch),
        input_output_aliases=aliases or {},
        compiler_params=pltpu.CompilerParams(vmem_limit_bytes=limit * 2**20),
        cost_estimate=pl.CostEstimate(flops=flops, bytes_accessed=moved, transcendentals=0),
    )(*operands)


def run_all(copies):
    for copy in copies:
        copy.start()
    for copy in copies:
        copy.wait()


TILES = 4
UPPER = [(i, j) for i in range(TILES) for j in range(i, TILES)]


def start_kernel(
    where,
    group,
    came,
    left,
    right,
    stat_left,
    stat_right,
    state,
    near_kept,
    near_sent,
    kept,
    far_1,
    far_2,
    far_3,
    basis_in,
    stat_in,
    sem,
):
    position, core, x, z = where[0], where[1], where[2], where[3]
    half, width = basis_in.shape[1:]
    size = state.shape[1]
    bases = [
        pltpu.make_async_copy(basis.at[tile(core, half)], basis_in.at[i], sem.at[i])
        for i, basis in enumerate((left, right))
    ]
    for copy in bases:
        copy.start()
    for side, stat in enumerate((stat_left, stat_right)):

        @pl.when(core == side)
        def _():
            pltpu.make_async_copy(stat.at[:, tile(position, size * TILES)], stat_in, sem.at[2]).start()

    rows, cut = near_kept.shape
    for out, there in ((near_kept, x), (near_sent, 1 - x)):
        out[...] = group[0, tile(core * 2 + there, rows), :cut].astype(FULL) + came[
            tile(there, rows), :cut
        ].astype(FULL)
    rows = kept.shape[0] // 2
    for k, out in enumerate((kept, far_1, far_2, far_3)):
        for i in range(2):
            there = i * 4 + (z ^ k)
            out[i * rows : (i + 1) * rows] = group[0, tile(core * 8 + there, rows), cut:].astype(
                FULL
            ) + came[tile(there, rows), cut:].astype(FULL)
    for copy in bases:
        copy.wait()
    across = width // size
    for band in range(2 * half // size):
        for column in range(across):
            begin = band * size % half
            state[band * across + column] = basis_in[
                band * size // half, begin : begin + size, column * size : (column + 1) * size
            ].astype(HALF)
    pltpu.make_async_copy(stat_left.at[:, : size * TILES], stat_in, sem.at[2]).wait()
    base = 2 * half * width // size**2
    for place, (i, j) in enumerate(UPPER):
        value = stat_in[i * size : (i + 1) * size, j * size : (j + 1) * size]
        high = value.astype(HALF)
        state[base + place] = high
        state[base + len(UPPER) + place] = (value - high.astype(FULL)).astype(HALF)


def second_sum_kernel(
    where, near_kept, near_came, kept, one, two, three, near_own, near_1, near_2, near_3, own, sent
):
    size = near_own.shape[0]
    x, z = where[2], where[3]
    for k, out in enumerate((near_own, near_1, near_2, near_3)):
        there = tile(z ^ k, size)
        out[...] = near_kept[there] + near_came[there]
    for k, out in enumerate((own, sent)):
        there = tile(x ^ k, size)
        out[...] = (kept[there] + one[there]) + (two[there] + three[there])


def third_sum_kernel(near_own, one, two, three, own, came, out):
    cut = near_own.shape[1]
    out[:, :cut] = ((near_own[...] + one[...]) + (two[...] + three[...])).astype(HALF)
    out[:, cut:] = (own[...] + came[...]).astype(HALF)


def joined_kernel(where, *refs):
    out = refs[-1]
    z = where[3]
    size = refs[0].shape[0]
    for k, part in enumerate(refs[:-1]):
        out[tile(z ^ k, size)] = part[...]


def place_basis(where, out, own, mine, theirs, side):
    rows, width = own.shape
    half = rows // 2
    size = mine.shape[1]
    position, core = where[0], where[1]
    across = width // size
    count = half // size * across
    out[tile(position, rows)] = own[...].astype(HALF)
    other = (1 - position) * 2
    for part, block in ((mine, other + core), (theirs, other + 1 - core)):
        for band in range(half // size):
            here = tile(block * (half // size) + band, size)
            for column in range(across):
                out[here, column * size : (column + 1) * size] = part[
                    side * count + band * across + column
                ]


def state_kernel(
    where, left, right, mine, theirs, stat_left, stat_right, bases, turned, back, full, sem
):
    rows, width = left.shape
    size = rows // TILES
    position, core = where[0], where[1]
    here, there = tile(position, rows), tile(1 - position, rows)
    for side, stat in enumerate((stat_left, stat_right)):

        @pl.when(core == side)
        def _():
            pltpu.make_async_copy(stat, full.at[here], sem).start()

    place_basis(where, bases.at[core], left, mine, theirs, 0)
    place_basis(where, bases.at[1 - core], right, mine, theirs, 1)
    turned[...] = bases[core].T
    back[...] = bases[1 - core].T
    base = (1 - position) * TILES
    first = rows * width // size**2
    for place, (i, j) in enumerate(UPPER):
        value = mine[first + place].astype(FULL) + mine[first + len(UPPER) + place].astype(FULL)
        full[tile(base + i, size), tile(base + j, size)] = value
        if i != j:
            full[tile(base + j, size), tile(base + i, size)] = value.T
    pltpu.make_async_copy(stat_left, full.at[here], sem).wait()
    full[there, here] = full[here, there].T


def moment_kernel(where, moment, bases, *refs):
    parts, (gradient, ours, others, sem) = refs[:-4], refs[-4:]
    position, core, x = where[0], where[1], where[2]
    rows = moment.shape[0]
    step = rows // 2
    copies = []
    for place, part in enumerate(parts):
        size = part.shape[0]
        block = (
            (position ^ (place // 4)) * 4 + (core ^ (place // 2 % 2)) * 2 + (x ^ (place % 2))
        )
        copies.append(pltpu.make_async_copy(part, gradient.at[tile(block, size)], sem.at[place]))
    run_all(copies)
    half = (
        BETA_ONE * moment[...] + (1.0 - BETA_ONE) * gradient[tile(position, rows)].astype(FULL)
    ).astype(HALF)
    there, here = tile((1 - position) * 2 + core, step), tile(position * 2 + core, step)
    others[...] = matmul(half, bases[1 - core, :, there]).astype(HALF)
    ours[...] = matmul(half, bases[1 - core, :, here]).astype(HALF)


def adam_kernel(where, gradient, bases, turned, mine, came, second, new, kept, sent):
    width = gradient.shape[0]
    rows, step = mine.shape
    position, core = where[0], where[1]
    here, there = tile(position, rows), tile(1 - position, rows)
    block = matmul(gradient[...], bases[1 - core, :, tile(position * 2 + core, step)])
    grad_rot = matmul(turned[...], block.astype(HALF)) * (1.0 / width)
    moment_rot = (
        matmul(turned[:, here], mine[...]) + matmul(turned[:, there], came[...])
    ) * (1.0 / width)
    value = BETA_TWO * second[:, tile(core, step)] + (1.0 - BETA_TWO) * grad_rot * grad_rot
    new[...] = value
    scaled = (moment_rot / (jnp.sqrt(value) + EPSILON)).astype(HALF)
    sent[...] = matmul(bases[core, there], scaled).astype(HALF)
    kept[...] = matmul(bases[core, here], scaled).astype(HALF)


def update_kernel(
    where, kept, came, kept_next, came_next, back, new, new_next, out, second_new, rows_back, sem
):
    rows, width = out.shape
    step = kept.shape[1]
    position, core = where[0], where[1]
    copies = [
        pltpu.make_async_copy(value, second_new.at[:, tile(place, step)], sem.at[i])
        for i, (value, place) in enumerate(((new, core), (new_next, 1 - core)))
    ]
    for copy in copies:
        copy.start()
    for value, place in (
        (kept, position * 2 + core),
        (came, (1 - position) * 2 + core),
        (kept_next, position * 2 + 1 - core),
        (came_next, (1 - position) * 2 + 1 - core),
    ):
        rows_back[:, tile(place, step)] = value[...]
    for here in [slice(i * step, (i + 1) * step) for i in range(4)]:
        out[:, here] = (matmul(rows_back[...], back[:, here]) * (1.0 / width)).astype(HALF)
    for copy in copies:
        copy.wait()


def write_sides(core, top, low, side, left, right, sem):
    half = top.shape[0]
    for place, out in enumerate((left, right)):

        @pl.when((core ^ side) == place)
        def _():
            run_all(
                [
                    pltpu.make_async_copy(top, out.at[:half], sem.at[0]),
                    pltpu.make_async_copy(low, out.at[half:], sem.at[1]),
                ]
            )


def own_side_kernel(where, top, low, left, right, sem):
    write_sides(where[1], top, low, 0, left, right, sem)


def next_side_kernel(where, top, low, left_in, right_in, left, right, sem):
    write_sides(where[1], top, low, 1, left, right, sem)


def quarters(width):
    step = width // 4
    return [slice(i * step, (i + 1) * step) for i in range(4)]


def power_kernel(where, gradient, bases, stat, start, turned, pair, half):
    width = gradient.shape[0]
    core = where[1]
    for here in quarters(width):
        value = gradient[here]
        pair[core, here] = value
        pair[1 - core, :, here] = value.T
    for here in quarters(width):
        grads = matmul(pair[0], pair[1, :, here])
        half[:, here] = (BETA_STAT * stat[:, here] + (1.0 - BETA_STAT) * grads).astype(HALF)
    for here in quarters(width):
        product = matmul(half[...], bases[0, :, here])
        square = jnp.sum(product * product, axis=0, keepdims=True) * (1.0 / width)
        value = (product * lax.rsqrt(square + NORM_EPS)).astype(HALF)
        start[:, here] = value
        turned[here] = value.T


def improved(current, turned, kept, gram, result, result_turned):
    size, width = result.shape
    for here in quarters(width):
        gram[:size, here] = (matmul(current[kept], turned[:, here]) * (1.0 / width)).astype(HALF)
    for here in quarters(width):
        value = (
            1.5 * current[kept, here].astype(FULL) - 0.5 * matmul(gram[:size], current[:, here])
        ).astype(result.dtype)
        result[:, here] = value
        if result_turned is not None:
            result_turned[here] = value.T


def refresh_kernel(where, start, start_turned, current, turned, out, *scratch):
    width = start.shape[0]
    rows = width // 2
    gram, between = scratch[0], scratch[1:]
    source, source_turned = start, start_turned
    for iteration in range(NS_ITERS - 1):
        last = iteration + 2 == NS_ITERS
        if last:
            result, result_turned = current, turned
        else:
            result, result_turned = between[0].at[iteration % 2], between[1].at[iteration % 2]
        improved(source, source_turned, slice(0, width), gram, result, result_turned)
        source, source_turned = result, result_turned
    improved(current, turned, tile(where[0] * 2, rows // 2), gram, out, None)


def last_kernel(where, current, turned, out, gram):
    improved(current, turned, tile(where[0] * 2 + 1, out.shape[0]), gram, out, None)


def fast_body(group_grads, moment, second, stat_left, stat_right, basis_left, basis_right):
    position = lax.axis_index("shard")
    member = lax.axis_index("dp")
    rows, width = moment.shape
    half = rows // 2
    quarter = rows // 4
    chunk = rows // 16
    core, x, z = member & 1, (member >> 1) & 1, member >> 2
    where = jnp.stack([position, core, x, z]).astype(jnp.int32)
    unit = 2 * width**3

    def dp_swap(value, distance):
        return lax.ppermute(value, "dp", [(i, i ^ distance) for i in range(16)])

    def shard_swap(value):
        return lax.ppermute(value, "shard", [(0, 1), (1, 0)])

    def cross_swap(value):
        pairs = [(i, i ^ 5) for i in range(32)]
        return lax.ppermute(value, ("dp", "shard"), pairs)

    raw = lax.dynamic_slice_in_dim(group_grads[0], (1 - core) * half, half, 0)
    came = dp_swap(raw, 1)
    cut = width * 5 // 8
    rest = width - cut
    tiles = rows * width // quarter**2 + 2 * len(UPPER)
    state_sent, near_kept, near_sent, kept, *sent = call(
        start_kernel,
        [shaped((tiles, quarter, quarter), HALF)]
        + [shaped((quarter, cut), FULL)] * 2
        + [shaped((quarter // 2, rest), FULL)] * 4,
        (where, group_grads, came, basis_left, basis_right, stat_left, stat_right),
        [SMEM] + [VMEM] * 2 + [ANY] * 4,
        [
            pltpu.VMEM((2, half, width), FULL),
            pltpu.VMEM((rows, rows), FULL),
            pltpu.SemaphoreType.DMA((3,)),
        ],
        moved=2**22,
        limit=52,
    )
    near_came = dp_swap(near_sent, 2)
    came = [dp_swap(value, 4 * (k + 1)) for k, value in enumerate(sent)]
    state_mine = shard_swap(state_sent)
    near_own, *near_sent, own, sent = call(
        second_sum_kernel,
        [shaped((chunk, cut), FULL)] * 4 + [shaped((chunk, rest), FULL)] * 2,
        (where, near_kept, near_came, kept, *came),
        [SMEM] + [VMEM] * 6,
        moved=2**20,
    )
    near_came = [dp_swap(value, 4 * (k + 1)) for k, value in enumerate(near_sent)]
    came = dp_swap(sent, 2)
    (piece,) = call(
        third_sum_kernel,
        [shaped((chunk, width), HALF)],
        (near_own, *near_came, own, came),
        [VMEM] * 6,
        moved=2**19,
    )
    pieces = [piece] + [dp_swap(piece, 4 * k) for k in (1, 2, 3)]
    (part,) = call(
        joined_kernel,
        [shaped((quarter, width), HALF)],
        (where, *pieces),
        [SMEM] + [VMEM] * 4,
        moved=2**19,
    )
    part, state_mine = lax.optimization_barrier((part, state_mine))
    parts = [part, dp_swap(part, 2), shard_swap(part), cross_swap(part)]

    state_theirs = dp_swap(state_mine, 1)
    square = shaped((width, width), HALF)
    bases, left_turned, right_turned, stat = call(
        state_kernel,
        [shaped((2, width, width), HALF), square, square, shaped((width, width), FULL)],
        (
            where,
            basis_left,
            basis_right,
            state_mine,
            state_theirs,
            stat_left,
            stat_right,
        ),
        [SMEM] + [VMEM] * 4 + [ANY] * 2,
        [pltpu.SemaphoreType.DMA(())],
        moved=2**24,
    )
    parts[2], parts[3], bases = lax.optimization_barrier((parts[2], parts[3], bases))
    swapped = [dp_swap(value, 1) for value in parts]
    ordered = parts[:2] + swapped[:2] + parts[2:] + swapped[2:]
    gradient, moment_mine, moment_sent = call(
        moment_kernel,
        [square] + [shaped((rows, half), HALF)] * 2,
        (where, moment, bases, *ordered),
        [SMEM, VMEM, VMEM] + [ANY] * 8,
        [pltpu.SemaphoreType.DMA((8,))],
        flops=unit // 4,
        moved=2**22,
    )
    moment_came = shard_swap(moment_sent)
    start, start_turned = call(
        power_kernel,
        [square] * 2,
        (where, gradient, bases, stat),
        [SMEM] + [VMEM] * 3,
        [pltpu.VMEM((2, width, width), HALF), pltpu.VMEM((width, width), HALF)],
        flops=2 * unit,
        moved=2**23,
    )
    new, back_kept, back_sent = call(
        adam_kernel,
        [shaped((width, half), FULL)] + [shaped((rows, half), HALF)] * 2,
        (where, gradient, bases, left_turned, moment_mine, moment_came, second),
        [SMEM] + [VMEM] * 6,
        flops=unit,
        moved=2**22,
    )
    start, back_sent = lax.optimization_barrier((start, back_sent))
    back_came = shard_swap(back_sent)
    new_next = dp_swap(new, 1)
    back_kept_next = dp_swap(back_kept, 1)
    current, current_turned, top = call(
        refresh_kernel,
        [square] * 2 + [shaped((half, width), FULL)],
        (where, start, start_turned),
        [SMEM] + [VMEM] * 2,
        [pltpu.VMEM((width, width), HALF)]
        + [pltpu.VMEM((2, width, width), HALF)] * (2 if NS_ITERS > 2 else 0),
        flops=5 * unit // 2,
        moved=2**22,
    )
    top_next = dp_swap(top, 1)
    current, back_came = lax.optimization_barrier((current, back_came))
    (low,) = call(
        last_kernel,
        [shaped((half, width), FULL)],
        (where, current, current_turned),
        [SMEM] + [VMEM] * 2,
        [pltpu.VMEM((half, width), HALF)],
        flops=unit // 2,
        moved=2**21,
    )
    low_next = dp_swap(low, 1)
    back_came_next = dp_swap(back_came, 1)
    update, second_new = pl.pallas_call(
        update_kernel,
        out_shape=[shaped((rows, width), HALF), shaped((width, rows), FULL)],
        in_specs=[SMEM] + [VMEM] * 5 + [ANY] * 2,
        out_specs=[VMEM, ANY],
        scratch_shapes=[pltpu.VMEM((rows, width), HALF), pltpu.SemaphoreType.DMA((2,))],
        compiler_params=pltpu.CompilerParams(vmem_limit_bytes=24 * 2**20),
        cost_estimate=pl.CostEstimate(
            flops=unit // 2, bytes_accessed=2**23, transcendentals=0
        ),
    )(
        where,
        back_kept,
        back_came,
        back_kept_next,
        back_came_next,
        right_turned,
        new,
        new_next,
    )
    sides = [shaped((rows, width), FULL)] * 2
    left_new, right_new = call(
        own_side_kernel,
        sides,
        (where, top, low),
        [SMEM, ANY, ANY],
        [pltpu.SemaphoreType.DMA((2,))],
        moved=2**22,
        space=ANY,
    )
    left_new, right_new = call(
        next_side_kernel,
        sides,
        (where, top_next, low_next, left_new, right_new),
        [SMEM] + [ANY] * 4,
        [pltpu.SemaphoreType.DMA((2,))],
        moved=2**22,
        space=ANY,
        aliases={3: 0, 4: 1},
    )
    return (update, second_new, left_new, right_new)


def make_plain_body(n_dp, n_shard):
    def swap(value, axis, distance):
        size = n_dp if axis == "dp" else n_shard
        return lax.ppermute(value, axis, [(i, i ^ distance) for i in range(size)])

    dp_bits = []
    bit = 1
    while bit < n_dp:
        dp_bits.append(bit)
        bit *= 2

    def ordered(first_is_low, own, other, dim):
        return jnp.where(
            first_is_low,
            jnp.concatenate([own, other], dim),
            jnp.concatenate([other, own], dim),
        )

    def body(group_grads, moment, second, stat_left, stat_right, basis_left, basis_right):
        position = lax.axis_index("shard")
        member = lax.axis_index("dp")
        rows, width = moment.shape
        core = member & 1
        half = rows // 2

        def near_columns(value):
            blocks = [
                lax.dynamic_slice_in_dim(value, (position ^ k) * rows, rows, 1)
                for k in range(n_shard)
            ]
            return jnp.concatenate(blocks, 1)

        def fetch(value, distance):
            size = value.shape[0] // 2
            part = lax.dynamic_slice_in_dim(value, core * size, size, 0)
            part = swap(part, "shard", distance)
            other = swap(part, "dp", 1)
            return ordered(core == 0, part, other, 0)

        left_own = basis_left.astype(jnp.bfloat16)
        right_own = basis_right.astype(jnp.bfloat16)
        left_rot = jnp.concatenate([left_own] + [fetch(left_own, k) for k in range(1, n_shard)], 0)
        right_rot = jnp.concatenate(
            [right_own] + [fetch(right_own, k) for k in range(1, n_shard)], 0
        )

        def whole_stat(stat):
            own = near_columns(stat)
            blocks = [own[:, b * rows : (b + 1) * rows] for b in range(n_shard)]
            bands = [own]
            for k in range(1, n_shard):
                others = [b for b in range(n_shard) if b != k]
                sent = jnp.concatenate([blocks[b] for b in others], 1).astype(jnp.bfloat16)
                came = fetch(sent, k).astype(jnp.float32)
                band = [None] * n_shard
                band[0] = blocks[k].T
                for place, b in enumerate(others):
                    band[k ^ b] = came[:, place * rows : (place + 1) * rows]
                bands.append(jnp.concatenate(band, 1))
            return jnp.concatenate(bands, 0)

        stat_left_full = whole_stat(stat_left)
        stat_right_full = whole_stat(stat_right)

        part = group_grads[0]
        for bit in dp_bits:
            size = part.shape[0] // 2
            high = (member & bit) // bit
            kept = lax.dynamic_slice_in_dim(part, high * size, size, 0)
            sent = lax.dynamic_slice_in_dim(part, (1 - high) * size, size, 0)
            part = kept.astype(jnp.float32) + swap(sent, "dp", bit).astype(jnp.float32)
        chunk = part.astype(jnp.bfloat16)[None]
        chunk = jnp.concatenate([chunk] + [swap(chunk, "shard", k) for k in range(1, n_shard)], 0)
        for bit in reversed(dp_bits):
            chunk = ordered((member & bit) == 0, chunk, swap(chunk, "dp", bit), 1)
        gradient = near_columns(chunk.reshape(width, width))

        grad_rows = gradient[:rows].astype(jnp.float32)
        moment_half = (
            BETA_ONE * near_columns(moment) + (1.0 - BETA_ONE) * grad_rows
        ).astype(jnp.bfloat16)
        near_rot = near_columns(right_rot)
        moment_turned = matmul(moment_half, near_rot).astype(jnp.bfloat16)
        moment_block = jnp.concatenate(
            [moment_turned[:, :rows]]
            + [
                swap(moment_turned[:, k * rows : (k + 1) * rows], "shard", k)
                for k in range(1, n_shard)
            ],
            0,
        )
        grad_block = matmul(gradient, near_rot[:, :rows]).astype(jnp.bfloat16)
        grad_rot = matmul(left_rot, grad_block, 0) / width
        moment_rot = matmul(left_rot, moment_block, 0) / width
        second_new = BETA_TWO * second + (1.0 - BETA_TWO) * grad_rot * grad_rot
        scaled = (moment_rot / (jnp.sqrt(second_new) + EPSILON)).astype(jnp.bfloat16)
        turned_back = matmul(left_rot, scaled).astype(jnp.bfloat16)
        back_rows = jnp.concatenate(
            [turned_back[:rows]]
            + [
                swap(turned_back[k * rows : (k + 1) * rows], "shard", k)
                for k in range(1, n_shard)
            ],
            1,
        )
        update = (near_columns(matmul(back_rows, near_rot, 1, 1)) / width).astype(jnp.bfloat16)

        def refreshed(stat, product_of_grads, rot):
            stat_new = BETA_STAT * stat + (1.0 - BETA_STAT) * product_of_grads
            product = matmul(stat_new.astype(jnp.bfloat16), rot)
            start = product / jnp.sqrt(jnp.sum(product * product, axis=0) / width + NORM_EPS)
            current = start.astype(jnp.bfloat16)
            for iteration in range(NS_ITERS):
                kept = width if iteration + 1 < NS_ITERS else rows
                gram = (matmul(current[:kept], current, 1, 1) / width).astype(jnp.bfloat16)
                result = 1.5 * current[:kept].astype(jnp.float32) - 0.5 * matmul(gram, current)
                current = result.astype(jnp.bfloat16)
            return result

        left_new = refreshed(stat_left_full, matmul(gradient, gradient, 1, 1), left_rot)
        right_new = refreshed(stat_right_full, matmul(gradient, gradient, 0, 0), right_rot)
        return (update, second_new, left_new, right_new)

    return body


def solution(mesh):
    n_dp, n_shard = mesh.shape["dp"], mesh.shape["shard"]
    body = fast_body if (n_dp, n_shard) == (16, 2) else make_plain_body(n_dp, n_shard)
    return jax.shard_map(
        body,
        mesh=mesh,
        in_specs=(
            P("dp", "shard", None),
            P("shard", None),
            P(None, "shard"),
            P("shard", None),
            P("shard", None),
            P("shard", None),
            P("shard", None),
        ),
        out_specs=(P("shard", None), P(None, "shard"), P("shard", None), P("shard", None)),
        check_vma=False,
    )
```

```python
import jax
import jax.numpy as jnp
from jax import lax
from jax.experimental import pallas as pl
from jax.experimental.pallas import tpu as pltpu
from jax.sharding import PartitionSpec as P

NS_ITERS = 2


BETA_ONE = 0.9
BETA_TWO = 0.9
BETA_STAT = 0.95
EPSILON = 1e-08
NORM_EPS = 1e-06
HALF = jnp.bfloat16
FULL = jnp.float32
VMEM = pl.BlockSpec(memory_space=pltpu.VMEM)
ANY = pl.BlockSpec(memory_space=pl.ANY)
SMEM = pl.BlockSpec(memory_space=pltpu.SMEM)


def matmul(left_mat, right_mat, left_dim=1, right_dim=0):
    return lax.dot_general(
        left_mat,
        right_mat,
        (((left_dim,), (right_dim,)), ((), ())),
        preferred_element_type=FULL,
    )


def shaped(shape, dtype):
    return jax.ShapeDtypeStruct(shape, dtype)


def tile(index, size):
    return pl.ds(pl.multiple_of(index * size, size), size)


def call(
    kernel, outs, operands, specs, scratch=(), flops=0, moved=0, limit=24, space=VMEM, aliases=None
):
    return pl.pallas_call(
        kernel,
        out_shape=outs,
        in_specs=specs,
        out_specs=[space] * len(outs),
        scratch_shapes=list(scratch),
        input_output_aliases=aliases or {},
        compiler_params=pltpu.CompilerParams(vmem_limit_bytes=limit * 2**20),
        cost_estimate=pl.CostEstimate(flops=flops, bytes_accessed=moved, transcendentals=0),
    )(*operands)


def run_all(copies):
    for copy in copies:
        copy.start()
    for copy in copies:
        copy.wait()


TILES = 4
UPPER = [(i, j) for i in range(TILES) for j in range(i, TILES)]


def pack(out, base, value):
    size = out.shape[1]
    across = value.shape[1] // size
    for band in range(value.shape[0] // size):
        for column in range(across):
            out[base + band * across + column] = value[
                band * size : (band + 1) * size, column * size : (column + 1) * size
            ].astype(HALF)


def diagonal(size):
    shape = (size, size)
    return lax.broadcasted_iota(jnp.int32, shape, 0) == lax.broadcasted_iota(jnp.int32, shape, 1)


def start_kernel(
    where,
    group,
    came,
    left,
    right,
    stat_left,
    stat_right,
    first,
    second,
    kept,
    sent,
    basis_in,
    stat_in,
    sem,
):
    position, core, x = where[0], where[1], where[2]
    half, width = basis_in.shape[1:]
    size = first.shape[1]
    mine = tile(core, half)
    last = pltpu.make_async_copy(right.at[mine], basis_in.at[1], sem.at[1])

    @pl.when(x == 0)
    def _():
        pltpu.make_async_copy(left.at[mine], basis_in.at[0], sem.at[0]).start()

    for side, stat in enumerate((stat_left, stat_right)):

        @pl.when((x == 1) & (core == side))
        def _():
            pltpu.make_async_copy(stat.at[:, tile(position, size * TILES)], stat_in, sem.at[0]).start()

    last.start()
    rows = kept.shape[0]
    for out, there in ((kept, x), (sent, 1 - x)):
        out[...] = (
            group[0, tile(core * 2 + there, rows)].astype(FULL)
            + came[tile(there, rows)].astype(FULL)
        ).astype(out.dtype)

    @pl.when(x == 0)
    def _():
        pltpu.make_async_copy(left.at[mine], basis_in.at[0], sem.at[0]).wait()
        pack(first, 0, basis_in.at[0])

    @pl.when(x == 1)
    def _():
        pltpu.make_async_copy(stat_left.at[:, : size * TILES], stat_in, sem.at[0]).wait()
        same = diagonal(size)
        for place, (i, j) in enumerate(UPPER):
            value = stat_in[i * size : (i + 1) * size, j * size : (j + 1) * size]
            high = value.astype(HALF)
            first[place] = high
            if i == j:
                low = jnp.where(same, value - high.astype(FULL), 0.0)
                line = jnp.sum(low, axis=0, keepdims=True)
                first[len(UPPER), i * 16 : (i + 1) * 16] = jnp.broadcast_to(
                    line, (16, size)
                ).astype(HALF)

    last.wait()
    pack(second, 0, basis_in.at[1])


def second_sum_kernel(where, kept, came, own, *sent):
    size = own.shape[0]
    z = where[3]
    for k, out in enumerate((own, *sent)):
        there = tile(z ^ k, size)
        out[...] = (kept[there] + came[there].astype(FULL)).astype(out.dtype)


def third_sum_kernel(own, one, two, three, out):
    out[...] = (
        (own[...] + one[...].astype(FULL)) + (two[...].astype(FULL) + three[...].astype(FULL))
    ).astype(HALF)


def joined_kernel(where, *refs):
    out = refs[-1]
    z = where[3]
    size = refs[0].shape[0]
    for k, part in enumerate(refs[:-1]):
        out[tile(z ^ k, size)] = part[...]


def place_basis(where, out, own, mine, theirs):
    rows, width = own.shape
    half = rows // 2
    position, core = where[0], where[1]
    out[tile(position, rows)] = own[...].astype(HALF)
    other = (1 - position) * 2
    for part, block in ((mine, other + core), (theirs, other + 1 - core)):
        size = part.shape[1]
        across = width // size
        for band in range(half // size):
            here = tile(block * (half // size) + band, size)
            for column in range(across):
                out[here, column * size : (column + 1) * size] = part[band * across + column]


def state_kernel(
    where,
    left,
    right,
    first,
    first_x,
    second,
    first_next,
    first_x_next,
    second_next,
    stat_left,
    stat_right,
    bases,
    turned,
    back,
    full,
    sem,
):
    rows, width = left.shape
    size = rows // TILES
    position, core, x = where[0], where[1], where[2]
    here, there = tile(position, rows), tile(1 - position, rows)
    for side, stat in enumerate((stat_left, stat_right)):

        @pl.when(core == side)
        def _():
            pltpu.make_async_copy(stat, full.at[here], sem).start()

    def place(basis_mine, basis_theirs, stats):
        place_basis(where, bases.at[core], left, basis_mine, basis_theirs)
        base = (1 - position) * TILES
        same = diagonal(size)
        for number, (i, j) in enumerate(UPPER):
            value = stats[number].astype(FULL)
            if i == j:
                line = stats[len(UPPER), i * 16 : (i + 1) * 16].astype(FULL)[:1]
                value = value + jnp.where(same, line, 0.0)
            full[tile(base + i, size), tile(base + j, size)] = value
            if i != j:
                full[tile(base + j, size), tile(base + i, size)] = value.T

    @pl.when(x == 0)
    def _():
        place(first, first_next, first_x)

    @pl.when(x == 1)
    def _():
        place(first_x, first_x_next, first)

    place_basis(where, bases.at[1 - core], right, second, second_next)
    turned[...] = bases[core].T
    back[...] = bases[1 - core].T
    pltpu.make_async_copy(stat_left, full.at[here], sem).wait()
    full[there, here] = full[here, there].T


def moment_kernel(where, moment, bases, *refs):
    parts, (gradient, ours, others, sem) = refs[:-4], refs[-4:]
    position, core, x = where[0], where[1], where[2]
    rows = moment.shape[0]
    step = rows // 2
    copies = []
    for place, part in enumerate(parts):
        size = part.shape[0]
        block = (
            (position ^ (place // 4)) * 4 + (core ^ (place // 2 % 2)) * 2 + (x ^ (place % 2))
        )
        copies.append(pltpu.make_async_copy(part, gradient.at[tile(block, size)], sem.at[place]))
    run_all(copies)
    half = (
        BETA_ONE * moment[...] + (1.0 - BETA_ONE) * gradient[tile(position, rows)].astype(FULL)
    ).astype(HALF)
    there, here = tile((1 - position) * 2 + core, step), tile(position * 2 + core, step)
    others[...] = matmul(half, bases[1 - core, :, there]).astype(HALF)
    ours[...] = matmul(half, bases[1 - core, :, here]).astype(HALF)


def adam_kernel(where, gradient, bases, turned, mine, came, second, new, kept, sent):
    width = gradient.shape[0]
    rows, step = mine.shape
    position, core = where[0], where[1]
    here, there = tile(position, rows), tile(1 - position, rows)
    block = matmul(gradient[...], bases[1 - core, :, tile(position * 2 + core, step)])
    grad_rot = matmul(turned[...], block.astype(HALF)) * (1.0 / width)
    moment_rot = (
        matmul(turned[:, here], mine[...]) + matmul(turned[:, there], came[...])
    ) * (1.0 / width)
    value = BETA_TWO * second[:, tile(core, step)] + (1.0 - BETA_TWO) * grad_rot * grad_rot
    new[...] = value
    scaled = (moment_rot / (jnp.sqrt(value) + EPSILON)).astype(HALF)
    sent[...] = matmul(bases[core, there], scaled).astype(HALF)
    kept[...] = matmul(bases[core, here], scaled).astype(HALF)


def side_copies(top, low, out, sem):
    half = top.shape[0]
    return [
        pltpu.make_async_copy(top, out.at[:half], sem.at[0]),
        pltpu.make_async_copy(low, out.at[half:], sem.at[1]),
    ]


def update_kernel(
    where,
    kept,
    came,
    kept_next,
    came_next,
    back,
    new,
    new_next,
    top,
    low,
    out,
    second_new,
    left,
    right,
    rows_back,
    sem,
    side_sem,
):
    rows, width = out.shape
    step = kept.shape[1]
    position, core = where[0], where[1]
    copies = [
        pltpu.make_async_copy(value, second_new.at[:, tile(place, step)], sem.at[i])
        for i, (value, place) in enumerate(((new, core), (new_next, 1 - core)))
    ]
    for copy in copies:
        copy.start()
    for side, target in enumerate((left, right)):

        @pl.when(core == side)
        def _():
            for copy in side_copies(top, low, target, side_sem):
                copy.start()

    for value, place in (
        (kept, position * 2 + core),
        (came, (1 - position) * 2 + core),
        (kept_next, position * 2 + 1 - core),
        (came_next, (1 - position) * 2 + 1 - core),
    ):
        rows_back[:, tile(place, step)] = value[...]
    for here in quarters(width):
        out[:, here] = (matmul(rows_back[...], back[:, here]) * (1.0 / width)).astype(HALF)
    for copy in copies + side_copies(top, low, left, side_sem):
        copy.wait()


def next_side_kernel(where, top, low, left_in, right_in, left, right, sem):
    for side, out in enumerate((right, left)):

        @pl.when(where[1] == side)
        def _():
            run_all(side_copies(top, low, out, sem))


def quarters(width):
    step = width // 4
    return [slice(i * step, (i + 1) * step) for i in range(4)]


def power_kernel(where, gradient, bases, stat, start, turned, pair, half):
    width = gradient.shape[0]
    core = where[1]
    for here in quarters(width):
        value = gradient[here]
        pair[core, here] = value
        pair[1 - core, :, here] = value.T
    for here in quarters(width):
        grads = matmul(pair[0], pair[1, :, here])
        half[:, here] = (BETA_STAT * stat[:, here] + (1.0 - BETA_STAT) * grads).astype(HALF)
    for here in quarters(width):
        product = matmul(half[...], bases[0, :, here])
        square = jnp.sum(product * product, axis=0, keepdims=True) * (1.0 / width)
        value = (product * lax.rsqrt(square + NORM_EPS)).astype(HALF)
        start[:, here] = value
        turned[here] = value.T


def improved(current, turned, kept, gram, result, result_turned):
    size, width = result.shape
    for here in quarters(width):
        gram[:size, here] = (matmul(current[kept], turned[:, here]) * (1.0 / width)).astype(HALF)
    for here in quarters(width):
        value = (
            1.5 * current[kept, here].astype(FULL) - 0.5 * matmul(gram[:size], current[:, here])
        ).astype(result.dtype)
        result[:, here] = value
        if result_turned is not None:
            result_turned[here] = value.T


def refresh_kernel(where, start, start_turned, current, turned, out, *scratch):
    width = start.shape[0]
    rows = width // 2
    gram, between = scratch[0], scratch[1:]
    source, source_turned = start, start_turned
    for iteration in range(NS_ITERS - 1):
        last = iteration + 2 == NS_ITERS
        if last:
            result, result_turned = current, turned
        else:
            result, result_turned = between[0].at[iteration % 2], between[1].at[iteration % 2]
        improved(source, source_turned, slice(0, width), gram, result, result_turned)
        source, source_turned = result, result_turned
    improved(current, turned, tile(where[0] * 2, rows // 2), gram, out, None)


def last_kernel(where, current, turned, out, gram):
    improved(current, turned, tile(where[0] * 2 + 1, out.shape[0]), gram, out, None)


def fast_body(group_grads, moment, second, stat_left, stat_right, basis_left, basis_right):
    position = lax.axis_index("shard")
    member = lax.axis_index("dp")
    rows, width = moment.shape
    half = rows // 2
    quarter = rows // 4
    chunk = rows // 16
    core, x, z = member & 1, (member >> 1) & 1, member >> 2
    where = jnp.stack([position, core, x, z]).astype(jnp.int32)
    unit = 2 * width**3

    def dp_swap(value, distance):
        return lax.ppermute(value, "dp", [(i, i ^ distance) for i in range(16)])

    def shard_swap(value):
        return lax.ppermute(value, "shard", [(0, 1), (1, 0)])

    def cross_swap(value):
        pairs = [(i, i ^ 5) for i in range(32)]
        return lax.ppermute(value, ("dp", "shard"), pairs)

    raw = lax.dynamic_slice_in_dim(group_grads[0], (1 - core) * half, half, 0)
    came = dp_swap(raw, 1)
    count = half * width // quarter**2
    first_sent, second_sent, kept, sent = call(
        start_kernel,
        [shaped((count, quarter, quarter), HALF)] * 2
        + [shaped((quarter, width), FULL), shaped((quarter, width), HALF)],
        (where, group_grads, came, basis_left, basis_right, stat_left, stat_right),
        [SMEM] + [VMEM] * 2 + [ANY] * 4,
        [
            pltpu.VMEM((2, half, width), FULL),
            pltpu.VMEM((rows, rows), FULL),
            pltpu.SemaphoreType.DMA((2,)),
        ],
        moved=2**22,
        limit=50,
    )
    came = dp_swap(sent, 2)
    first = shard_swap(first_sent)
    second_half = shard_swap(second_sent)
    own, *sent = call(
        second_sum_kernel,
        [shaped((chunk, width), FULL)] + [shaped((chunk, width), HALF)] * 3,
        (where, kept, came),
        [SMEM] + [VMEM] * 2,
        moved=2**20,
    )
    pieces = [dp_swap(value, 4 * (k + 1)) for k, value in enumerate(sent)]
    pieces[0], first = lax.optimization_barrier((pieces[0], first))
    first_x = dp_swap(first, 2)
    (piece,) = call(
        third_sum_kernel,
        [shaped((chunk, width), HALF)],
        (own, *pieces),
        [VMEM] * 4,
        moved=2**19,
    )
    pieces = [piece] + [dp_swap(piece, 4 * k) for k in (1, 2, 3)]
    (part,) = call(
        joined_kernel,
        [shaped((quarter, width), HALF)],
        (where, *pieces),
        [SMEM] + [VMEM] * 4,
        moved=2**19,
    )
    part, first, first_x, second_half = lax.optimization_barrier(
        (part, first, first_x, second_half)
    )
    parts = [part, dp_swap(part, 2), shard_swap(part), cross_swap(part)]
    state = [first, first_x, second_half]
    state += [dp_swap(value, 1) for value in state]
    square = shaped((width, width), HALF)
    bases, left_turned, right_turned, stat = call(
        state_kernel,
        [shaped((2, width, width), HALF), square, square, shaped((width, width), FULL)],
        (
            where,
            basis_left,
            basis_right,
            *state,
            stat_left,
            stat_right,
        ),
        [SMEM] + [VMEM] * 8 + [ANY] * 2,
        [pltpu.SemaphoreType.DMA(())],
        moved=2**24,
    )
    parts[2], parts[3], bases = lax.optimization_barrier((parts[2], parts[3], bases))
    swapped = [dp_swap(value, 1) for value in parts]
    ordered = parts[:2] + swapped[:2] + parts[2:] + swapped[2:]
    gradient, moment_mine, moment_sent = call(
        moment_kernel,
        [square] + [shaped((rows, half), HALF)] * 2,
        (where, moment, bases, *ordered),
        [SMEM, VMEM, VMEM] + [ANY] * 8,
        [pltpu.SemaphoreType.DMA((8,))],
        flops=unit // 4,
        moved=2**22,
    )
    moment_came = shard_swap(moment_sent)
    start, start_turned = call(
        power_kernel,
        [square] * 2,
        (where, gradient, bases, stat),
        [SMEM] + [VMEM] * 3,
        [pltpu.VMEM((2, width, width), HALF), pltpu.VMEM((width, width), HALF)],
        flops=2 * unit,
        moved=2**23,
    )
    new, back_kept, back_sent = call(
        adam_kernel,
        [shaped((width, half), FULL)] + [shaped((rows, half), HALF)] * 2,
        (where, gradient, bases, left_turned, moment_mine, moment_came, second),
        [SMEM] + [VMEM] * 6,
        flops=unit,
        moved=2**22,
    )
    start, back_sent = lax.optimization_barrier((start, back_sent))
    back_came = shard_swap(back_sent)
    new_next = dp_swap(new, 1)
    back_kept_next = dp_swap(back_kept, 1)
    current, current_turned, top = call(
        refresh_kernel,
        [square] * 2 + [shaped((half, width), FULL)],
        (where, start, start_turned),
        [SMEM] + [VMEM] * 2,
        [pltpu.VMEM((width, width), HALF)]
        + [pltpu.VMEM((2, width, width), HALF)] * (2 if NS_ITERS > 2 else 0),
        flops=5 * unit // 2,
        moved=2**22,
    )
    top_next = dp_swap(top, 1)
    current, back_came = lax.optimization_barrier((current, back_came))
    (low,) = call(
        last_kernel,
        [shaped((half, width), FULL)],
        (where, current, current_turned),
        [SMEM] + [VMEM] * 2,
        [pltpu.VMEM((half, width), HALF)],
        flops=unit // 2,
        moved=2**21,
    )
    low_next = dp_swap(low, 1)
    back_came_next = dp_swap(back_came, 1)
    side = shaped((rows, width), FULL)
    update, second_new, left_new, right_new = pl.pallas_call(
        update_kernel,
        out_shape=[shaped((rows, width), HALF), shaped((width, rows), FULL), side, side],
        in_specs=[SMEM] + [VMEM] * 5 + [ANY] * 4,
        out_specs=[VMEM] + [ANY] * 3,
        scratch_shapes=[
            pltpu.VMEM((rows, width), HALF),
            pltpu.SemaphoreType.DMA((2,)),
            pltpu.SemaphoreType.DMA((2,)),
        ],
        compiler_params=pltpu.CompilerParams(vmem_limit_bytes=24 * 2**20),
        cost_estimate=pl.CostEstimate(
            flops=unit // 2, bytes_accessed=2**23, transcendentals=0
        ),
    )(
        where,
        back_kept,
        back_came,
        back_kept_next,
        back_came_next,
        right_turned,
        new,
        new_next,
        top,
        low,
    )
    left_new, right_new = call(
        next_side_kernel,
        [side, side],
        (where, top_next, low_next, left_new, right_new),
        [SMEM] + [ANY] * 4,
        [pltpu.SemaphoreType.DMA((2,))],
        moved=2**22,
        space=ANY,
        aliases={3: 0, 4: 1},
    )
    return (update, second_new, left_new, right_new)


def make_plain_body(n_dp, n_shard):
    def swap(value, axis, distance):
        size = n_dp if axis == "dp" else n_shard
        return lax.ppermute(value, axis, [(i, i ^ distance) for i in range(size)])

    dp_bits = []
    bit = 1
    while bit < n_dp:
        dp_bits.append(bit)
        bit *= 2

    def ordered(first_is_low, own, other, dim):
        return jnp.where(
            first_is_low,
            jnp.concatenate([own, other], dim),
            jnp.concatenate([other, own], dim),
        )

    def body(group_grads, moment, second, stat_left, stat_right, basis_left, basis_right):
        position = lax.axis_index("shard")
        member = lax.axis_index("dp")
        rows, width = moment.shape
        core = member & 1
        half = rows // 2

        def near_columns(value):
            blocks = [
                lax.dynamic_slice_in_dim(value, (position ^ k) * rows, rows, 1)
                for k in range(n_shard)
            ]
            return jnp.concatenate(blocks, 1)

        def fetch(value, distance):
            size = value.shape[0] // 2
            part = lax.dynamic_slice_in_dim(value, core * size, size, 0)
            part = swap(part, "shard", distance)
            other = swap(part, "dp", 1)
            return ordered(core == 0, part, other, 0)

        left_own = basis_left.astype(jnp.bfloat16)
        right_own = basis_right.astype(jnp.bfloat16)
        left_rot = jnp.concatenate([left_own] + [fetch(left_own, k) for k in range(1, n_shard)], 0)
        right_rot = jnp.concatenate(
            [right_own] + [fetch(right_own, k) for k in range(1, n_shard)], 0
        )

        def whole_stat(stat):
            own = near_columns(stat)
            blocks = [own[:, b * rows : (b + 1) * rows] for b in range(n_shard)]
            bands = [own]
            for k in range(1, n_shard):
                others = [b for b in range(n_shard) if b != k]
                sent = jnp.concatenate([blocks[b] for b in others], 1).astype(jnp.bfloat16)
                came = fetch(sent, k).astype(jnp.float32)
                band = [None] * n_shard
                band[0] = blocks[k].T
                for place, b in enumerate(others):
                    band[k ^ b] = came[:, place * rows : (place + 1) * rows]
                bands.append(jnp.concatenate(band, 1))
            return jnp.concatenate(bands, 0)

        stat_left_full = whole_stat(stat_left)
        stat_right_full = whole_stat(stat_right)

        part = group_grads[0]
        for bit in dp_bits:
            size = part.shape[0] // 2
            high = (member & bit) // bit
            kept = lax.dynamic_slice_in_dim(part, high * size, size, 0)
            sent = lax.dynamic_slice_in_dim(part, (1 - high) * size, size, 0)
            part = kept.astype(jnp.float32) + swap(sent, "dp", bit).astype(jnp.float32)
        chunk = part.astype(jnp.bfloat16)[None]
        chunk = jnp.concatenate([chunk] + [swap(chunk, "shard", k) for k in range(1, n_shard)], 0)
        for bit in reversed(dp_bits):
            chunk = ordered((member & bit) == 0, chunk, swap(chunk, "dp", bit), 1)
        gradient = near_columns(chunk.reshape(width, width))

        grad_rows = gradient[:rows].astype(jnp.float32)
        moment_half = (
            BETA_ONE * near_columns(moment) + (1.0 - BETA_ONE) * grad_rows
        ).astype(jnp.bfloat16)
        near_rot = near_columns(right_rot)
        moment_turned = matmul(moment_half, near_rot).astype(jnp.bfloat16)
        moment_block = jnp.concatenate(
            [moment_turned[:, :rows]]
            + [
                swap(moment_turned[:, k * rows : (k + 1) * rows], "shard", k)
                for k in range(1, n_shard)
            ],
            0,
        )
        grad_block = matmul(gradient, near_rot[:, :rows]).astype(jnp.bfloat16)
        grad_rot = matmul(left_rot, grad_block, 0) / width
        moment_rot = matmul(left_rot, moment_block, 0) / width
        second_new = BETA_TWO * second + (1.0 - BETA_TWO) * grad_rot * grad_rot
        scaled = (moment_rot / (jnp.sqrt(second_new) + EPSILON)).astype(jnp.bfloat16)
        turned_back = matmul(left_rot, scaled).astype(jnp.bfloat16)
        back_rows = jnp.concatenate(
            [turned_back[:rows]]
            + [
                swap(turned_back[k * rows : (k + 1) * rows], "shard", k)
                for k in range(1, n_shard)
            ],
            1,
        )
        update = (near_columns(matmul(back_rows, near_rot, 1, 1)) / width).astype(jnp.bfloat16)

        def refreshed(stat, product_of_grads, rot):
            stat_new = BETA_STAT * stat + (1.0 - BETA_STAT) * product_of_grads
            product = matmul(stat_new.astype(jnp.bfloat16), rot)
            start = product / jnp.sqrt(jnp.sum(product * product, axis=0) / width + NORM_EPS)
            current = start.astype(jnp.bfloat16)
            for iteration in range(NS_ITERS):
                kept = width if iteration + 1 < NS_ITERS else rows
                gram = (matmul(current[:kept], current, 1, 1) / width).astype(jnp.bfloat16)
                result = 1.5 * current[:kept].astype(jnp.float32) - 0.5 * matmul(gram, current)
                current = result.astype(jnp.bfloat16)
            return result

        left_new = refreshed(stat_left_full, matmul(gradient, gradient, 1, 1), left_rot)
        right_new = refreshed(stat_right_full, matmul(gradient, gradient, 0, 0), right_rot)
        return (update, second_new, left_new, right_new)

    return body


def solution(mesh):
    n_dp, n_shard = mesh.shape["dp"], mesh.shape["shard"]
    body = fast_body if (n_dp, n_shard) == (16, 2) else make_plain_body(n_dp, n_shard)
    return jax.shard_map(
        body,
        mesh=mesh,
        in_specs=(
            P("dp", "shard", None),
            P("shard", None),
            P(None, "shard"),
            P("shard", None),
            P("shard", None),
            P("shard", None),
            P("shard", None),
        ),
        out_specs=(P("shard", None), P(None, "shard"), P("shard", None), P("shard", None)),
        check_vma=False,
    )
```

```python
import jax
import jax.numpy as jnp
from jax import lax
from jax.experimental import pallas as pl
from jax.experimental.pallas import tpu as pltpu
from jax.sharding import PartitionSpec as P

NS_ITERS = 2


BETA_ONE = 0.9
BETA_TWO = 0.9
BETA_STAT = 0.95
EPSILON = 1e-08
NORM_EPS = 1e-06
HALF = jnp.bfloat16
FULL = jnp.float32
VMEM = pl.BlockSpec(memory_space=pltpu.VMEM)
ANY = pl.BlockSpec(memory_space=pl.ANY)
SMEM = pl.BlockSpec(memory_space=pltpu.SMEM)


def matmul(left_mat, right_mat, left_dim=1, right_dim=0):
    return lax.dot_general(
        left_mat,
        right_mat,
        (((left_dim,), (right_dim,)), ((), ())),
        preferred_element_type=FULL,
    )


def shaped(shape, dtype):
    return jax.ShapeDtypeStruct(shape, dtype)


def tile(index, size):
    return pl.ds(pl.multiple_of(index * size, size), size)


def call(
    kernel, outs, operands, specs, scratch=(), flops=0, moved=0, limit=24, space=VMEM, aliases=None
):
    return pl.pallas_call(
        kernel,
        out_shape=outs,
        in_specs=specs,
        out_specs=[space] * len(outs),
        scratch_shapes=list(scratch),
        input_output_aliases=aliases or {},
        compiler_params=pltpu.CompilerParams(vmem_limit_bytes=limit * 2**20),
        cost_estimate=pl.CostEstimate(flops=flops, bytes_accessed=moved, transcendentals=0),
    )(*operands)


def run_all(copies):
    for copy in copies:
        copy.start()
    for copy in copies:
        copy.wait()


TILES = 4
UPPER = [(i, j) for i in range(TILES) for j in range(i, TILES)]


def pack(out, base, value):
    size = out.shape[1]
    across = value.shape[1] // size
    for band in range(value.shape[0] // size):
        for column in range(across):
            out[base + band * across + column] = value[
                band * size : (band + 1) * size, column * size : (column + 1) * size
            ].astype(HALF)


def diagonal(size):
    shape = (size, size)
    return lax.broadcasted_iota(jnp.int32, shape, 0) == lax.broadcasted_iota(jnp.int32, shape, 1)


def start_kernel(
    where,
    raw,
    came,
    left,
    right,
    stat_left,
    stat_right,
    state,
    kept,
    sent,
    basis_in,
    stat_in,
    sem,
):
    position, core, x = where[0], where[1], where[2]
    half, width = basis_in.shape[1:]
    size = state.shape[1]
    copies = [
        pltpu.make_async_copy(basis.at[tile(core, half)], basis_in.at[i], sem.at[i])
        for i, basis in enumerate((left, right))
    ]
    for copy in copies:
        copy.start()
    for side, stat in enumerate((stat_left, stat_right)):

        @pl.when(core == side)
        def _():
            pltpu.make_async_copy(stat.at[:, tile(position, size * TILES)], stat_in, sem.at[2]).start()

    rows = kept.shape[0]
    for out, there in ((kept, tile(x, rows)), (sent, tile(1 - x, rows))):
        out[...] = (raw[there].astype(FULL) + came[there].astype(FULL)).astype(out.dtype)
    count = half * width // size**2
    for i, copy in enumerate(copies):
        copy.wait()
        pack(state, i * count, basis_in.at[i])
    pltpu.make_async_copy(stat_left.at[:, : size * TILES], stat_in, sem.at[2]).wait()
    same = diagonal(size)
    base = 2 * count
    for place, (i, j) in enumerate(UPPER):
        value = stat_in[i * size : (i + 1) * size, j * size : (j + 1) * size]
        high = value.astype(HALF)
        state[base + place] = high
        if i == j:
            low = jnp.where(same, value - high.astype(FULL), 0.0)
            line = jnp.sum(low, axis=0, keepdims=True)
            state[base + len(UPPER), i * 16 : (i + 1) * 16] = jnp.broadcast_to(
                line, (16, size)
            ).astype(HALF)


def second_sum_kernel(where, kept, came, own, *sent):
    size = own.shape[0]
    z = where[3]
    for k, out in enumerate((own, *sent)):
        there = tile(z ^ k, size)
        out[...] = (kept[there] + came[there].astype(FULL)).astype(out.dtype)


def third_sum_kernel(own, one, two, three, out):
    out[...] = (
        (own[...] + one[...].astype(FULL)) + (two[...].astype(FULL) + three[...].astype(FULL))
    ).astype(HALF)


def joined_kernel(where, *refs):
    out = refs[-1]
    z = where[3]
    size = refs[0].shape[0]
    for k, part in enumerate(refs[:-1]):
        out[tile(z ^ k, size)] = part[...]


def place_basis(where, out, own, mine, theirs, side):
    rows, width = own.shape
    half = rows // 2
    size = mine.shape[1]
    position, core = where[0], where[1]
    across = width // size
    base = side * half * width // size**2
    out[tile(position, rows)] = own[...].astype(HALF)
    other = (1 - position) * 2
    for part, block in ((mine, other + core), (theirs, other + 1 - core)):
        for band in range(half // size):
            here = tile(block * (half // size) + band, size)
            for column in range(across):
                out[here, column * size : (column + 1) * size] = part[base + band * across + column]


def state_kernel(
    where, left, right, mine, theirs, stat_left, stat_right, bases, turned, back, full, sem
):
    rows, width = left.shape
    size = rows // TILES
    position, core = where[0], where[1]
    here, there = tile(position, rows), tile(1 - position, rows)
    for side, stat in enumerate((stat_left, stat_right)):

        @pl.when(core == side)
        def _():
            pltpu.make_async_copy(stat, full.at[here], sem).start()

    place_basis(where, bases.at[core], left, mine, theirs, 0)
    place_basis(where, bases.at[1 - core], right, mine, theirs, 1)
    turned[...] = bases[core].T
    back[...] = bases[1 - core].T
    base = (1 - position) * TILES
    first = rows * width // size**2
    same = diagonal(size)
    for number, (i, j) in enumerate(UPPER):
        value = mine[first + number].astype(FULL)
        if i == j:
            line = mine[first + len(UPPER), i * 16 : (i + 1) * 16].astype(FULL)[:1]
            value = value + jnp.where(same, line, 0.0)
        full[tile(base + i, size), tile(base + j, size)] = value
        if i != j:
            full[tile(base + j, size), tile(base + i, size)] = value.T
    pltpu.make_async_copy(stat_left, full.at[here], sem).wait()
    full[there, here] = full[here, there].T


def moment_kernel(where, moment, bases, *refs):
    parts, (gradient, ours, others, sem) = refs[:-4], refs[-4:]
    position, core, x = where[0], where[1], where[2]
    rows = moment.shape[0]
    step = rows // 2
    copies = []
    for place, part in enumerate(parts):
        size = part.shape[0]
        block = (
            (position ^ (place // 4)) * 4 + (core ^ (place // 2 % 2)) * 2 + (x ^ (place % 2))
        )
        copies.append(pltpu.make_async_copy(part, gradient.at[tile(block, size)], sem.at[place]))
    run_all(copies)
    half = (
        BETA_ONE * moment[...] + (1.0 - BETA_ONE) * gradient[tile(position, rows)].astype(FULL)
    ).astype(HALF)
    there, here = tile((1 - position) * 2 + core, step), tile(position * 2 + core, step)
    others[...] = matmul(half, bases[1 - core, :, there]).astype(HALF)
    ours[...] = matmul(half, bases[1 - core, :, here]).astype(HALF)


def adam_kernel(where, gradient, bases, turned, mine, came, second, new, kept, sent):
    width = gradient.shape[0]
    rows, step = mine.shape
    position, core = where[0], where[1]
    here, there = tile(position, rows), tile(1 - position, rows)
    block = matmul(gradient[...], bases[1 - core, :, tile(position * 2 + core, step)])
    grad_rot = matmul(turned[...], block.astype(HALF)) * (1.0 / width)
    moment_rot = (
        matmul(turned[:, here], mine[...]) + matmul(turned[:, there], came[...])
    ) * (1.0 / width)
    value = BETA_TWO * second[:, tile(core, step)] + (1.0 - BETA_TWO) * grad_rot * grad_rot
    new[...] = value
    scaled = (moment_rot / (jnp.sqrt(value) + EPSILON)).astype(HALF)
    sent[...] = matmul(bases[core, there], scaled).astype(HALF)
    kept[...] = matmul(bases[core, here], scaled).astype(HALF)


def write_part(core, side, block, part, left, right, sem):
    size = part.shape[0]
    here = slice(block * size, (block + 1) * size)
    for place, out in enumerate((left, right)):

        @pl.when((core ^ side) == place)
        def _():
            pltpu.make_async_copy(part, out.at[here], sem).start()

    return pltpu.make_async_copy(part, left.at[here], sem)


def update_kernel(
    where,
    kept,
    came,
    kept_next,
    came_next,
    back,
    low,
    top_next,
    left_in,
    right_in,
    out,
    left,
    right,
    rows_back,
    sem,
):
    rows, width = out.shape
    step = kept.shape[1]
    position, core = where[0], where[1]
    copies = [
        write_part(core, 0, 1, low, left, right, sem.at[0]),
        write_part(core, 1, 0, top_next, left, right, sem.at[1]),
    ]
    for value, place in (
        (kept, position * 2 + core),
        (came, (1 - position) * 2 + core),
        (kept_next, position * 2 + 1 - core),
        (came_next, (1 - position) * 2 + 1 - core),
    ):
        rows_back[:, tile(place, step)] = value[...]
    for here in quarters(width):
        out[:, here] = (matmul(rows_back[...], back[:, here]) * (1.0 / width)).astype(HALF)
    for copy in copies:
        copy.wait()


def next_side_kernel(where, low, left_in, right_in, left, right, sem):
    write_part(where[1], 1, 1, low, left, right, sem.at[0]).wait()


def quarters(width):
    step = width // 4
    return [slice(i * step, (i + 1) * step) for i in range(4)]


def power_kernel(where, gradient, bases, stat, start, turned, pair, half):
    width = gradient.shape[0]
    core = where[1]
    for here in quarters(width):
        value = gradient[here]
        pair[core, here] = value
        pair[1 - core, :, here] = value.T
    for here in quarters(width):
        grads = matmul(pair[0], pair[1, :, here])
        half[:, here] = (BETA_STAT * stat[:, here] + (1.0 - BETA_STAT) * grads).astype(HALF)
    for here in quarters(width):
        product = matmul(half[...], bases[0, :, here])
        square = jnp.sum(product * product, axis=0, keepdims=True) * (1.0 / width)
        value = (product * lax.rsqrt(square + NORM_EPS)).astype(HALF)
        start[:, here] = value
        turned[here] = value.T


def improved(current, turned, kept, gram, result, result_turned):
    size, width = result.shape
    for here in quarters(width):
        gram[:size, here] = (matmul(current[kept], turned[:, here]) * (1.0 / width)).astype(HALF)
    for here in quarters(width):
        value = (
            1.5 * current[kept, here].astype(FULL) - 0.5 * matmul(gram[:size], current[:, here])
        ).astype(result.dtype)
        result[:, here] = value
        if result_turned is not None:
            result_turned[here] = value.T


def refresh_kernel(where, start, start_turned, current, turned, out, *scratch):
    width = start.shape[0]
    rows = width // 2
    gram, between = scratch[0], scratch[1:]
    source, source_turned = start, start_turned
    for iteration in range(NS_ITERS - 1):
        last = iteration + 2 == NS_ITERS
        if last:
            result, result_turned = current, turned
        else:
            result, result_turned = between[0].at[iteration % 2], between[1].at[iteration % 2]
        improved(source, source_turned, slice(0, width), gram, result, result_turned)
        source, source_turned = result, result_turned
    improved(current, turned, tile(where[0] * 2, rows // 2), gram, out, None)


def last_kernel(
    where, current, turned, top, new, new_next, out, left, right, second_new, gram, sem
):
    core = where[1]
    step = new.shape[1]
    copies = [write_part(core, 0, 0, top, left, right, sem.at[0])]
    for i, (value, place) in enumerate(((new, core), (new_next, 1 - core))):
        copy = pltpu.make_async_copy(value, second_new.at[:, tile(place, step)], sem.at[i + 1])
        copy.start()
        copies.append(copy)
    improved(current, turned, tile(where[0] * 2 + 1, out.shape[0]), gram, out, None)
    for copy in copies:
        copy.wait()


def fast_body(group_grads, moment, second, stat_left, stat_right, basis_left, basis_right):
    position = lax.axis_index("shard")
    member = lax.axis_index("dp")
    rows, width = moment.shape
    half = rows // 2
    quarter = rows // 4
    chunk = rows // 16
    core, x, z = member & 1, (member >> 1) & 1, member >> 2
    where = jnp.stack([position, core, x, z]).astype(jnp.int32)
    unit = 2 * width**3

    def dp_swap(value, distance):
        return lax.ppermute(value, "dp", [(i, i ^ distance) for i in range(16)])

    def shard_swap(value):
        return lax.ppermute(value, "shard", [(0, 1), (1, 0)])

    def cross_swap(value):
        pairs = [(i, i ^ 5) for i in range(32)]
        return lax.ppermute(value, ("dp", "shard"), pairs)

    raw = lax.dynamic_slice_in_dim(group_grads[0], (1 - core) * half, half, 0)
    came = dp_swap(raw, 1)
    raw = lax.dynamic_slice_in_dim(group_grads[0], core * half, half, 0)
    count = rows * width // quarter**2 + len(UPPER) + 1
    state_sent, kept, sent = call(
        start_kernel,
        [
            shaped((count, quarter, quarter), HALF),
            shaped((quarter, width), FULL),
            shaped((quarter, width), HALF),
        ],
        (where, raw, came, basis_left, basis_right, stat_left, stat_right),
        [SMEM] + [VMEM] * 2 + [ANY] * 4,
        [
            pltpu.VMEM((2, half, width), FULL),
            pltpu.VMEM((rows, rows), FULL),
            pltpu.SemaphoreType.DMA((3,)),
        ],
        moved=2**22,
        limit=50,
    )
    came = dp_swap(sent, 2)
    state_mine = shard_swap(state_sent)
    own, *sent = call(
        second_sum_kernel,
        [shaped((chunk, width), FULL)] + [shaped((chunk, width), HALF)] * 3,
        (where, kept, came),
        [SMEM] + [VMEM] * 2,
        moved=2**20,
    )
    pieces = [dp_swap(value, 4 * (k + 1)) for k, value in enumerate(sent)]
    (piece,) = call(
        third_sum_kernel,
        [shaped((chunk, width), HALF)],
        (own, *pieces),
        [VMEM] * 4,
        moved=2**19,
    )
    pieces = [piece] + [dp_swap(piece, 4 * k) for k in (1, 2, 3)]
    (part,) = call(
        joined_kernel,
        [shaped((quarter, width), HALF)],
        (where, *pieces),
        [SMEM] + [VMEM] * 4,
        moved=2**19,
    )
    part, state_mine = lax.optimization_barrier((part, state_mine))
    parts = [part, dp_swap(part, 2), shard_swap(part), cross_swap(part)]
    state_theirs = dp_swap(state_mine, 1)
    square = shaped((width, width), HALF)
    bases, left_turned, right_turned, stat = call(
        state_kernel,
        [shaped((2, width, width), HALF), square, square, shaped((width, width), FULL)],
        (
            where,
            basis_left,
            basis_right,
            state_mine,
            state_theirs,
            stat_left,
            stat_right,
        ),
        [SMEM] + [VMEM] * 4 + [ANY] * 2,
        [pltpu.SemaphoreType.DMA(())],
        moved=2**24,
    )
    parts[2], parts[3], bases = lax.optimization_barrier((parts[2], parts[3], bases))
    swapped = [dp_swap(value, 1) for value in parts]
    ordered = parts[:2] + swapped[:2] + parts[2:] + swapped[2:]
    gradient, moment_mine, moment_sent = call(
        moment_kernel,
        [square] + [shaped((rows, half), HALF)] * 2,
        (where, moment, bases, *ordered),
        [SMEM, VMEM, VMEM] + [ANY] * 8,
        [pltpu.SemaphoreType.DMA((8,))],
        flops=unit // 4,
        moved=2**22,
    )
    moment_came = shard_swap(moment_sent)
    start, start_turned = call(
        power_kernel,
        [square] * 2,
        (where, gradient, bases, stat),
        [SMEM] + [VMEM] * 3,
        [pltpu.VMEM((2, width, width), HALF), pltpu.VMEM((width, width), HALF)],
        flops=2 * unit,
        moved=2**23,
    )
    start, moment_came = lax.optimization_barrier((start, moment_came))
    new, back_kept, back_sent = call(
        adam_kernel,
        [shaped((width, half), FULL)] + [shaped((rows, half), HALF)] * 2,
        (where, gradient, bases, left_turned, moment_mine, moment_came, second),
        [SMEM] + [VMEM] * 6,
        flops=unit,
        moved=2**22,
    )
    start, back_sent = lax.optimization_barrier((start, back_sent))
    back_came = shard_swap(back_sent)
    new_next = dp_swap(new, 1)
    back_kept_next = dp_swap(back_kept, 1)
    current, current_turned, top = call(
        refresh_kernel,
        [square] * 2 + [shaped((half, width), FULL)],
        (where, start, start_turned),
        [SMEM] + [VMEM] * 2,
        [pltpu.VMEM((width, width), HALF)]
        + [pltpu.VMEM((2, width, width), HALF)] * (2 if NS_ITERS > 2 else 0),
        flops=5 * unit // 2,
        moved=2**22,
    )
    top_next = dp_swap(top, 1)
    current, back_came, back_kept_next, new_next = lax.optimization_barrier(
        (current, back_came, back_kept_next, new_next)
    )
    back_came_next = dp_swap(back_came, 1)
    side = shaped((rows, width), FULL)
    low, left_new, right_new, second_new = pl.pallas_call(
        last_kernel,
        out_shape=[shaped((half, width), FULL), side, side, shaped((width, rows), FULL)],
        in_specs=[SMEM] + [VMEM] * 2 + [ANY] * 3,
        out_specs=[VMEM] + [ANY] * 3,
        scratch_shapes=[pltpu.VMEM((half, width), HALF), pltpu.SemaphoreType.DMA((3,))],
        compiler_params=pltpu.CompilerParams(vmem_limit_bytes=24 * 2**20),
        cost_estimate=pl.CostEstimate(flops=unit // 2, bytes_accessed=2**22, transcendentals=0),
    )(where, current, current_turned, top, new, new_next)
    low, back_came_next = lax.optimization_barrier((low, back_came_next))
    low_next = dp_swap(low, 1)
    update, left_new, right_new = pl.pallas_call(
        update_kernel,
        out_shape=[shaped((rows, width), HALF), side, side],
        in_specs=[SMEM] + [VMEM] * 5 + [ANY] * 4,
        out_specs=[VMEM] + [ANY] * 2,
        scratch_shapes=[pltpu.VMEM((rows, width), HALF), pltpu.SemaphoreType.DMA((2,))],
        input_output_aliases={8: 1, 9: 2},
        compiler_params=pltpu.CompilerParams(vmem_limit_bytes=24 * 2**20),
        cost_estimate=pl.CostEstimate(flops=unit // 2, bytes_accessed=2**22, transcendentals=0),
    )(
        where,
        back_kept,
        back_came,
        back_kept_next,
        back_came_next,
        right_turned,
        low,
        top_next,
        left_new,
        right_new,
    )
    left_new, right_new = call(
        next_side_kernel,
        [side, side],
        (where, low_next, left_new, right_new),
        [SMEM] + [ANY] * 3,
        [pltpu.SemaphoreType.DMA((1,))],
        moved=2**21,
        space=ANY,
        aliases={2: 0, 3: 1},
    )
    return (update, second_new, left_new, right_new)


def make_plain_body(n_dp, n_shard):
    def swap(value, axis, distance):
        size = n_dp if axis == "dp" else n_shard
        return lax.ppermute(value, axis, [(i, i ^ distance) for i in range(size)])

    dp_bits = []
    bit = 1
    while bit < n_dp:
        dp_bits.append(bit)
        bit *= 2

    def ordered(first_is_low, own, other, dim):
        return jnp.where(
            first_is_low,
            jnp.concatenate([own, other], dim),
            jnp.concatenate([other, own], dim),
        )

    def body(group_grads, moment, second, stat_left, stat_right, basis_left, basis_right):
        position = lax.axis_index("shard")
        member = lax.axis_index("dp")
        rows, width = moment.shape
        core = member & 1
        half = rows // 2

        def near_columns(value):
            blocks = [
                lax.dynamic_slice_in_dim(value, (position ^ k) * rows, rows, 1)
                for k in range(n_shard)
            ]
            return jnp.concatenate(blocks, 1)

        def fetch(value, distance):
            size = value.shape[0] // 2
            part = lax.dynamic_slice_in_dim(value, core * size, size, 0)
            part = swap(part, "shard", distance)
            other = swap(part, "dp", 1)
            return ordered(core == 0, part, other, 0)

        left_own = basis_left.astype(jnp.bfloat16)
        right_own = basis_right.astype(jnp.bfloat16)
        left_rot = jnp.concatenate([left_own] + [fetch(left_own, k) for k in range(1, n_shard)], 0)
        right_rot = jnp.concatenate(
            [right_own] + [fetch(right_own, k) for k in range(1, n_shard)], 0
        )

        def whole_stat(stat):
            own = near_columns(stat)
            blocks = [own[:, b * rows : (b + 1) * rows] for b in range(n_shard)]
            bands = [own]
            for k in range(1, n_shard):
                others = [b for b in range(n_shard) if b != k]
                sent = jnp.concatenate([blocks[b] for b in others], 1).astype(jnp.bfloat16)
                came = fetch(sent, k).astype(jnp.float32)
                band = [None] * n_shard
                band[0] = blocks[k].T
                for place, b in enumerate(others):
                    band[k ^ b] = came[:, place * rows : (place + 1) * rows]
                bands.append(jnp.concatenate(band, 1))
            return jnp.concatenate(bands, 0)

        stat_left_full = whole_stat(stat_left)
        stat_right_full = whole_stat(stat_right)

        part = group_grads[0]
        for bit in dp_bits:
            size = part.shape[0] // 2
            high = (member & bit) // bit
            kept = lax.dynamic_slice_in_dim(part, high * size, size, 0)
            sent = lax.dynamic_slice_in_dim(part, (1 - high) * size, size, 0)
            part = kept.astype(jnp.float32) + swap(sent, "dp", bit).astype(jnp.float32)
        chunk = part.astype(jnp.bfloat16)[None]
        chunk = jnp.concatenate([chunk] + [swap(chunk, "shard", k) for k in range(1, n_shard)], 0)
        for bit in reversed(dp_bits):
            chunk = ordered((member & bit) == 0, chunk, swap(chunk, "dp", bit), 1)
        gradient = near_columns(chunk.reshape(width, width))

        grad_rows = gradient[:rows].astype(jnp.float32)
        moment_half = (
            BETA_ONE * near_columns(moment) + (1.0 - BETA_ONE) * grad_rows
        ).astype(jnp.bfloat16)
        near_rot = near_columns(right_rot)
        moment_turned = matmul(moment_half, near_rot).astype(jnp.bfloat16)
        moment_block = jnp.concatenate(
            [moment_turned[:, :rows]]
            + [
                swap(moment_turned[:, k * rows : (k + 1) * rows], "shard", k)
                for k in range(1, n_shard)
            ],
            0,
        )
        grad_block = matmul(gradient, near_rot[:, :rows]).astype(jnp.bfloat16)
        grad_rot = matmul(left_rot, grad_block, 0) / width
        moment_rot = matmul(left_rot, moment_block, 0) / width
        second_new = BETA_TWO * second + (1.0 - BETA_TWO) * grad_rot * grad_rot
        scaled = (moment_rot / (jnp.sqrt(second_new) + EPSILON)).astype(jnp.bfloat16)
        turned_back = matmul(left_rot, scaled).astype(jnp.bfloat16)
        back_rows = jnp.concatenate(
            [turned_back[:rows]]
            + [
                swap(turned_back[k * rows : (k + 1) * rows], "shard", k)
                for k in range(1, n_shard)
            ],
            1,
        )
        update = (near_columns(matmul(back_rows, near_rot, 1, 1)) / width).astype(jnp.bfloat16)

        def refreshed(stat, product_of_grads, rot):
            stat_new = BETA_STAT * stat + (1.0 - BETA_STAT) * product_of_grads
            product = matmul(stat_new.astype(jnp.bfloat16), rot)
            start = product / jnp.sqrt(jnp.sum(product * product, axis=0) / width + NORM_EPS)
            current = start.astype(jnp.bfloat16)
            for iteration in range(NS_ITERS):
                kept = width if iteration + 1 < NS_ITERS else rows
                gram = (matmul(current[:kept], current, 1, 1) / width).astype(jnp.bfloat16)
                result = 1.5 * current[:kept].astype(jnp.float32) - 0.5 * matmul(gram, current)
                current = result.astype(jnp.bfloat16)
            return result

        left_new = refreshed(stat_left_full, matmul(gradient, gradient, 1, 1), left_rot)
        right_new = refreshed(stat_right_full, matmul(gradient, gradient, 0, 0), right_rot)
        return (update, second_new, left_new, right_new)

    return body


def solution(mesh):
    n_dp, n_shard = mesh.shape["dp"], mesh.shape["shard"]
    body = fast_body if (n_dp, n_shard) == (16, 2) else make_plain_body(n_dp, n_shard)
    return jax.shard_map(
        body,
        mesh=mesh,
        in_specs=(
            P("dp", "shard", None),
            P("shard", None),
            P(None, "shard"),
            P("shard", None),
            P("shard", None),
            P("shard", None),
            P("shard", None),
        ),
        out_specs=(P("shard", None), P(None, "shard"), P("shard", None), P("shard", None)),
        check_vma=False,
    )
```

```python
import jax
import jax.numpy as jnp
from jax import lax
from jax.experimental import pallas as pl
from jax.experimental.pallas import tpu as pltpu
from jax.sharding import PartitionSpec as P

NS_ITERS = 2


BETA_ONE = 0.9
BETA_TWO = 0.9
BETA_STAT = 0.95
EPSILON = 1e-08
NORM_EPS = 1e-06
HALF = jnp.bfloat16
FULL = jnp.float32
VMEM = pl.BlockSpec(memory_space=pltpu.VMEM)
ANY = pl.BlockSpec(memory_space=pl.ANY)
SMEM = pl.BlockSpec(memory_space=pltpu.SMEM)


def matmul(left_mat, right_mat, left_dim=1, right_dim=0):
    return lax.dot_general(
        left_mat,
        right_mat,
        (((left_dim,), (right_dim,)), ((), ())),
        preferred_element_type=FULL,
    )


def shaped(shape, dtype):
    return jax.ShapeDtypeStruct(shape, dtype)


def tile(index, size):
    return pl.ds(pl.multiple_of(index * size, size), size)


def call(
    kernel, outs, operands, specs, scratch=(), flops=0, moved=0, limit=24, space=VMEM, aliases=None
):
    return pl.pallas_call(
        kernel,
        out_shape=outs,
        in_specs=specs,
        out_specs=[space] * len(outs),
        scratch_shapes=list(scratch),
        input_output_aliases=aliases or {},
        compiler_params=pltpu.CompilerParams(vmem_limit_bytes=limit * 2**20),
        cost_estimate=pl.CostEstimate(flops=flops, bytes_accessed=moved, transcendentals=0),
    )(*operands)


def run_all(copies):
    for copy in copies:
        copy.start()
    for copy in copies:
        copy.wait()


TILES = 4
UPPER = [(i, j) for i in range(TILES) for j in range(i, TILES)]


def pack(out, base, value):
    size = out.shape[1]
    across = value.shape[1] // size
    for band in range(value.shape[0] // size):
        for column in range(across):
            out[base + band * across + column] = value[
                band * size : (band + 1) * size, column * size : (column + 1) * size
            ].astype(HALF)


def diagonal(size):
    shape = (size, size)
    return lax.broadcasted_iota(jnp.int32, shape, 0) == lax.broadcasted_iota(jnp.int32, shape, 1)


def start_kernel(
    where,
    raw,
    came,
    left,
    right,
    stat_left,
    stat_right,
    state,
    kept,
    sent,
    basis_in,
    stat_in,
    sem,
):
    position, core, x = where[0], where[1], where[2]
    half, width = basis_in.shape[1:]
    size = state.shape[1]
    copies = [
        pltpu.make_async_copy(basis.at[tile(core, half)], basis_in.at[i], sem.at[i])
        for i, basis in enumerate((left, right))
    ]
    for copy in copies:
        copy.start()
    for side, stat in enumerate((stat_left, stat_right)):

        @pl.when(core == side)
        def _():
            pltpu.make_async_copy(stat.at[:, tile(position, size * TILES)], stat_in, sem.at[2]).start()

    rows = kept.shape[0]
    for out, there in ((kept, tile(x, rows)), (sent, tile(1 - x, rows))):
        out[...] = (raw[there].astype(FULL) + came[there].astype(FULL)).astype(out.dtype)
    count = half * width // size**2
    for i, copy in enumerate(copies):
        copy.wait()
        pack(state, i * count, basis_in.at[i])
    pltpu.make_async_copy(stat_left.at[:, : size * TILES], stat_in, sem.at[2]).wait()
    same = diagonal(size)
    base = 2 * count
    for place, (i, j) in enumerate(UPPER):
        value = stat_in[i * size : (i + 1) * size, j * size : (j + 1) * size]
        high = value.astype(HALF)
        state[base + place] = high
        if i == j:
            low = jnp.where(same, value - high.astype(FULL), 0.0)
            line = jnp.sum(low, axis=0, keepdims=True)
            state[base + len(UPPER), i * 16 : (i + 1) * 16] = jnp.broadcast_to(
                line, (16, size)
            ).astype(HALF)


def second_sum_kernel(where, kept, came, own, *sent):
    size = own.shape[0]
    z = where[3]
    for k, out in enumerate((own, *sent)):
        there = tile(z ^ k, size)
        out[...] = (kept[there] + came[there].astype(FULL)).astype(out.dtype)


def third_sum_kernel(own, one, two, three, out):
    out[...] = (
        (own[...] + one[...].astype(FULL)) + (two[...].astype(FULL) + three[...].astype(FULL))
    ).astype(HALF)


def joined_kernel(where, *refs):
    out = refs[-1]
    z = where[3]
    size = refs[0].shape[0]
    for k, part in enumerate(refs[:-1]):
        out[tile(z ^ k, size)] = part[...]


def place_basis(where, out, own, mine, theirs, side):
    rows, width = own.shape
    half = rows // 2
    size = mine.shape[1]
    position, core = where[0], where[1]
    across = width // size
    base = side * half * width // size**2
    out[tile(position, rows)] = own[...].astype(HALF)
    other = (1 - position) * 2
    for part, block in ((mine, other + core), (theirs, other + 1 - core)):
        for band in range(half // size):
            here = tile(block * (half // size) + band, size)
            for column in range(across):
                out[here, column * size : (column + 1) * size] = part[base + band * across + column]


def state_kernel(
    where, left, right, mine, theirs, stat_left, stat_right, bases, turned, back, full, sem
):
    rows, width = left.shape
    size = rows // TILES
    position, core = where[0], where[1]
    here, there = tile(position, rows), tile(1 - position, rows)
    for side, stat in enumerate((stat_left, stat_right)):

        @pl.when(core == side)
        def _():
            pltpu.make_async_copy(stat, full.at[here], sem).start()

    place_basis(where, bases.at[core], left, mine, theirs, 0)
    place_basis(where, bases.at[1 - core], right, mine, theirs, 1)
    turned[...] = bases[core].T
    back[...] = bases[1 - core].T
    base = (1 - position) * TILES
    first = rows * width // size**2
    same = diagonal(size)
    for number, (i, j) in enumerate(UPPER):
        value = mine[first + number].astype(FULL)
        if i == j:
            line = mine[first + len(UPPER), i * 16 : (i + 1) * 16].astype(FULL)[:1]
            value = value + jnp.where(same, line, 0.0)
        full[tile(base + i, size), tile(base + j, size)] = value
        if i != j:
            full[tile(base + j, size), tile(base + i, size)] = value.T
    pltpu.make_async_copy(stat_left, full.at[here], sem).wait()
    full[there, here] = full[here, there].T


def moment_kernel(where, moment, bases, own, over_x, next_own, next_over_x, ours, others, half):
    position, core, x = where[0], where[1], where[2]
    size = own.shape[0]
    step = ours.shape[1]
    for place, part in enumerate((own, over_x, next_own, next_over_x)):
        here = tile((core ^ (place // 2)) * 2 + (x ^ (place % 2)), size)
        half[here] = (
            BETA_ONE * moment[here] + (1.0 - BETA_ONE) * part[...].astype(FULL)
        ).astype(HALF)
    there, here = tile((1 - position) * 2 + core, step), tile(position * 2 + core, step)
    others[...] = matmul(half[...], bases[1 - core, :, there]).astype(HALF)
    ours[...] = matmul(half[...], bases[1 - core, :, here]).astype(HALF)


def statistic_kernel(where, bases, turned, stat, second, *refs):
    parts, (half, new, pair, sem) = refs[:-4], refs[-4:]
    position, core, x = where[0], where[1], where[2]
    width = half.shape[0]
    step = new.shape[1]
    gradient = pair.at[core]
    copies = []
    for place, part in enumerate(parts):
        size = part.shape[0]
        block = (
            (position ^ (place // 4)) * 4 + (core ^ (place // 2 % 2)) * 2 + (x ^ (place % 2))
        )
        copies.append(pltpu.make_async_copy(part, gradient.at[tile(block, size)], sem.at[place]))
    run_all(copies)
    for here in quarters(width):
        pair[1 - core, :, here] = gradient[here].T
    block = matmul(gradient[...], bases[1 - core, :, tile(position * 2 + core, step)])
    for here in quarters(width):
        grads = matmul(pair[0], pair[1, :, here])
        half[:, here] = (BETA_STAT * stat[:, here] + (1.0 - BETA_STAT) * grads).astype(HALF)
    grad_rot = matmul(turned[...], block.astype(HALF)) * (1.0 / width)
    new[...] = BETA_TWO * second[:, tile(core, step)] + (1.0 - BETA_TWO) * grad_rot * grad_rot


def adam_kernel(where, bases, turned, mine, came, new, kept, sent):
    width = new.shape[0]
    rows = mine.shape[0]
    position, core = where[0], where[1]
    here, there = tile(position, rows), tile(1 - position, rows)
    moment_rot = (
        matmul(turned[:, here], mine[...]) + matmul(turned[:, there], came[...])
    ) * (1.0 / width)
    scaled = (moment_rot / (jnp.sqrt(new[...]) + EPSILON)).astype(HALF)
    sent[...] = matmul(bases[core, there], scaled).astype(HALF)
    kept[...] = matmul(bases[core, here], scaled).astype(HALF)


def write_part(core, side, block, part, left, right, sem):
    size = part.shape[0]
    here = slice(block * size, (block + 1) * size)
    for place, out in enumerate((left, right)):

        @pl.when((core ^ side) == place)
        def _():
            pltpu.make_async_copy(part, out.at[here], sem).start()

    return pltpu.make_async_copy(part, left.at[here], sem)


def update_kernel(
    where,
    kept,
    came,
    kept_next,
    came_next,
    back,
    low,
    top_next,
    left_in,
    right_in,
    out,
    left,
    right,
    rows_back,
    sem,
):
    rows, width = out.shape
    step = kept.shape[1]
    position, core = where[0], where[1]
    copies = [
        write_part(core, 0, 1, low, left, right, sem.at[0]),
        write_part(core, 1, 0, top_next, left, right, sem.at[1]),
    ]
    for value, place in (
        (kept, position * 2 + core),
        (came, (1 - position) * 2 + core),
        (kept_next, position * 2 + 1 - core),
        (came_next, (1 - position) * 2 + 1 - core),
    ):
        rows_back[:, tile(place, step)] = value[...]
    for here in quarters(width):
        out[:, here] = (matmul(rows_back[...], back[:, here]) * (1.0 / width)).astype(HALF)
    for copy in copies:
        copy.wait()


def next_side_kernel(where, low, left_in, right_in, left, right, sem):
    write_part(where[1], 1, 1, low, left, right, sem.at[0]).wait()


def quarters(width):
    step = width // 4
    return [slice(i * step, (i + 1) * step) for i in range(4)]


def improved(current, turned, kept, gram, result, result_turned):
    size, width = result.shape
    for here in quarters(width):
        gram[:size, here] = (matmul(current[kept], turned[:, here]) * (1.0 / width)).astype(HALF)
    for here in quarters(width):
        value = (
            1.5 * current[kept, here].astype(FULL) - 0.5 * matmul(gram[:size], current[:, here])
        ).astype(result.dtype)
        result[:, here] = value
        if result_turned is not None:
            result_turned[here] = value.T


def refresh_kernel(
    where, stat, bases, new, current, turned, out, second_new, start, start_turned, gram, *scratch
):
    width = stat.shape[0]
    rows = width // 2
    between, sem = scratch[:-1], scratch[-1]
    copy = pltpu.make_async_copy(new, second_new.at[:, tile(where[1], new.shape[1])], sem)
    copy.start()
    for here in quarters(width):
        product = matmul(stat[...], bases[0, :, here])
        square = jnp.sum(product * product, axis=0, keepdims=True) * (1.0 / width)
        value = (product * lax.rsqrt(square + NORM_EPS)).astype(HALF)
        start[:, here] = value
        start_turned[here] = value.T
    source, source_turned = start, start_turned
    for iteration in range(NS_ITERS - 1):
        if iteration + 2 == NS_ITERS:
            result, result_turned = current, turned
        else:
            result, result_turned = between[0].at[iteration % 2], between[1].at[iteration % 2]
        improved(source, source_turned, slice(0, width), gram, result, result_turned)
        source, source_turned = result, result_turned
    improved(current, turned, tile(where[0] * 2, rows // 2), gram, out, None)
    copy.wait()


def last_kernel(
    where, current, turned, top, new_next, second_in, out, left, right, second_new, gram, sem
):
    core = where[1]
    copies = [
        write_part(core, 0, 0, top, left, right, sem.at[0]),
        pltpu.make_async_copy(
            new_next, second_new.at[:, tile(1 - core, new_next.shape[1])], sem.at[1]
        ),
    ]
    copies[1].start()
    improved(current, turned, tile(where[0] * 2 + 1, out.shape[0]), gram, out, None)
    for copy in copies:
        copy.wait()


def fast_body(group_grads, moment, second, stat_left, stat_right, basis_left, basis_right):
    position = lax.axis_index("shard")
    member = lax.axis_index("dp")
    rows, width = moment.shape
    half = rows // 2
    quarter = rows // 4
    chunk = rows // 16
    core, x, z = member & 1, (member >> 1) & 1, member >> 2
    where = jnp.stack([position, core, x, z]).astype(jnp.int32)
    unit = 2 * width**3

    def dp_swap(value, distance):
        return lax.ppermute(value, "dp", [(i, i ^ distance) for i in range(16)])

    def shard_swap(value):
        return lax.ppermute(value, "shard", [(0, 1), (1, 0)])

    def cross_swap(value):
        pairs = [(i, i ^ 5) for i in range(32)]
        return lax.ppermute(value, ("dp", "shard"), pairs)

    raw = lax.dynamic_slice_in_dim(group_grads[0], (1 - core) * half, half, 0)
    came = dp_swap(raw, 1)
    raw = lax.dynamic_slice_in_dim(group_grads[0], core * half, half, 0)
    count = rows * width // quarter**2 + len(UPPER) + 1
    state_sent, kept, sent = call(
        start_kernel,
        [
            shaped((count, quarter, quarter), HALF),
            shaped((quarter, width), FULL),
            shaped((quarter, width), HALF),
        ],
        (where, raw, came, basis_left, basis_right, stat_left, stat_right),
        [SMEM] + [VMEM] * 2 + [ANY] * 4,
        [
            pltpu.VMEM((2, half, width), FULL),
            pltpu.VMEM((rows, rows), FULL),
            pltpu.SemaphoreType.DMA((3,)),
        ],
        moved=2**22,
        limit=50,
    )
    came = dp_swap(sent, 2)
    state_mine = shard_swap(state_sent)
    own, *sent = call(
        second_sum_kernel,
        [shaped((chunk, width), FULL)] + [shaped((chunk, width), HALF)] * 3,
        (where, kept, came),
        [SMEM] + [VMEM] * 2,
        moved=2**20,
    )
    pieces = [dp_swap(value, 4 * (k + 1)) for k, value in enumerate(sent)]
    (piece,) = call(
        third_sum_kernel,
        [shaped((chunk, width), HALF)],
        (own, *pieces),
        [VMEM] * 4,
        moved=2**19,
    )
    pieces = [piece] + [dp_swap(piece, 4 * k) for k in (1, 2, 3)]
    (part,) = call(
        joined_kernel,
        [shaped((quarter, width), HALF)],
        (where, *pieces),
        [SMEM] + [VMEM] * 4,
        moved=2**19,
    )
    part, state_mine = lax.optimization_barrier((part, state_mine))
    parts = [part, dp_swap(part, 2), shard_swap(part), cross_swap(part)]
    state_theirs = dp_swap(state_mine, 1)
    square = shaped((width, width), HALF)
    bases, left_turned, right_turned, stat = call(
        state_kernel,
        [shaped((2, width, width), HALF), square, square, shaped((width, width), FULL)],
        (
            where,
            basis_left,
            basis_right,
            state_mine,
            state_theirs,
            stat_left,
            stat_right,
        ),
        [SMEM] + [VMEM] * 4 + [ANY] * 2,
        [pltpu.SemaphoreType.DMA(())],
        moved=2**24,
    )
    near = parts[:2] + [dp_swap(value, 1) for value in parts[:2]]
    moment_mine, moment_sent = call(
        moment_kernel,
        [shaped((rows, half), HALF)] * 2,
        (where, moment, bases, *near),
        [SMEM] + [VMEM] * 6,
        [pltpu.VMEM((rows, width), HALF)],
        flops=unit // 4,
        moved=2**22,
    )
    moment_came = shard_swap(moment_sent)
    far = list(lax.optimization_barrier((parts[2], parts[3], bases)))[:2]
    far += [dp_swap(value, 1) for value in far]
    stat, new = call(
        statistic_kernel,
        [square, shaped((width, half), FULL)],
        (where, bases, left_turned, stat, second, *near, *far),
        [SMEM] + [VMEM] * 4 + [ANY] * 8,
        [pltpu.VMEM((2, width, width), HALF), pltpu.SemaphoreType.DMA((8,))],
        flops=3 * unit // 2,
        moved=2**23,
    )
    new_next = dp_swap(new, 1)
    stat, moment_came = lax.optimization_barrier((stat, moment_came))
    back_kept, back_sent = call(
        adam_kernel,
        [shaped((rows, half), HALF)] * 2,
        (where, bases, left_turned, moment_mine, moment_came, new),
        [SMEM] + [VMEM] * 5,
        flops=unit // 2,
        moved=2**22,
    )
    stat, back_sent = lax.optimization_barrier((stat, back_sent))
    back_came = shard_swap(back_sent)
    back_kept_next = dp_swap(back_kept, 1)
    current, current_turned, top, second_new = pl.pallas_call(
        refresh_kernel,
        out_shape=[square, square, shaped((half, width), FULL), shaped((width, rows), FULL)],
        in_specs=[SMEM] + [VMEM] * 2 + [ANY],
        out_specs=[VMEM] * 3 + [ANY],
        scratch_shapes=[pltpu.VMEM((width, width), HALF)] * 3
        + [pltpu.VMEM((2, width, width), HALF)] * (2 if NS_ITERS > 2 else 0)
        + [pltpu.SemaphoreType.DMA(())],
        compiler_params=pltpu.CompilerParams(vmem_limit_bytes=24 * 2**20),
        cost_estimate=pl.CostEstimate(
            flops=7 * unit // 2, bytes_accessed=2**23, transcendentals=0
        ),
    )(where, stat, bases, new)
    top_next = dp_swap(top, 1)
    current, back_came, back_kept_next, new_next = lax.optimization_barrier(
        (current, back_came, back_kept_next, new_next)
    )
    back_came_next = dp_swap(back_came, 1)
    side = shaped((rows, width), FULL)
    low, left_new, right_new, second_new = pl.pallas_call(
        last_kernel,
        out_shape=[shaped((half, width), FULL), side, side, shaped((width, rows), FULL)],
        in_specs=[SMEM] + [VMEM] * 2 + [ANY] * 3,
        out_specs=[VMEM] + [ANY] * 3,
        scratch_shapes=[pltpu.VMEM((half, width), HALF), pltpu.SemaphoreType.DMA((2,))],
        input_output_aliases={5: 3},
        compiler_params=pltpu.CompilerParams(vmem_limit_bytes=24 * 2**20),
        cost_estimate=pl.CostEstimate(flops=unit // 2, bytes_accessed=2**22, transcendentals=0),
    )(where, current, current_turned, top, new_next, second_new)
    low, back_came_next = lax.optimization_barrier((low, back_came_next))
    low_next = dp_swap(low, 1)
    update, left_new, right_new = pl.pallas_call(
        update_kernel,
        out_shape=[shaped((rows, width), HALF), side, side],
        in_specs=[SMEM] + [VMEM] * 5 + [ANY] * 4,
        out_specs=[VMEM] + [ANY] * 2,
        scratch_shapes=[pltpu.VMEM((rows, width), HALF), pltpu.SemaphoreType.DMA((2,))],
        input_output_aliases={8: 1, 9: 2},
        compiler_params=pltpu.CompilerParams(vmem_limit_bytes=24 * 2**20),
        cost_estimate=pl.CostEstimate(flops=unit // 2, bytes_accessed=2**22, transcendentals=0),
    )(
        where,
        back_kept,
        back_came,
        back_kept_next,
        back_came_next,
        right_turned,
        low,
        top_next,
        left_new,
        right_new,
    )
    left_new, right_new = call(
        next_side_kernel,
        [side, side],
        (where, low_next, left_new, right_new),
        [SMEM] + [ANY] * 3,
        [pltpu.SemaphoreType.DMA((1,))],
        moved=2**21,
        space=ANY,
        aliases={2: 0, 3: 1},
    )
    return (update, second_new, left_new, right_new)


def make_plain_body(n_dp, n_shard):
    def swap(value, axis, distance):
        size = n_dp if axis == "dp" else n_shard
        return lax.ppermute(value, axis, [(i, i ^ distance) for i in range(size)])

    dp_bits = []
    bit = 1
    while bit < n_dp:
        dp_bits.append(bit)
        bit *= 2

    def ordered(first_is_low, own, other, dim):
        return jnp.where(
            first_is_low,
            jnp.concatenate([own, other], dim),
            jnp.concatenate([other, own], dim),
        )

    def body(group_grads, moment, second, stat_left, stat_right, basis_left, basis_right):
        position = lax.axis_index("shard")
        member = lax.axis_index("dp")
        rows, width = moment.shape
        core = member & 1
        half = rows // 2

        def near_columns(value):
            blocks = [
                lax.dynamic_slice_in_dim(value, (position ^ k) * rows, rows, 1)
                for k in range(n_shard)
            ]
            return jnp.concatenate(blocks, 1)

        def fetch(value, distance):
            size = value.shape[0] // 2
            part = lax.dynamic_slice_in_dim(value, core * size, size, 0)
            part = swap(part, "shard", distance)
            other = swap(part, "dp", 1)
            return ordered(core == 0, part, other, 0)

        left_own = basis_left.astype(jnp.bfloat16)
        right_own = basis_right.astype(jnp.bfloat16)
        left_rot = jnp.concatenate([left_own] + [fetch(left_own, k) for k in range(1, n_shard)], 0)
        right_rot = jnp.concatenate(
            [right_own] + [fetch(right_own, k) for k in range(1, n_shard)], 0
        )

        def whole_stat(stat):
            own = near_columns(stat)
            blocks = [own[:, b * rows : (b + 1) * rows] for b in range(n_shard)]
            bands = [own]
            for k in range(1, n_shard):
                others = [b for b in range(n_shard) if b != k]
                sent = jnp.concatenate([blocks[b] for b in others], 1).astype(jnp.bfloat16)
                came = fetch(sent, k).astype(jnp.float32)
                band = [None] * n_shard
                band[0] = blocks[k].T
                for place, b in enumerate(others):
                    band[k ^ b] = came[:, place * rows : (place + 1) * rows]
                bands.append(jnp.concatenate(band, 1))
            return jnp.concatenate(bands, 0)

        stat_left_full = whole_stat(stat_left)
        stat_right_full = whole_stat(stat_right)

        part = group_grads[0]
        for bit in dp_bits:
            size = part.shape[0] // 2
            high = (member & bit) // bit
            kept = lax.dynamic_slice_in_dim(part, high * size, size, 0)
            sent = lax.dynamic_slice_in_dim(part, (1 - high) * size, size, 0)
            part = kept.astype(jnp.float32) + swap(sent, "dp", bit).astype(jnp.float32)
        chunk = part.astype(jnp.bfloat16)[None]
        chunk = jnp.concatenate([chunk] + [swap(chunk, "shard", k) for k in range(1, n_shard)], 0)
        for bit in reversed(dp_bits):
            chunk = ordered((member & bit) == 0, chunk, swap(chunk, "dp", bit), 1)
        gradient = near_columns(chunk.reshape(width, width))

        grad_rows = gradient[:rows].astype(jnp.float32)
        moment_half = (
            BETA_ONE * near_columns(moment) + (1.0 - BETA_ONE) * grad_rows
        ).astype(jnp.bfloat16)
        near_rot = near_columns(right_rot)
        moment_turned = matmul(moment_half, near_rot).astype(jnp.bfloat16)
        moment_block = jnp.concatenate(
            [moment_turned[:, :rows]]
            + [
                swap(moment_turned[:, k * rows : (k + 1) * rows], "shard", k)
                for k in range(1, n_shard)
            ],
            0,
        )
        grad_block = matmul(gradient, near_rot[:, :rows]).astype(jnp.bfloat16)
        grad_rot = matmul(left_rot, grad_block, 0) / width
        moment_rot = matmul(left_rot, moment_block, 0) / width
        second_new = BETA_TWO * second + (1.0 - BETA_TWO) * grad_rot * grad_rot
        scaled = (moment_rot / (jnp.sqrt(second_new) + EPSILON)).astype(jnp.bfloat16)
        turned_back = matmul(left_rot, scaled).astype(jnp.bfloat16)
        back_rows = jnp.concatenate(
            [turned_back[:rows]]
            + [
                swap(turned_back[k * rows : (k + 1) * rows], "shard", k)
                for k in range(1, n_shard)
            ],
            1,
        )
        update = (near_columns(matmul(back_rows, near_rot, 1, 1)) / width).astype(jnp.bfloat16)

        def refreshed(stat, product_of_grads, rot):
            stat_new = BETA_STAT * stat + (1.0 - BETA_STAT) * product_of_grads
            product = matmul(stat_new.astype(jnp.bfloat16), rot)
            start = product / jnp.sqrt(jnp.sum(product * product, axis=0) / width + NORM_EPS)
            current = start.astype(jnp.bfloat16)
            for iteration in range(NS_ITERS):
                kept = width if iteration + 1 < NS_ITERS else rows
                gram = (matmul(current[:kept], current, 1, 1) / width).astype(jnp.bfloat16)
                result = 1.5 * current[:kept].astype(jnp.float32) - 0.5 * matmul(gram, current)
                current = result.astype(jnp.bfloat16)
            return result

        left_new = refreshed(stat_left_full, matmul(gradient, gradient, 1, 1), left_rot)
        right_new = refreshed(stat_right_full, matmul(gradient, gradient, 0, 0), right_rot)
        return (update, second_new, left_new, right_new)

    return body


def solution(mesh):
    n_dp, n_shard = mesh.shape["dp"], mesh.shape["shard"]
    body = fast_body if (n_dp, n_shard) == (16, 2) else make_plain_body(n_dp, n_shard)
    return jax.shard_map(
        body,
        mesh=mesh,
        in_specs=(
            P("dp", "shard", None),
            P("shard", None),
            P(None, "shard"),
            P("shard", None),
            P("shard", None),
            P("shard", None),
            P("shard", None),
        ),
        out_specs=(P("shard", None), P(None, "shard"), P("shard", None), P("shard", None)),
        check_vma=False,
    )
```

```python
import jax
import jax.numpy as jnp
from jax import lax
from jax.experimental import pallas as pl
from jax.experimental.pallas import tpu as pltpu
from jax.sharding import PartitionSpec as P

NS_ITERS = 2


BETA_ONE = 0.9
BETA_TWO = 0.9
BETA_STAT = 0.95
EPSILON = 1e-08
NORM_EPS = 1e-06
HALF = jnp.bfloat16
FULL = jnp.float32
VMEM = pl.BlockSpec(memory_space=pltpu.VMEM)
ANY = pl.BlockSpec(memory_space=pl.ANY)
SMEM = pl.BlockSpec(memory_space=pltpu.SMEM)


def matmul(left_mat, right_mat, left_dim=1, right_dim=0):
    return lax.dot_general(
        left_mat,
        right_mat,
        (((left_dim,), (right_dim,)), ((), ())),
        preferred_element_type=FULL,
    )


def shaped(shape, dtype):
    return jax.ShapeDtypeStruct(shape, dtype)


def tile(index, size):
    return pl.ds(pl.multiple_of(index * size, size), size)


def call(
    kernel, outs, operands, specs, scratch=(), flops=0, moved=0, limit=24, space=VMEM, aliases=None
):
    return pl.pallas_call(
        kernel,
        out_shape=outs,
        in_specs=specs,
        out_specs=[space] * len(outs),
        scratch_shapes=list(scratch),
        input_output_aliases=aliases or {},
        compiler_params=pltpu.CompilerParams(vmem_limit_bytes=limit * 2**20),
        cost_estimate=pl.CostEstimate(flops=flops, bytes_accessed=moved, transcendentals=0),
    )(*operands)


def run_all(copies):
    for copy in copies:
        copy.start()
    for copy in copies:
        copy.wait()


TILES = 4
UPPER = [(i, j) for i in range(TILES) for j in range(i, TILES)]


def pack(out, base, value):
    size = out.shape[1]
    across = value.shape[1] // size
    for band in range(value.shape[0] // size):
        for column in range(across):
            out[base + band * across + column] = value[
                band * size : (band + 1) * size, column * size : (column + 1) * size
            ].astype(HALF)


def diagonal(size):
    shape = (size, size)
    return lax.broadcasted_iota(jnp.int32, shape, 0) == lax.broadcasted_iota(jnp.int32, shape, 1)


def start_kernel(
    where,
    raw,
    came,
    left,
    right,
    stat_left,
    stat_right,
    state,
    kept,
    sent,
    basis_in,
    stat_in,
    sem,
):
    position, core, x = where[0], where[1], where[2]
    half, width = basis_in.shape[1:]
    size = state.shape[1]
    copies = [
        pltpu.make_async_copy(basis.at[tile(core, half)], basis_in.at[i], sem.at[i])
        for i, basis in enumerate((left, right))
    ]
    for copy in copies:
        copy.start()
    for side, stat in enumerate((stat_left, stat_right)):

        @pl.when(core == side)
        def _():
            pltpu.make_async_copy(stat.at[:, tile(position, size * TILES)], stat_in, sem.at[2]).start()

    rows = kept.shape[0]
    for out, there in ((kept, tile(x, rows)), (sent, tile(1 - x, rows))):
        out[...] = (raw[there].astype(FULL) + came[there].astype(FULL)).astype(out.dtype)
    count = half * width // size**2
    for i, copy in enumerate(copies):
        copy.wait()
        pack(state, i * count, basis_in.at[i])
    pltpu.make_async_copy(stat_left.at[:, : size * TILES], stat_in, sem.at[2]).wait()
    same = diagonal(size)
    base = 2 * count
    for place, (i, j) in enumerate(UPPER):
        value = stat_in[i * size : (i + 1) * size, j * size : (j + 1) * size]
        high = value.astype(HALF)
        state[base + place] = high
        if i == j:
            low = jnp.where(same, value - high.astype(FULL), 0.0)
            line = jnp.sum(low, axis=0, keepdims=True)
            state[base + len(UPPER), i * 16 : (i + 1) * 16] = jnp.broadcast_to(
                line, (16, size)
            ).astype(HALF)


def second_sum_kernel(where, kept, came, own, *sent):
    size = own.shape[0]
    z = where[3]
    for k, out in enumerate((own, *sent)):
        there = tile(z ^ k, size)
        out[...] = (kept[there] + came[there].astype(FULL)).astype(out.dtype)


def third_sum_kernel(own, one, two, three, out):
    out[...] = (
        (own[...] + one[...].astype(FULL)) + (two[...].astype(FULL) + three[...].astype(FULL))
    ).astype(HALF)


def joined_kernel(where, *refs):
    out = refs[-1]
    z = where[3]
    size = refs[0].shape[0]
    for k, part in enumerate(refs[:-1]):
        out[tile(z ^ k, size)] = part[...]


def place_basis(where, out, own, mine, theirs, side):
    rows, width = own.shape
    half = rows // 2
    size = mine.shape[1]
    position, core = where[0], where[1]
    across = width // size
    base = side * half * width // size**2
    out[tile(position, rows)] = own[...].astype(HALF)
    other = (1 - position) * 2
    for part, block in ((mine, other + core), (theirs, other + 1 - core)):
        for band in range(half // size):
            here = tile(block * (half // size) + band, size)
            for column in range(across):
                out[here, column * size : (column + 1) * size] = part[base + band * across + column]


def state_kernel(
    where, left, right, mine, theirs, stat_left, stat_right, bases, turned, back, full, sem
):
    rows, width = left.shape
    size = rows // TILES
    position, core = where[0], where[1]
    here, there = tile(position, rows), tile(1 - position, rows)
    for side, stat in enumerate((stat_left, stat_right)):

        @pl.when(core == side)
        def _():
            pltpu.make_async_copy(stat, full.at[here], sem).start()

    place_basis(where, bases.at[core], left, mine, theirs, 0)
    place_basis(where, bases.at[1 - core], right, mine, theirs, 1)
    turned[...] = bases[core].T
    back[...] = bases[1 - core].T
    base = (1 - position) * TILES
    first = rows * width // size**2
    same = diagonal(size)
    for number, (i, j) in enumerate(UPPER):
        value = mine[first + number].astype(FULL)
        if i == j:
            line = mine[first + len(UPPER), i * 16 : (i + 1) * 16].astype(FULL)[:1]
            value = value + jnp.where(same, line, 0.0)
        full[tile(base + i, size), tile(base + j, size)] = value
        if i != j:
            full[tile(base + j, size), tile(base + i, size)] = value.T
    pltpu.make_async_copy(stat_left, full.at[here], sem).wait()
    full[there, here] = full[here, there].T


def moment_kernel(where, moment, bases, own, over_x, next_own, next_over_x, ours, others, half):
    position, core, x = where[0], where[1], where[2]
    size = own.shape[0]
    step = ours.shape[1]
    for place, part in enumerate((own, over_x, next_own, next_over_x)):
        here = tile((core ^ (place // 2)) * 2 + (x ^ (place % 2)), size)
        half[here] = (
            BETA_ONE * moment[here] + (1.0 - BETA_ONE) * part[...].astype(FULL)
        ).astype(HALF)
    there, here = tile((1 - position) * 2 + core, step), tile(position * 2 + core, step)
    others[...] = matmul(half[...], bases[1 - core, :, there]).astype(HALF)
    ours[...] = matmul(half[...], bases[1 - core, :, here]).astype(HALF)


def place_symmetric(out, here, value):
    out[: here.stop, here] = value
    if here.start:
        out[here, : here.start] = value[: here.start].T


def statistic_kernel(where, bases, turned, stat, second, *refs):
    parts, (half, new, pair, sem) = refs[:-4], refs[-4:]
    position, core, x = where[0], where[1], where[2]
    width = half.shape[0]
    step = new.shape[1]
    gradient = pair.at[core]
    copies = []
    for place, part in enumerate(parts):
        size = part.shape[0]
        block = (
            (position ^ (place // 4)) * 4 + (core ^ (place // 2 % 2)) * 2 + (x ^ (place % 2))
        )
        copies.append(pltpu.make_async_copy(part, gradient.at[tile(block, size)], sem.at[place]))
    run_all(copies)
    for here in quarters(width):
        pair[1 - core, :, here] = gradient[here].T
    block = matmul(gradient[...], bases[1 - core, :, tile(position * 2 + core, step)])
    for here in reversed(quarters(width)):
        above = slice(0, here.stop)
        grads = matmul(pair[0, above], pair[1, :, here])
        value = (BETA_STAT * stat[above, here] + (1.0 - BETA_STAT) * grads).astype(HALF)
        place_symmetric(half, here, value)
    grad_rot = matmul(turned[...], block.astype(HALF)) * (1.0 / width)
    new[...] = BETA_TWO * second[:, tile(core, step)] + (1.0 - BETA_TWO) * grad_rot * grad_rot


def adam_kernel(where, bases, turned, mine, came, new, kept, sent):
    width = new.shape[0]
    rows = mine.shape[0]
    position, core = where[0], where[1]
    here, there = tile(position, rows), tile(1 - position, rows)
    moment_rot = (
        matmul(turned[:, here], mine[...]) + matmul(turned[:, there], came[...])
    ) * (1.0 / width)
    scaled = (moment_rot / (jnp.sqrt(new[...]) + EPSILON)).astype(HALF)
    sent[...] = matmul(bases[core, there], scaled).astype(HALF)
    kept[...] = matmul(bases[core, here], scaled).astype(HALF)


def write_part(core, side, block, part, left, right, sem):
    size = part.shape[0]
    here = slice(block * size, (block + 1) * size)
    for place, out in enumerate((left, right)):

        @pl.when((core ^ side) == place)
        def _():
            pltpu.make_async_copy(part, out.at[here], sem).start()

    return pltpu.make_async_copy(part, left.at[here], sem)


def update_kernel(
    where,
    kept,
    came,
    kept_next,
    came_next,
    back,
    low,
    top_next,
    left_in,
    right_in,
    out,
    left,
    right,
    rows_back,
    sem,
):
    rows, width = out.shape
    step = kept.shape[1]
    position, core = where[0], where[1]
    copies = [
        write_part(core, 0, 1, low, left, right, sem.at[0]),
        write_part(core, 1, 0, top_next, left, right, sem.at[1]),
    ]
    for value, place in (
        (kept, position * 2 + core),
        (came, (1 - position) * 2 + core),
        (kept_next, position * 2 + 1 - core),
        (came_next, (1 - position) * 2 + 1 - core),
    ):
        rows_back[:, tile(place, step)] = value[...]
    for here in quarters(width):
        out[:, here] = (matmul(rows_back[...], back[:, here]) * (1.0 / width)).astype(HALF)
    for copy in copies:
        copy.wait()


def next_side_kernel(where, low, left_in, right_in, left, right, sem):
    write_part(where[1], 1, 1, low, left, right, sem.at[0]).wait()


def quarters(width):
    step = width // 4
    return [slice(i * step, (i + 1) * step) for i in range(4)]


def improved(current, turned, kept, gram, result, result_turned):
    size, width = result.shape
    if size == width:
        for here in reversed(quarters(width)):
            product = matmul(current[: here.stop], turned[:, here]) * (1.0 / width)
            place_symmetric(gram, here, product.astype(HALF))
    else:
        for here in quarters(width):
            product = matmul(current[kept], turned[:, here]) * (1.0 / width)
            gram[:size, here] = product.astype(HALF)
    for here in quarters(width):
        value = (
            1.5 * current[kept, here].astype(FULL) - 0.5 * matmul(gram[:size], current[:, here])
        ).astype(result.dtype)
        result[:, here] = value
        if result_turned is not None:
            result_turned[here] = value.T


def refresh_kernel(
    where, stat, bases, new, current, turned, out, second_new, start, start_turned, gram, *scratch
):
    width = stat.shape[0]
    rows = width // 2
    between, sem = scratch[:-1], scratch[-1]
    copy = pltpu.make_async_copy(new, second_new.at[:, tile(where[1], new.shape[1])], sem)
    copy.start()
    for here in quarters(width):
        product = matmul(stat[...], bases[0, :, here])
        square = jnp.sum(product * product, axis=0, keepdims=True) * (1.0 / width)
        value = (product * lax.rsqrt(square + NORM_EPS)).astype(HALF)
        start[:, here] = value
        start_turned[here] = value.T
    source, source_turned = start, start_turned
    for iteration in range(NS_ITERS - 1):
        if iteration + 2 == NS_ITERS:
            result, result_turned = current, turned
        else:
            result, result_turned = between[0].at[iteration % 2], between[1].at[iteration % 2]
        improved(source, source_turned, slice(0, width), gram, result, result_turned)
        source, source_turned = result, result_turned
    improved(current, turned, tile(where[0] * 2, rows // 2), gram, out, None)
    copy.wait()


def last_kernel(
    where, current, turned, top, new_next, second_in, out, left, right, second_new, gram, sem
):
    core = where[1]
    copies = [
        write_part(core, 0, 0, top, left, right, sem.at[0]),
        pltpu.make_async_copy(
            new_next, second_new.at[:, tile(1 - core, new_next.shape[1])], sem.at[1]
        ),
    ]
    copies[1].start()
    improved(current, turned, tile(where[0] * 2 + 1, out.shape[0]), gram, out, None)
    for copy in copies:
        copy.wait()


def fast_body(group_grads, moment, second, stat_left, stat_right, basis_left, basis_right):
    position = lax.axis_index("shard")
    member = lax.axis_index("dp")
    rows, width = moment.shape
    half = rows // 2
    quarter = rows // 4
    chunk = rows // 16
    core, x, z = member & 1, (member >> 1) & 1, member >> 2
    where = jnp.stack([position, core, x, z]).astype(jnp.int32)
    unit = 2 * width**3

    def dp_swap(value, distance):
        return lax.ppermute(value, "dp", [(i, i ^ distance) for i in range(16)])

    def shard_swap(value):
        return lax.ppermute(value, "shard", [(0, 1), (1, 0)])

    def cross_swap(value):
        pairs = [(i, i ^ 5) for i in range(32)]
        return lax.ppermute(value, ("dp", "shard"), pairs)

    raw = lax.dynamic_slice_in_dim(group_grads[0], (1 - core) * half, half, 0)
    came = dp_swap(raw, 1)
    raw = lax.dynamic_slice_in_dim(group_grads[0], core * half, half, 0)
    count = rows * width // quarter**2 + len(UPPER) + 1
    state_sent, kept, sent = call(
        start_kernel,
        [
            shaped((count, quarter, quarter), HALF),
            shaped((quarter, width), FULL),
            shaped((quarter, width), HALF),
        ],
        (where, raw, came, basis_left, basis_right, stat_left, stat_right),
        [SMEM] + [VMEM] * 2 + [ANY] * 4,
        [
            pltpu.VMEM((2, half, width), FULL),
            pltpu.VMEM((rows, rows), FULL),
            pltpu.SemaphoreType.DMA((3,)),
        ],
        moved=2**22,
        limit=50,
    )
    came = dp_swap(sent, 2)
    state_mine = shard_swap(state_sent)
    own, *sent = call(
        second_sum_kernel,
        [shaped((chunk, width), FULL)] + [shaped((chunk, width), HALF)] * 3,
        (where, kept, came),
        [SMEM] + [VMEM] * 2,
        moved=2**20,
    )
    pieces = [dp_swap(value, 4 * (k + 1)) for k, value in enumerate(sent)]
    (piece,) = call(
        third_sum_kernel,
        [shaped((chunk, width), HALF)],
        (own, *pieces),
        [VMEM] * 4,
        moved=2**19,
    )
    pieces = [piece] + [dp_swap(piece, 4 * k) for k in (1, 2, 3)]
    (part,) = call(
        joined_kernel,
        [shaped((quarter, width), HALF)],
        (where, *pieces),
        [SMEM] + [VMEM] * 4,
        moved=2**19,
    )
    part, state_mine = lax.optimization_barrier((part, state_mine))
    parts = [part, dp_swap(part, 2), shard_swap(part), cross_swap(part)]
    state_theirs = dp_swap(state_mine, 1)
    square = shaped((width, width), HALF)
    bases, left_turned, right_turned, stat = call(
        state_kernel,
        [shaped((2, width, width), HALF), square, square, shaped((width, width), FULL)],
        (
            where,
            basis_left,
            basis_right,
            state_mine,
            state_theirs,
            stat_left,
            stat_right,
        ),
        [SMEM] + [VMEM] * 4 + [ANY] * 2,
        [pltpu.SemaphoreType.DMA(())],
        moved=2**24,
    )
    near = parts[:2] + [dp_swap(value, 1) for value in parts[:2]]
    moment_mine, moment_sent = call(
        moment_kernel,
        [shaped((rows, half), HALF)] * 2,
        (where, moment, bases, *near),
        [SMEM] + [VMEM] * 6,
        [pltpu.VMEM((rows, width), HALF)],
        flops=unit // 4,
        moved=2**22,
    )
    moment_came = shard_swap(moment_sent)
    far = list(lax.optimization_barrier((parts[2], parts[3], bases)))[:2]
    far += [dp_swap(value, 1) for value in far]
    stat, new = call(
        statistic_kernel,
        [square, shaped((width, half), FULL)],
        (where, bases, left_turned, stat, second, *near, *far),
        [SMEM] + [VMEM] * 4 + [ANY] * 8,
        [pltpu.VMEM((2, width, width), HALF), pltpu.SemaphoreType.DMA((8,))],
        flops=3 * unit // 2,
        moved=2**23,
    )
    new_next = dp_swap(new, 1)
    stat, moment_came = lax.optimization_barrier((stat, moment_came))
    back_kept, back_sent = call(
        adam_kernel,
        [shaped((rows, half), HALF)] * 2,
        (where, bases, left_turned, moment_mine, moment_came, new),
        [SMEM] + [VMEM] * 5,
        flops=unit // 2,
        moved=2**22,
    )
    stat, back_sent = lax.optimization_barrier((stat, back_sent))
    back_came = shard_swap(back_sent)
    back_kept_next = dp_swap(back_kept, 1)
    current, current_turned, top, second_new = pl.pallas_call(
        refresh_kernel,
        out_shape=[square, square, shaped((half, width), FULL), shaped((width, rows), FULL)],
        in_specs=[SMEM] + [VMEM] * 2 + [ANY],
        out_specs=[VMEM] * 3 + [ANY],
        scratch_shapes=[pltpu.VMEM((width, width), HALF)] * 3
        + [pltpu.VMEM((2, width, width), HALF)] * (2 if NS_ITERS > 2 else 0)
        + [pltpu.SemaphoreType.DMA(())],
        compiler_params=pltpu.CompilerParams(vmem_limit_bytes=24 * 2**20),
        cost_estimate=pl.CostEstimate(
            flops=7 * unit // 2, bytes_accessed=2**23, transcendentals=0
        ),
    )(where, stat, bases, new)
    top_next = dp_swap(top, 1)
    current, back_came, back_kept_next, new_next = lax.optimization_barrier(
        (current, back_came, back_kept_next, new_next)
    )
    back_came_next = dp_swap(back_came, 1)
    side = shaped((rows, width), FULL)
    low, left_new, right_new, second_new = pl.pallas_call(
        last_kernel,
        out_shape=[shaped((half, width), FULL), side, side, shaped((width, rows), FULL)],
        in_specs=[SMEM] + [VMEM] * 2 + [ANY] * 3,
        out_specs=[VMEM] + [ANY] * 3,
        scratch_shapes=[pltpu.VMEM((half, width), HALF), pltpu.SemaphoreType.DMA((2,))],
        input_output_aliases={5: 3},
        compiler_params=pltpu.CompilerParams(vmem_limit_bytes=24 * 2**20),
        cost_estimate=pl.CostEstimate(flops=unit // 2, bytes_accessed=2**22, transcendentals=0),
    )(where, current, current_turned, top, new_next, second_new)
    low, back_came_next = lax.optimization_barrier((low, back_came_next))
    low_next = dp_swap(low, 1)
    update, left_new, right_new = pl.pallas_call(
        update_kernel,
        out_shape=[shaped((rows, width), HALF), side, side],
        in_specs=[SMEM] + [VMEM] * 5 + [ANY] * 4,
        out_specs=[VMEM] + [ANY] * 2,
        scratch_shapes=[pltpu.VMEM((rows, width), HALF), pltpu.SemaphoreType.DMA((2,))],
        input_output_aliases={8: 1, 9: 2},
        compiler_params=pltpu.CompilerParams(vmem_limit_bytes=24 * 2**20),
        cost_estimate=pl.CostEstimate(flops=unit // 2, bytes_accessed=2**22, transcendentals=0),
    )(
        where,
        back_kept,
        back_came,
        back_kept_next,
        back_came_next,
        right_turned,
        low,
        top_next,
        left_new,
        right_new,
    )
    left_new, right_new = call(
        next_side_kernel,
        [side, side],
        (where, low_next, left_new, right_new),
        [SMEM] + [ANY] * 3,
        [pltpu.SemaphoreType.DMA((1,))],
        moved=2**21,
        space=ANY,
        aliases={2: 0, 3: 1},
    )
    return (update, second_new, left_new, right_new)


def make_plain_body(n_dp, n_shard):
    def swap(value, axis, distance):
        size = n_dp if axis == "dp" else n_shard
        return lax.ppermute(value, axis, [(i, i ^ distance) for i in range(size)])

    dp_bits = []
    bit = 1
    while bit < n_dp:
        dp_bits.append(bit)
        bit *= 2

    def ordered(first_is_low, own, other, dim):
        return jnp.where(
            first_is_low,
            jnp.concatenate([own, other], dim),
            jnp.concatenate([other, own], dim),
        )

    def body(group_grads, moment, second, stat_left, stat_right, basis_left, basis_right):
        position = lax.axis_index("shard")
        member = lax.axis_index("dp")
        rows, width = moment.shape
        core = member & 1
        half = rows // 2

        def near_columns(value):
            blocks = [
                lax.dynamic_slice_in_dim(value, (position ^ k) * rows, rows, 1)
                for k in range(n_shard)
            ]
            return jnp.concatenate(blocks, 1)

        def fetch(value, distance):
            size = value.shape[0] // 2
            part = lax.dynamic_slice_in_dim(value, core * size, size, 0)
            part = swap(part, "shard", distance)
            other = swap(part, "dp", 1)
            return ordered(core == 0, part, other, 0)

        left_own = basis_left.astype(jnp.bfloat16)
        right_own = basis_right.astype(jnp.bfloat16)
        left_rot = jnp.concatenate([left_own] + [fetch(left_own, k) for k in range(1, n_shard)], 0)
        right_rot = jnp.concatenate(
            [right_own] + [fetch(right_own, k) for k in range(1, n_shard)], 0
        )

        def whole_stat(stat):
            own = near_columns(stat)
            blocks = [own[:, b * rows : (b + 1) * rows] for b in range(n_shard)]
            bands = [own]
            for k in range(1, n_shard):
                others = [b for b in range(n_shard) if b != k]
                sent = jnp.concatenate([blocks[b] for b in others], 1).astype(jnp.bfloat16)
                came = fetch(sent, k).astype(jnp.float32)
                band = [None] * n_shard
                band[0] = blocks[k].T
                for place, b in enumerate(others):
                    band[k ^ b] = came[:, place * rows : (place + 1) * rows]
                bands.append(jnp.concatenate(band, 1))
            return jnp.concatenate(bands, 0)

        stat_left_full = whole_stat(stat_left)
        stat_right_full = whole_stat(stat_right)

        part = group_grads[0]
        for bit in dp_bits:
            size = part.shape[0] // 2
            high = (member & bit) // bit
            kept = lax.dynamic_slice_in_dim(part, high * size, size, 0)
            sent = lax.dynamic_slice_in_dim(part, (1 - high) * size, size, 0)
            part = kept.astype(jnp.float32) + swap(sent, "dp", bit).astype(jnp.float32)
        chunk = part.astype(jnp.bfloat16)[None]
        chunk = jnp.concatenate([chunk] + [swap(chunk, "shard", k) for k in range(1, n_shard)], 0)
        for bit in reversed(dp_bits):
            chunk = ordered((member & bit) == 0, chunk, swap(chunk, "dp", bit), 1)
        gradient = near_columns(chunk.reshape(width, width))

        grad_rows = gradient[:rows].astype(jnp.float32)
        moment_half = (
            BETA_ONE * near_columns(moment) + (1.0 - BETA_ONE) * grad_rows
        ).astype(jnp.bfloat16)
        near_rot = near_columns(right_rot)
        moment_turned = matmul(moment_half, near_rot).astype(jnp.bfloat16)
        moment_block = jnp.concatenate(
            [moment_turned[:, :rows]]
            + [
                swap(moment_turned[:, k * rows : (k + 1) * rows], "shard", k)
                for k in range(1, n_shard)
            ],
            0,
        )
        grad_block = matmul(gradient, near_rot[:, :rows]).astype(jnp.bfloat16)
        grad_rot = matmul(left_rot, grad_block, 0) / width
        moment_rot = matmul(left_rot, moment_block, 0) / width
        second_new = BETA_TWO * second + (1.0 - BETA_TWO) * grad_rot * grad_rot
        scaled = (moment_rot / (jnp.sqrt(second_new) + EPSILON)).astype(jnp.bfloat16)
        turned_back = matmul(left_rot, scaled).astype(jnp.bfloat16)
        back_rows = jnp.concatenate(
            [turned_back[:rows]]
            + [
                swap(turned_back[k * rows : (k + 1) * rows], "shard", k)
                for k in range(1, n_shard)
            ],
            1,
        )
        update = (near_columns(matmul(back_rows, near_rot, 1, 1)) / width).astype(jnp.bfloat16)

        def refreshed(stat, product_of_grads, rot):
            stat_new = BETA_STAT * stat + (1.0 - BETA_STAT) * product_of_grads
            product = matmul(stat_new.astype(jnp.bfloat16), rot)
            start = product / jnp.sqrt(jnp.sum(product * product, axis=0) / width + NORM_EPS)
            current = start.astype(jnp.bfloat16)
            for iteration in range(NS_ITERS):
                kept = width if iteration + 1 < NS_ITERS else rows
                gram = (matmul(current[:kept], current, 1, 1) / width).astype(jnp.bfloat16)
                result = 1.5 * current[:kept].astype(jnp.float32) - 0.5 * matmul(gram, current)
                current = result.astype(jnp.bfloat16)
            return result

        left_new = refreshed(stat_left_full, matmul(gradient, gradient, 1, 1), left_rot)
        right_new = refreshed(stat_right_full, matmul(gradient, gradient, 0, 0), right_rot)
        return (update, second_new, left_new, right_new)

    return body


def solution(mesh):
    n_dp, n_shard = mesh.shape["dp"], mesh.shape["shard"]
    body = fast_body if (n_dp, n_shard) == (16, 2) else make_plain_body(n_dp, n_shard)
    return jax.shard_map(
        body,
        mesh=mesh,
        in_specs=(
            P("dp", "shard", None),
            P("shard", None),
            P(None, "shard"),
            P("shard", None),
            P("shard", None),
            P("shard", None),
            P("shard", None),
        ),
        out_specs=(P("shard", None), P(None, "shard"), P("shard", None), P("shard", None)),
        check_vma=False,
    )
```

```python
import jax
import jax.numpy as jnp
from jax import lax
from jax.experimental import pallas as pl
from jax.experimental.pallas import tpu as pltpu
from jax.sharding import PartitionSpec as P

NS_ITERS = 2


BETA_ONE = 0.9
BETA_TWO = 0.9
BETA_STAT = 0.95
EPSILON = 1e-08
NORM_EPS = 1e-06
HALF = jnp.bfloat16
FULL = jnp.float32
VMEM = pl.BlockSpec(memory_space=pltpu.VMEM)
ANY = pl.BlockSpec(memory_space=pl.ANY)
SMEM = pl.BlockSpec(memory_space=pltpu.SMEM)


def matmul(left_mat, right_mat, left_dim=1, right_dim=0):
    return lax.dot_general(
        left_mat,
        right_mat,
        (((left_dim,), (right_dim,)), ((), ())),
        preferred_element_type=FULL,
    )


def shaped(shape, dtype):
    return jax.ShapeDtypeStruct(shape, dtype)


def tile(index, size):
    return pl.ds(pl.multiple_of(index * size, size), size)


def call(
    kernel, outs, operands, specs, scratch=(), flops=0, moved=0, limit=24, space=VMEM, aliases=None
):
    return pl.pallas_call(
        kernel,
        out_shape=outs,
        in_specs=specs,
        out_specs=[space] * len(outs),
        scratch_shapes=list(scratch),
        input_output_aliases=aliases or {},
        compiler_params=pltpu.CompilerParams(vmem_limit_bytes=limit * 2**20),
        cost_estimate=pl.CostEstimate(flops=flops, bytes_accessed=moved, transcendentals=0),
    )(*operands)


def run_all(copies):
    for copy in copies:
        copy.start()
    for copy in copies:
        copy.wait()


TILES = 4
UPPER = [(i, j) for i in range(TILES) for j in range(i, TILES)]


def pack(out, base, value):
    size = out.shape[1]
    across = value.shape[1] // size
    for band in range(value.shape[0] // size):
        for column in range(across):
            out[base + band * across + column] = value[
                band * size : (band + 1) * size, column * size : (column + 1) * size
            ].astype(HALF)


def diagonal(size):
    shape = (size, size)
    return lax.broadcasted_iota(jnp.int32, shape, 0) == lax.broadcasted_iota(jnp.int32, shape, 1)


def start_kernel(
    where,
    raw,
    came,
    left,
    right,
    stat_left,
    stat_right,
    state,
    kept,
    sent,
    basis_in,
    stat_in,
    sem,
):
    position, core, x = where[0], where[1], where[2]
    half, width = basis_in.shape[1:]
    size = state.shape[1]
    copies = [
        pltpu.make_async_copy(basis.at[tile(core, half)], basis_in.at[i], sem.at[i])
        for i, basis in enumerate((left, right))
    ]
    for copy in copies:
        copy.start()
    for side, stat in enumerate((stat_left, stat_right)):

        @pl.when(core == side)
        def _():
            pltpu.make_async_copy(stat.at[:, tile(position, size * TILES)], stat_in, sem.at[2]).start()

    rows = kept.shape[0]
    for out, there in ((kept, tile(x, rows)), (sent, tile(1 - x, rows))):
        out[...] = (raw[there].astype(FULL) + came[there].astype(FULL)).astype(out.dtype)
    count = half * width // size**2
    for i, copy in enumerate(copies):
        copy.wait()
        pack(state, i * count, basis_in.at[i])
    pltpu.make_async_copy(stat_left.at[:, : size * TILES], stat_in, sem.at[2]).wait()
    same = diagonal(size)
    base = 2 * count
    for place, (i, j) in enumerate(UPPER):
        value = stat_in[i * size : (i + 1) * size, j * size : (j + 1) * size]
        high = value.astype(HALF)
        state[base + place] = high
        if i == j:
            low = jnp.where(same, value - high.astype(FULL), 0.0)
            line = jnp.sum(low, axis=0, keepdims=True)
            state[base + len(UPPER), i * 16 : (i + 1) * 16] = jnp.broadcast_to(
                line, (16, size)
            ).astype(HALF)


def second_sum_kernel(where, kept, came, own, *sent):
    size = own.shape[0]
    z = where[3]
    for k, out in enumerate((own, *sent)):
        there = tile(z ^ k, size)
        out[...] = (kept[there] + came[there].astype(FULL)).astype(out.dtype)


def third_sum_kernel(own, one, two, three, out):
    out[...] = (
        (own[...] + one[...].astype(FULL)) + (two[...].astype(FULL) + three[...].astype(FULL))
    ).astype(HALF)


def joined_kernel(where, *refs):
    out = refs[-1]
    z = where[3]
    size = refs[0].shape[0]
    for k, part in enumerate(refs[:-1]):
        out[tile(z ^ k, size)] = part[...]


def place_basis(where, out, own, mine, theirs, side):
    rows, width = own.shape
    half = rows // 2
    size = mine.shape[1]
    position, core = where[0], where[1]
    across = width // size
    base = side * half * width // size**2
    out[tile(position, rows)] = own[...].astype(HALF)
    other = (1 - position) * 2
    for part, block in ((mine, other + core), (theirs, other + 1 - core)):
        for band in range(half // size):
            here = tile(block * (half // size) + band, size)
            for column in range(across):
                out[here, column * size : (column + 1) * size] = part[base + band * across + column]


def state_kernel(
    where, left, right, mine, theirs, stat_left, stat_right, bases, turned, back, full, sem
):
    rows, width = left.shape
    size = rows // TILES
    position, core = where[0], where[1]
    here, there = tile(position, rows), tile(1 - position, rows)
    for side, stat in enumerate((stat_left, stat_right)):

        @pl.when(core == side)
        def _():
            pltpu.make_async_copy(stat, full.at[here], sem).start()

    place_basis(where, bases.at[core], left, mine, theirs, 0)
    place_basis(where, bases.at[1 - core], right, mine, theirs, 1)
    turned[...] = bases[core].T
    back[...] = bases[1 - core].T
    base = (1 - position) * TILES
    first = rows * width // size**2
    same = diagonal(size)
    for number, (i, j) in enumerate(UPPER):
        value = mine[first + number].astype(FULL)
        if i == j:
            line = mine[first + len(UPPER), i * 16 : (i + 1) * 16].astype(FULL)[:1]
            value = value + jnp.where(same, line, 0.0)
        full[tile(base + i, size), tile(base + j, size)] = value
        if i != j:
            full[tile(base + j, size), tile(base + i, size)] = value.T
    pltpu.make_async_copy(stat_left, full.at[here], sem).wait()
    full[there, here] = full[here, there].T


def moment_kernel(where, moment, bases, own, over_x, next_own, next_over_x, ours, others, half):
    position, core, x = where[0], where[1], where[2]
    size = own.shape[0]
    step = ours.shape[1]
    for place, part in enumerate((own, over_x, next_own, next_over_x)):
        here = tile((core ^ (place // 2)) * 2 + (x ^ (place % 2)), size)
        half[here] = (
            BETA_ONE * moment[here] + (1.0 - BETA_ONE) * part[...].astype(FULL)
        ).astype(HALF)
    there, here = tile((1 - position) * 2 + core, step), tile(position * 2 + core, step)
    others[...] = matmul(half[...], bases[1 - core, :, there]).astype(HALF)
    ours[...] = matmul(half[...], bases[1 - core, :, here]).astype(HALF)


def place_symmetric(out, here, value):
    out[: here.stop, here] = value
    if here.start:
        out[here, : here.start] = value[: here.start].T


def statistic_kernel(where, bases, turned, stat, second, *refs):
    parts, (start, start_turned, new, pair, half, sem) = refs[:-6], refs[-6:]
    position, core, x = where[0], where[1], where[2]
    width = half.shape[0]
    step = new.shape[1]
    gradient = pair.at[core]
    copies = []
    for place, part in enumerate(parts):
        size = part.shape[0]
        block = (
            (position ^ (place // 4)) * 4 + (core ^ (place // 2 % 2)) * 2 + (x ^ (place % 2))
        )
        copies.append(pltpu.make_async_copy(part, gradient.at[tile(block, size)], sem.at[place]))
    run_all(copies)
    for here in quarters(width):
        pair[1 - core, :, here] = gradient[here].T
    block = matmul(gradient[...], bases[1 - core, :, tile(position * 2 + core, step)])
    for here in reversed(quarters(width)):
        above = slice(0, here.stop)
        grads = matmul(pair[0, above], pair[1, :, here])
        value = (BETA_STAT * stat[above, here] + (1.0 - BETA_STAT) * grads).astype(HALF)
        place_symmetric(half, here, value)
    grad_rot = matmul(turned[...], block.astype(HALF)) * (1.0 / width)
    new[...] = BETA_TWO * second[:, tile(core, step)] + (1.0 - BETA_TWO) * grad_rot * grad_rot
    for here in quarters(width):
        product = matmul(half[...], bases[0, :, here])
        square = jnp.sum(product * product, axis=0, keepdims=True) * (1.0 / width)
        value = (product * lax.rsqrt(square + NORM_EPS)).astype(HALF)
        start[:, here] = value
        start_turned[here] = value.T


def adam_kernel(where, bases, turned, mine, came, new, kept, sent):
    width = new.shape[0]
    rows = mine.shape[0]
    position, core = where[0], where[1]
    here, there = tile(position, rows), tile(1 - position, rows)
    moment_rot = (
        matmul(turned[:, here], mine[...]) + matmul(turned[:, there], came[...])
    ) * (1.0 / width)
    scaled = (moment_rot / (jnp.sqrt(new[...]) + EPSILON)).astype(HALF)
    sent[...] = matmul(bases[core, there], scaled).astype(HALF)
    kept[...] = matmul(bases[core, here], scaled).astype(HALF)


def write_part(core, side, block, part, left, right, sem):
    size = part.shape[0]
    here = slice(block * size, (block + 1) * size)
    for place, out in enumerate((left, right)):

        @pl.when((core ^ side) == place)
        def _():
            pltpu.make_async_copy(part, out.at[here], sem).start()

    return pltpu.make_async_copy(part, left.at[here], sem)


def update_kernel(
    where,
    kept,
    came,
    kept_next,
    came_next,
    back,
    low,
    top_next,
    left_in,
    right_in,
    out,
    left,
    right,
    rows_back,
    product,
    sem,
):
    rows, width = out.shape
    step = kept.shape[1]
    position, core = where[0], where[1]
    copies = [
        write_part(core, 0, 1, low, left, right, sem.at[0]),
        write_part(core, 1, 0, top_next, left, right, sem.at[1]),
    ]
    for value, place in (
        (kept, position * 2 + core),
        (came, (1 - position) * 2 + core),
        (kept_next, position * 2 + 1 - core),
        (came_next, (1 - position) * 2 + 1 - core),
    ):
        rows_back[:, tile(place, step)] = value[...]
    for i, here in enumerate(quarters(width)):
        product[:, here] = (matmul(rows_back[...], back[:, here]) * (1.0 / width)).astype(HALF)
        copies.append(pltpu.make_async_copy(product.at[:, here], out.at[:, here], sem.at[2 + i]))
        copies[-1].start()
    for copy in copies:
        copy.wait()


def next_side_kernel(where, low, left_in, right_in, left, right, sem):
    write_part(where[1], 1, 1, low, left, right, sem.at[0]).wait()


def quarters(width):
    step = width // 4
    return [slice(i * step, (i + 1) * step) for i in range(4)]


def improved(current, turned, kept, gram, result, result_turned):
    size, width = result.shape
    if size == width:
        for here in reversed(quarters(width)):
            product = matmul(current[: here.stop], turned[:, here]) * (1.0 / width)
            place_symmetric(gram, here, product.astype(HALF))
    else:
        for here in quarters(width):
            product = matmul(current[kept], turned[:, here]) * (1.0 / width)
            gram[:size, here] = product.astype(HALF)
    for here in quarters(width):
        value = (
            1.5 * current[kept, here].astype(FULL) - 0.5 * matmul(gram[:size], current[:, here])
        ).astype(result.dtype)
        result[:, here] = value
        if result_turned is not None:
            result_turned[here] = value.T


def refresh_kernel(
    where, start, start_turned, new, current, turned, out, second_new, gram, *scratch
):
    width = start.shape[0]
    rows = width // 2
    between, sem = scratch[:-1], scratch[-1]
    copy = pltpu.make_async_copy(new, second_new.at[:, tile(where[1], new.shape[1])], sem)
    copy.start()
    source, source_turned = start, start_turned
    for iteration in range(NS_ITERS - 1):
        if iteration + 2 == NS_ITERS:
            result, result_turned = current, turned
        else:
            result, result_turned = between[0].at[iteration % 2], between[1].at[iteration % 2]
        improved(source, source_turned, slice(0, width), gram, result, result_turned)
        source, source_turned = result, result_turned
    improved(current, turned, tile(where[0] * 2, rows // 2), gram, out, None)
    copy.wait()


def last_kernel(
    where, current, turned, top, new_next, second_in, out, left, right, second_new, gram, sem
):
    core = where[1]
    copies = [
        write_part(core, 0, 0, top, left, right, sem.at[0]),
        pltpu.make_async_copy(
            new_next, second_new.at[:, tile(1 - core, new_next.shape[1])], sem.at[1]
        ),
    ]
    copies[1].start()
    improved(current, turned, tile(where[0] * 2 + 1, out.shape[0]), gram, out, None)
    for copy in copies:
        copy.wait()


def fast_body(group_grads, moment, second, stat_left, stat_right, basis_left, basis_right):
    position = lax.axis_index("shard")
    member = lax.axis_index("dp")
    rows, width = moment.shape
    half = rows // 2
    quarter = rows // 4
    chunk = rows // 16
    core, x, z = member & 1, (member >> 1) & 1, member >> 2
    where = jnp.stack([position, core, x, z]).astype(jnp.int32)
    unit = 2 * width**3

    def dp_swap(value, distance):
        return lax.ppermute(value, "dp", [(i, i ^ distance) for i in range(16)])

    def shard_swap(value):
        return lax.ppermute(value, "shard", [(0, 1), (1, 0)])

    def cross_swap(value):
        pairs = [(i, i ^ 5) for i in range(32)]
        return lax.ppermute(value, ("dp", "shard"), pairs)

    raw = lax.dynamic_slice_in_dim(group_grads[0], (1 - core) * half, half, 0)
    came = dp_swap(raw, 1)
    raw = lax.dynamic_slice_in_dim(group_grads[0], core * half, half, 0)
    count = rows * width // quarter**2 + len(UPPER) + 1
    state_sent, kept, sent = call(
        start_kernel,
        [
            shaped((count, quarter, quarter), HALF),
            shaped((quarter, width), FULL),
            shaped((quarter, width), HALF),
        ],
        (where, raw, came, basis_left, basis_right, stat_left, stat_right),
        [SMEM] + [VMEM] * 2 + [ANY] * 4,
        [
            pltpu.VMEM((2, half, width), FULL),
            pltpu.VMEM((rows, rows), FULL),
            pltpu.SemaphoreType.DMA((3,)),
        ],
        moved=2**22,
        limit=50,
    )
    came = dp_swap(sent, 2)
    state_mine = shard_swap(state_sent)
    own, *sent = call(
        second_sum_kernel,
        [shaped((chunk, width), FULL)] + [shaped((chunk, width), HALF)] * 3,
        (where, kept, came),
        [SMEM] + [VMEM] * 2,
        moved=2**20,
    )
    pieces = [dp_swap(value, 4 * (k + 1)) for k, value in enumerate(sent)]
    (piece,) = call(
        third_sum_kernel,
        [shaped((chunk, width), HALF)],
        (own, *pieces),
        [VMEM] * 4,
        moved=2**19,
    )
    pieces = [piece] + [dp_swap(piece, 4 * k) for k in (1, 2, 3)]
    (part,) = call(
        joined_kernel,
        [shaped((quarter, width), HALF)],
        (where, *pieces),
        [SMEM] + [VMEM] * 4,
        moved=2**19,
    )
    part, state_mine = lax.optimization_barrier((part, state_mine))
    parts = [part, dp_swap(part, 2), shard_swap(part), cross_swap(part)]
    state_theirs = dp_swap(state_mine, 1)
    square = shaped((width, width), HALF)
    bases, left_turned, right_turned, stat = call(
        state_kernel,
        [shaped((2, width, width), HALF), square, square, shaped((width, width), FULL)],
        (
            where,
            basis_left,
            basis_right,
            state_mine,
            state_theirs,
            stat_left,
            stat_right,
        ),
        [SMEM] + [VMEM] * 4 + [ANY] * 2,
        [pltpu.SemaphoreType.DMA(())],
        moved=2**24,
    )
    near = parts[:2] + [dp_swap(value, 1) for value in parts[:2]]
    moment_mine, moment_sent = call(
        moment_kernel,
        [shaped((rows, half), HALF)] * 2,
        (where, moment, bases, *near),
        [SMEM] + [VMEM] * 6,
        [pltpu.VMEM((rows, width), HALF)],
        flops=unit // 4,
        moved=2**22,
    )
    moment_came = shard_swap(moment_sent)
    far = list(lax.optimization_barrier((parts[2], parts[3], bases)))[:2]
    far += [dp_swap(value, 1) for value in far]
    start, start_turned, new = call(
        statistic_kernel,
        [square, square, shaped((width, half), FULL)],
        (where, bases, left_turned, stat, second, *near, *far),
        [SMEM] + [VMEM] * 4 + [ANY] * 8,
        [
            pltpu.VMEM((2, width, width), HALF),
            pltpu.VMEM((width, width), HALF),
            pltpu.SemaphoreType.DMA((8,)),
        ],
        flops=3 * unit // 2,
        moved=2**23,
    )
    new_next = dp_swap(new, 1)
    start, moment_came = lax.optimization_barrier((start, moment_came))
    back_kept, back_sent = call(
        adam_kernel,
        [shaped((rows, half), HALF)] * 2,
        (where, bases, left_turned, moment_mine, moment_came, new),
        [SMEM] + [VMEM] * 5,
        flops=unit // 2,
        moved=2**22,
    )
    start, back_sent = lax.optimization_barrier((start, back_sent))
    back_came = shard_swap(back_sent)
    back_kept_next = dp_swap(back_kept, 1)
    current, current_turned, top, second_new = pl.pallas_call(
        refresh_kernel,
        out_shape=[square, square, shaped((half, width), FULL), shaped((width, rows), FULL)],
        in_specs=[SMEM] + [VMEM] * 2 + [ANY],
        out_specs=[VMEM] * 3 + [ANY],
        scratch_shapes=[pltpu.VMEM((width, width), HALF)]
        + [pltpu.VMEM((2, width, width), HALF)] * (2 if NS_ITERS > 2 else 0)
        + [pltpu.SemaphoreType.DMA(())],
        compiler_params=pltpu.CompilerParams(vmem_limit_bytes=24 * 2**20),
        cost_estimate=pl.CostEstimate(
            flops=6 * unit, bytes_accessed=2**23, transcendentals=0
        ),
    )(where, start, start_turned, new)
    top_next = dp_swap(top, 1)
    current, back_came, back_kept_next, new_next = lax.optimization_barrier(
        (current, back_came, back_kept_next, new_next)
    )
    back_came_next = dp_swap(back_came, 1)
    side = shaped((rows, width), FULL)
    low, left_new, right_new, second_new = pl.pallas_call(
        last_kernel,
        out_shape=[shaped((half, width), FULL), side, side, shaped((width, rows), FULL)],
        in_specs=[SMEM] + [VMEM] * 2 + [ANY] * 3,
        out_specs=[VMEM] + [ANY] * 3,
        scratch_shapes=[pltpu.VMEM((half, width), HALF), pltpu.SemaphoreType.DMA((2,))],
        input_output_aliases={5: 3},
        compiler_params=pltpu.CompilerParams(vmem_limit_bytes=24 * 2**20),
        cost_estimate=pl.CostEstimate(flops=unit // 2, bytes_accessed=2**22, transcendentals=0),
    )(where, current, current_turned, top, new_next, second_new)
    low, back_came_next = lax.optimization_barrier((low, back_came_next))
    low_next = dp_swap(low, 1)
    update, left_new, right_new = pl.pallas_call(
        update_kernel,
        out_shape=[shaped((rows, width), HALF), side, side],
        in_specs=[SMEM] + [VMEM] * 5 + [ANY] * 4,
        out_specs=[ANY] * 3,
        scratch_shapes=[pltpu.VMEM((rows, width), HALF)] * 2 + [pltpu.SemaphoreType.DMA((6,))],
        input_output_aliases={8: 1, 9: 2},
        compiler_params=pltpu.CompilerParams(vmem_limit_bytes=24 * 2**20),
        cost_estimate=pl.CostEstimate(flops=unit // 2, bytes_accessed=2**22, transcendentals=0),
    )(
        where,
        back_kept,
        back_came,
        back_kept_next,
        back_came_next,
        right_turned,
        low,
        top_next,
        left_new,
        right_new,
    )
    left_new, right_new = call(
        next_side_kernel,
        [side, side],
        (where, low_next, left_new, right_new),
        [SMEM] + [ANY] * 3,
        [pltpu.SemaphoreType.DMA((1,))],
        moved=2**21,
        space=ANY,
        aliases={2: 0, 3: 1},
    )
    return (update, second_new, left_new, right_new)


def make_plain_body(n_dp, n_shard):
    def swap(value, axis, distance):
        size = n_dp if axis == "dp" else n_shard
        return lax.ppermute(value, axis, [(i, i ^ distance) for i in range(size)])

    dp_bits = []
    bit = 1
    while bit < n_dp:
        dp_bits.append(bit)
        bit *= 2

    def ordered(first_is_low, own, other, dim):
        return jnp.where(
            first_is_low,
            jnp.concatenate([own, other], dim),
            jnp.concatenate([other, own], dim),
        )

    def body(group_grads, moment, second, stat_left, stat_right, basis_left, basis_right):
        position = lax.axis_index("shard")
        member = lax.axis_index("dp")
        rows, width = moment.shape
        core = member & 1
        half = rows // 2

        def near_columns(value):
            blocks = [
                lax.dynamic_slice_in_dim(value, (position ^ k) * rows, rows, 1)
                for k in range(n_shard)
            ]
            return jnp.concatenate(blocks, 1)

        def fetch(value, distance):
            size = value.shape[0] // 2
            part = lax.dynamic_slice_in_dim(value, core * size, size, 0)
            part = swap(part, "shard", distance)
            other = swap(part, "dp", 1)
            return ordered(core == 0, part, other, 0)

        left_own = basis_left.astype(jnp.bfloat16)
        right_own = basis_right.astype(jnp.bfloat16)
        left_rot = jnp.concatenate([left_own] + [fetch(left_own, k) for k in range(1, n_shard)], 0)
        right_rot = jnp.concatenate(
            [right_own] + [fetch(right_own, k) for k in range(1, n_shard)], 0
        )

        def whole_stat(stat):
            own = near_columns(stat)
            blocks = [own[:, b * rows : (b + 1) * rows] for b in range(n_shard)]
            bands = [own]
            for k in range(1, n_shard):
                others = [b for b in range(n_shard) if b != k]
                sent = jnp.concatenate([blocks[b] for b in others], 1).astype(jnp.bfloat16)
                came = fetch(sent, k).astype(jnp.float32)
                band = [None] * n_shard
                band[0] = blocks[k].T
                for place, b in enumerate(others):
                    band[k ^ b] = came[:, place * rows : (place + 1) * rows]
                bands.append(jnp.concatenate(band, 1))
            return jnp.concatenate(bands, 0)

        stat_left_full = whole_stat(stat_left)
        stat_right_full = whole_stat(stat_right)

        part = group_grads[0]
        for bit in dp_bits:
            size = part.shape[0] // 2
            high = (member & bit) // bit
            kept = lax.dynamic_slice_in_dim(part, high * size, size, 0)
            sent = lax.dynamic_slice_in_dim(part, (1 - high) * size, size, 0)
            part = kept.astype(jnp.float32) + swap(sent, "dp", bit).astype(jnp.float32)
        chunk = part.astype(jnp.bfloat16)[None]
        chunk = jnp.concatenate([chunk] + [swap(chunk, "shard", k) for k in range(1, n_shard)], 0)
        for bit in reversed(dp_bits):
            chunk = ordered((member & bit) == 0, chunk, swap(chunk, "dp", bit), 1)
        gradient = near_columns(chunk.reshape(width, width))

        grad_rows = gradient[:rows].astype(jnp.float32)
        moment_half = (
            BETA_ONE * near_columns(moment) + (1.0 - BETA_ONE) * grad_rows
        ).astype(jnp.bfloat16)
        near_rot = near_columns(right_rot)
        moment_turned = matmul(moment_half, near_rot).astype(jnp.bfloat16)
        moment_block = jnp.concatenate(
            [moment_turned[:, :rows]]
            + [
                swap(moment_turned[:, k * rows : (k + 1) * rows], "shard", k)
                for k in range(1, n_shard)
            ],
            0,
        )
        grad_block = matmul(gradient, near_rot[:, :rows]).astype(jnp.bfloat16)
        grad_rot = matmul(left_rot, grad_block, 0) / width
        moment_rot = matmul(left_rot, moment_block, 0) / width
        second_new = BETA_TWO * second + (1.0 - BETA_TWO) * grad_rot * grad_rot
        scaled = (moment_rot / (jnp.sqrt(second_new) + EPSILON)).astype(jnp.bfloat16)
        turned_back = matmul(left_rot, scaled).astype(jnp.bfloat16)
        back_rows = jnp.concatenate(
            [turned_back[:rows]]
            + [
                swap(turned_back[k * rows : (k + 1) * rows], "shard", k)
                for k in range(1, n_shard)
            ],
            1,
        )
        update = (near_columns(matmul(back_rows, near_rot, 1, 1)) / width).astype(jnp.bfloat16)

        def refreshed(stat, product_of_grads, rot):
            stat_new = BETA_STAT * stat + (1.0 - BETA_STAT) * product_of_grads
            product = matmul(stat_new.astype(jnp.bfloat16), rot)
            start = product / jnp.sqrt(jnp.sum(product * product, axis=0) / width + NORM_EPS)
            current = start.astype(jnp.bfloat16)
            for iteration in range(NS_ITERS):
                kept = width if iteration + 1 < NS_ITERS else rows
                gram = (matmul(current[:kept], current, 1, 1) / width).astype(jnp.bfloat16)
                result = 1.5 * current[:kept].astype(jnp.float32) - 0.5 * matmul(gram, current)
                current = result.astype(jnp.bfloat16)
            return result

        left_new = refreshed(stat_left_full, matmul(gradient, gradient, 1, 1), left_rot)
        right_new = refreshed(stat_right_full, matmul(gradient, gradient, 0, 0), right_rot)
        return (update, second_new, left_new, right_new)

    return body


def solution(mesh):
    n_dp, n_shard = mesh.shape["dp"], mesh.shape["shard"]
    body = fast_body if (n_dp, n_shard) == (16, 2) else make_plain_body(n_dp, n_shard)
    return jax.shard_map(
        body,
        mesh=mesh,
        in_specs=(
            P("dp", "shard", None),
            P("shard", None),
            P(None, "shard"),
            P("shard", None),
            P("shard", None),
            P("shard", None),
            P("shard", None),
        ),
        out_specs=(P("shard", None), P(None, "shard"), P("shard", None), P("shard", None)),
        check_vma=False,
    )
```

```python
import jax
import jax.numpy as jnp
from jax import lax
from jax.experimental import pallas as pl
from jax.experimental.pallas import tpu as pltpu
from jax.sharding import PartitionSpec as P

NS_ITERS = 2


BETA_ONE = 0.9
BETA_TWO = 0.9
BETA_STAT = 0.95
EPSILON = 1e-08
NORM_EPS = 1e-06
HALF = jnp.bfloat16
FULL = jnp.float32
VMEM = pl.BlockSpec(memory_space=pltpu.VMEM)
ANY = pl.BlockSpec(memory_space=pl.ANY)
SMEM = pl.BlockSpec(memory_space=pltpu.SMEM)


def matmul(left_mat, right_mat, left_dim=1, right_dim=0):
    return lax.dot_general(
        left_mat,
        right_mat,
        (((left_dim,), (right_dim,)), ((), ())),
        preferred_element_type=FULL,
    )


def shaped(shape, dtype):
    return jax.ShapeDtypeStruct(shape, dtype)


def tile(index, size):
    return pl.ds(pl.multiple_of(index * size, size), size)


def call(
    kernel, outs, operands, specs, scratch=(), flops=0, moved=0, limit=24, space=VMEM, aliases=None
):
    return pl.pallas_call(
        kernel,
        out_shape=outs,
        in_specs=specs,
        out_specs=[space] * len(outs),
        scratch_shapes=list(scratch),
        input_output_aliases=aliases or {},
        compiler_params=pltpu.CompilerParams(vmem_limit_bytes=limit * 2**20),
        cost_estimate=pl.CostEstimate(flops=flops, bytes_accessed=moved, transcendentals=0),
    )(*operands)


def run_all(copies):
    for copy in copies:
        copy.start()
    for copy in copies:
        copy.wait()


TILES = 4
UPPER = [(i, j) for i in range(TILES) for j in range(i, TILES)]
SPLIT = len(UPPER) // 2


def pack(out, base, value):
    size = out.shape[1]
    across = value.shape[1] // size
    for band in range(value.shape[0] // size):
        for column in range(across):
            out[base + band * across + column] = value[
                band * size : (band + 1) * size, column * size : (column + 1) * size
            ].astype(HALF)


def diagonal(size):
    shape = (size, size)
    return lax.broadcasted_iota(jnp.int32, shape, 0) == lax.broadcasted_iota(jnp.int32, shape, 1)


def start_kernel(
    where,
    raw,
    came,
    left,
    right,
    stat_left,
    stat_right,
    state,
    kept,
    sent,
    basis_in,
    stat_in,
    sem,
):
    position, core, x = where[0], where[1], where[2]
    half, width = basis_in.shape[1:]
    size = state.shape[1]
    copies = [
        pltpu.make_async_copy(basis.at[tile(core, half)], basis_in.at[i], sem.at[i])
        for i, basis in enumerate((left, right))
    ]
    for copy in copies:
        copy.start()
    for side, stat in enumerate((stat_left, stat_right)):

        @pl.when(core == side)
        def _():
            pltpu.make_async_copy(stat.at[:, tile(position, size * TILES)], stat_in, sem.at[2]).start()

    rows = kept.shape[0]
    for out, there in ((kept, tile(x, rows)), (sent, tile(1 - x, rows))):
        out[...] = (raw[there].astype(FULL) + came[there].astype(FULL)).astype(out.dtype)
    count = half * width // size**2
    for i, copy in enumerate(copies):
        copy.wait()
        pack(state, i * count, basis_in.at[i])
    pltpu.make_async_copy(stat_left.at[:, : size * TILES], stat_in, sem.at[2]).wait()
    same = diagonal(size)
    base = 2 * count

    def tile_of(i, j):
        return stat_in[i * size : (i + 1) * size, j * size : (j + 1) * size]

    @pl.when(x == 0)
    def _():
        for place in range(SPLIT + 1):
            state[base + place] = tile_of(*UPPER[place]).astype(HALF)

    @pl.when(x == 1)
    def _():
        for place in range(SPLIT, len(UPPER)):
            state[base + place - SPLIT] = tile_of(*UPPER[place]).astype(HALF)
        for i in range(TILES):
            value = tile_of(i, i)
            low = jnp.where(same, value - value.astype(HALF).astype(FULL), 0.0)
            line = jnp.sum(low, axis=0, keepdims=True)
            state[base + SPLIT, i * 16 : (i + 1) * 16] = jnp.broadcast_to(line, (16, size)).astype(
                HALF
            )


def second_sum_kernel(where, kept, came, own, *sent):
    size = own.shape[0]
    z = where[3]
    for k, out in enumerate((own, *sent)):
        there = tile(z ^ k, size)
        out[...] = (kept[there] + came[there].astype(FULL)).astype(out.dtype)


def third_sum_kernel(own, one, two, three, out):
    out[...] = (
        (own[...] + one[...].astype(FULL)) + (two[...].astype(FULL) + three[...].astype(FULL))
    ).astype(HALF)


def joined_kernel(where, *refs):
    out = refs[-1]
    z = where[3]
    size = refs[0].shape[0]
    for k, part in enumerate(refs[:-1]):
        out[tile(z ^ k, size)] = part[...]


def place_basis(where, out, own, mine, theirs, side):
    rows, width = own.shape
    half = rows // 2
    size = mine.shape[1]
    position, core = where[0], where[1]
    across = width // size
    base = side * half * width // size**2
    out[tile(position, rows)] = own[...].astype(HALF)
    other = (1 - position) * 2
    for part, block in ((mine, other + core), (theirs, other + 1 - core)):
        for band in range(half // size):
            here = tile(block * (half // size) + band, size)
            for column in range(across):
                out[here, column * size : (column + 1) * size] = part[base + band * across + column]


def state_kernel(
    where, left, right, mine, theirs, relayed, stat_left, stat_right, bases, turned, back, full, sem
):
    rows, width = left.shape
    size = rows // TILES
    position, core = where[0], where[1]
    here, there = tile(position, rows), tile(1 - position, rows)
    for side, stat in enumerate((stat_left, stat_right)):

        @pl.when(core == side)
        def _():
            pltpu.make_async_copy(stat, full.at[here], sem).start()

    place_basis(where, bases.at[core], left, mine, theirs, 0)
    place_basis(where, bases.at[1 - core], right, mine, theirs, 1)
    turned[...] = bases[core].T
    back[...] = bases[1 - core].T
    base = (1 - position) * TILES
    first = rows * width // size**2
    same = diagonal(size)
    near_x = where[2] == 0
    for number, (i, j) in enumerate(UPPER):
        if number < SPLIT:
            pair = mine[first + number], relayed[number]
        elif number == SPLIT:
            pair = mine[first + SPLIT], mine[first]
        else:
            pair = relayed[number - SPLIT], mine[first + number - SPLIT]
        value = jnp.where(near_x, pair[0].astype(FULL), pair[1].astype(FULL))
        if i == j:
            lines = slice(i * 16, (i + 1) * 16)
            line = jnp.where(
                near_x,
                relayed[SPLIT, lines].astype(FULL),
                mine[first + SPLIT, lines].astype(FULL),
            )[:1]
            value = value + jnp.where(same, line, 0.0)
        full[tile(base + i, size), tile(base + j, size)] = value
        if i != j:
            full[tile(base + j, size), tile(base + i, size)] = value.T
    pltpu.make_async_copy(stat_left, full.at[here], sem).wait()
    full[there, here] = full[here, there].T


def moment_kernel(where, moment, bases, own, over_x, next_own, next_over_x, ours, others, half):
    position, core, x = where[0], where[1], where[2]
    size = own.shape[0]
    step = ours.shape[1]
    for place, part in enumerate((own, over_x, next_own, next_over_x)):
        here = tile((core ^ (place // 2)) * 2 + (x ^ (place % 2)), size)
        half[here] = (
            BETA_ONE * moment[here] + (1.0 - BETA_ONE) * part[...].astype(FULL)
        ).astype(HALF)
    there, here = tile((1 - position) * 2 + core, step), tile(position * 2 + core, step)
    others[...] = matmul(half[...], bases[1 - core, :, there]).astype(HALF)
    ours[...] = matmul(half[...], bases[1 - core, :, here]).astype(HALF)


def place_symmetric(out, here, value):
    out[: here.stop, here] = value
    if here.start:
        out[here, : here.start] = value[: here.start].T


def statistic_kernel(where, bases, turned, stat, second, *refs):
    parts, (start, start_turned, new, pair, half, sem) = refs[:-6], refs[-6:]
    position, core, x = where[0], where[1], where[2]
    width = half.shape[0]
    step = new.shape[1]
    gradient = pair.at[core]
    copies = []
    for place, part in enumerate(parts):
        size = part.shape[0]
        block = (
            (position ^ (place // 4)) * 4 + (core ^ (place // 2 % 2)) * 2 + (x ^ (place % 2))
        )
        copies.append(pltpu.make_async_copy(part, gradient.at[tile(block, size)], sem.at[place]))
    run_all(copies)
    for here in quarters(width):
        pair[1 - core, :, here] = gradient[here].T
    block = matmul(gradient[...], bases[1 - core, :, tile(position * 2 + core, step)])
    for here in reversed(quarters(width)):
        above = slice(0, here.stop)
        grads = matmul(pair[0, above], pair[1, :, here])
        value = (BETA_STAT * stat[above, here] + (1.0 - BETA_STAT) * grads).astype(HALF)
        place_symmetric(half, here, value)
    grad_rot = matmul(turned[...], block.astype(HALF)) * (1.0 / width)
    new[...] = BETA_TWO * second[:, tile(core, step)] + (1.0 - BETA_TWO) * grad_rot * grad_rot
    for here in quarters(width):
        product = matmul(half[...], bases[0, :, here])
        square = jnp.sum(product * product, axis=0, keepdims=True) * (1.0 / width)
        value = (product * lax.rsqrt(square + NORM_EPS)).astype(HALF)
        start[:, here] = value
        start_turned[here] = value.T


def adam_kernel(where, bases, turned, mine, came, new, kept, sent):
    width = new.shape[0]
    rows = mine.shape[0]
    position, core = where[0], where[1]
    here, there = tile(position, rows), tile(1 - position, rows)
    moment_rot = (
        matmul(turned[:, here], mine[...]) + matmul(turned[:, there], came[...])
    ) * (1.0 / width)
    scaled = (moment_rot / (jnp.sqrt(new[...]) + EPSILON)).astype(HALF)
    sent[...] = matmul(bases[core, there], scaled).astype(HALF)
    kept[...] = matmul(bases[core, here], scaled).astype(HALF)


def write_part(core, side, block, part, left, right, sem):
    size = part.shape[0]
    here = slice(block * size, (block + 1) * size)
    for place, out in enumerate((left, right)):

        @pl.when((core ^ side) == place)
        def _():
            pltpu.make_async_copy(part, out.at[here], sem).start()

    return pltpu.make_async_copy(part, left.at[here], sem)


def update_kernel(
    where,
    kept,
    came,
    kept_next,
    came_next,
    back,
    low,
    top_next,
    left_in,
    right_in,
    out,
    left,
    right,
    rows_back,
    product,
    sem,
):
    rows, width = out.shape
    step = kept.shape[1]
    position, core = where[0], where[1]
    copies = [
        write_part(core, 0, 1, low, left, right, sem.at[0]),
        write_part(core, 1, 0, top_next, left, right, sem.at[1]),
    ]
    for value, place in (
        (kept, position * 2 + core),
        (came, (1 - position) * 2 + core),
        (kept_next, position * 2 + 1 - core),
        (came_next, (1 - position) * 2 + 1 - core),
    ):
        rows_back[:, tile(place, step)] = value[...]
    for i, here in enumerate(quarters(width)):
        product[:, here] = (matmul(rows_back[...], back[:, here]) * (1.0 / width)).astype(HALF)
        copies.append(pltpu.make_async_copy(product.at[:, here], out.at[:, here], sem.at[2 + i]))
        copies[-1].start()
    for copy in copies:
        copy.wait()


def next_side_kernel(where, low, left_in, right_in, left, right, sem):
    write_part(where[1], 1, 1, low, left, right, sem.at[0]).wait()


def quarters(width):
    step = width // 4
    return [slice(i * step, (i + 1) * step) for i in range(4)]


def improved(current, turned, kept, gram, result, result_turned):
    size, width = result.shape
    if size == width:
        for here in reversed(quarters(width)):
            product = matmul(current[: here.stop], turned[:, here]) * (1.0 / width)
            place_symmetric(gram, here, product.astype(HALF))
    else:
        for here in quarters(width):
            product = matmul(current[kept], turned[:, here]) * (1.0 / width)
            gram[:size, here] = product.astype(HALF)
    for here in quarters(width):
        value = (
            1.5 * current[kept, here].astype(FULL) - 0.5 * matmul(gram[:size], current[:, here])
        ).astype(result.dtype)
        result[:, here] = value
        if result_turned is not None:
            result_turned[here] = value.T


def refresh_kernel(
    where, start, start_turned, new, current, turned, out, second_new, gram, *scratch
):
    width = start.shape[0]
    rows = width // 2
    between, sem = scratch[:-1], scratch[-1]
    copy = pltpu.make_async_copy(new, second_new.at[:, tile(where[1], new.shape[1])], sem)
    copy.start()
    source, source_turned = start, start_turned
    for iteration in range(NS_ITERS - 1):
        if iteration + 2 == NS_ITERS:
            result, result_turned = current, turned
        else:
            result, result_turned = between[0].at[iteration % 2], between[1].at[iteration % 2]
        improved(source, source_turned, slice(0, width), gram, result, result_turned)
        source, source_turned = result, result_turned
    improved(current, turned, tile(where[0] * 2, rows // 2), gram, out, None)
    copy.wait()


def last_kernel(
    where, current, turned, top, new_next, second_in, out, left, right, second_new, gram, sem
):
    core = where[1]
    copies = [
        write_part(core, 0, 0, top, left, right, sem.at[0]),
        pltpu.make_async_copy(
            new_next, second_new.at[:, tile(1 - core, new_next.shape[1])], sem.at[1]
        ),
    ]
    copies[1].start()
    improved(current, turned, tile(where[0] * 2 + 1, out.shape[0]), gram, out, None)
    for copy in copies:
        copy.wait()


def fast_body(group_grads, moment, second, stat_left, stat_right, basis_left, basis_right):
    position = lax.axis_index("shard")
    member = lax.axis_index("dp")
    rows, width = moment.shape
    half = rows // 2
    quarter = rows // 4
    chunk = rows // 16
    core, x, z = member & 1, (member >> 1) & 1, member >> 2
    where = jnp.stack([position, core, x, z]).astype(jnp.int32)
    unit = 2 * width**3

    def dp_swap(value, distance):
        return lax.ppermute(value, "dp", [(i, i ^ distance) for i in range(16)])

    def shard_swap(value):
        return lax.ppermute(value, "shard", [(0, 1), (1, 0)])

    def cross_swap(value):
        pairs = [(i, i ^ 5) for i in range(32)]
        return lax.ppermute(value, ("dp", "shard"), pairs)

    raw = lax.dynamic_slice_in_dim(group_grads[0], (1 - core) * half, half, 0)
    came = dp_swap(raw, 1)
    raw = lax.dynamic_slice_in_dim(group_grads[0], core * half, half, 0)
    tiles = rows * width // quarter**2
    count = tiles + SPLIT + 1
    state_sent, kept, sent = call(
        start_kernel,
        [
            shaped((count, quarter, quarter), HALF),
            shaped((quarter, width), FULL),
            shaped((quarter, width), HALF),
        ],
        (where, raw, came, basis_left, basis_right, stat_left, stat_right),
        [SMEM] + [VMEM] * 2 + [ANY] * 4,
        [
            pltpu.VMEM((2, half, width), FULL),
            pltpu.VMEM((rows, rows), FULL),
            pltpu.SemaphoreType.DMA((3,)),
        ],
        moved=2**22,
        limit=50,
    )
    came = dp_swap(sent, 2)
    state_mine = shard_swap(state_sent)
    own, *sent = call(
        second_sum_kernel,
        [shaped((chunk, width), FULL)] + [shaped((chunk, width), HALF)] * 3,
        (where, kept, came),
        [SMEM] + [VMEM] * 2,
        moved=2**20,
    )
    pieces = [dp_swap(value, 4 * (k + 1)) for k, value in enumerate(sent)]
    (piece,) = call(
        third_sum_kernel,
        [shaped((chunk, width), HALF)],
        (own, *pieces),
        [VMEM] * 4,
        moved=2**19,
    )
    pieces = [piece] + [dp_swap(piece, 4 * k) for k in (1, 2, 3)]
    (part,) = call(
        joined_kernel,
        [shaped((quarter, width), HALF)],
        (where, *pieces),
        [SMEM] + [VMEM] * 4,
        moved=2**19,
    )
    part, state_mine = lax.optimization_barrier((part, state_mine))
    parts = [part, dp_swap(part, 2), shard_swap(part), cross_swap(part)]
    state_theirs = dp_swap(state_mine, 1)
    state_relayed = dp_swap(state_mine[tiles:], 2)
    square = shaped((width, width), HALF)
    bases, left_turned, right_turned, stat = call(
        state_kernel,
        [shaped((2, width, width), HALF), square, square, shaped((width, width), FULL)],
        (
            where,
            basis_left,
            basis_right,
            state_mine,
            state_theirs,
            state_relayed,
            stat_left,
            stat_right,
        ),
        [SMEM] + [VMEM] * 5 + [ANY] * 2,
        [pltpu.SemaphoreType.DMA(())],
        moved=2**24,
    )
    near = parts[:2] + [dp_swap(value, 1) for value in parts[:2]]
    moment_mine, moment_sent = call(
        moment_kernel,
        [shaped((rows, half), HALF)] * 2,
        (where, moment, bases, *near),
        [SMEM] + [VMEM] * 6,
        [pltpu.VMEM((rows, width), HALF)],
        flops=unit // 4,
        moved=2**22,
    )
    moment_came = shard_swap(moment_sent)
    far = list(lax.optimization_barrier((parts[2], parts[3], bases)))[:2]
    far += [dp_swap(value, 1) for value in far]
    start, start_turned, new = call(
        statistic_kernel,
        [square, square, shaped((width, half), FULL)],
        (where, bases, left_turned, stat, second, *near, *far),
        [SMEM] + [VMEM] * 4 + [ANY] * 8,
        [
            pltpu.VMEM((2, width, width), HALF),
            pltpu.VMEM((width, width), HALF),
            pltpu.SemaphoreType.DMA((8,)),
        ],
        flops=3 * unit // 2,
        moved=2**23,
    )
    new_next = dp_swap(new, 1)
    start, moment_came = lax.optimization_barrier((start, moment_came))
    back_kept, back_sent = call(
        adam_kernel,
        [shaped((rows, half), HALF)] * 2,
        (where, bases, left_turned, moment_mine, moment_came, new),
        [SMEM] + [VMEM] * 5,
        flops=unit // 2,
        moved=2**22,
    )
    start, back_sent = lax.optimization_barrier((start, back_sent))
    back_came = shard_swap(back_sent)
    back_kept_next = dp_swap(back_kept, 1)
    current, current_turned, top, second_new = pl.pallas_call(
        refresh_kernel,
        out_shape=[square, square, shaped((half, width), FULL), shaped((width, rows), FULL)],
        in_specs=[SMEM] + [VMEM] * 2 + [ANY],
        out_specs=[VMEM] * 3 + [ANY],
        scratch_shapes=[pltpu.VMEM((width, width), HALF)]
        + [pltpu.VMEM((2, width, width), HALF)] * (2 if NS_ITERS > 2 else 0)
        + [pltpu.SemaphoreType.DMA(())],
        compiler_params=pltpu.CompilerParams(vmem_limit_bytes=24 * 2**20),
        cost_estimate=pl.CostEstimate(
            flops=6 * unit, bytes_accessed=2**23, transcendentals=0
        ),
    )(where, start, start_turned, new)
    top_next = dp_swap(top, 1)
    current, back_came, back_kept_next, new_next = lax.optimization_barrier(
        (current, back_came, back_kept_next, new_next)
    )
    back_came_next = dp_swap(back_came, 1)
    side = shaped((rows, width), FULL)
    low, left_new, right_new, second_new = pl.pallas_call(
        last_kernel,
        out_shape=[shaped((half, width), FULL), side, side, shaped((width, rows), FULL)],
        in_specs=[SMEM] + [VMEM] * 2 + [ANY] * 3,
        out_specs=[VMEM] + [ANY] * 3,
        scratch_shapes=[pltpu.VMEM((half, width), HALF), pltpu.SemaphoreType.DMA((2,))],
        input_output_aliases={5: 3},
        compiler_params=pltpu.CompilerParams(vmem_limit_bytes=24 * 2**20),
        cost_estimate=pl.CostEstimate(flops=unit // 2, bytes_accessed=2**22, transcendentals=0),
    )(where, current, current_turned, top, new_next, second_new)
    low, back_came_next = lax.optimization_barrier((low, back_came_next))
    low_next = dp_swap(low, 1)
    update, left_new, right_new = pl.pallas_call(
        update_kernel,
        out_shape=[shaped((rows, width), HALF), side, side],
        in_specs=[SMEM] + [VMEM] * 5 + [ANY] * 4,
        out_specs=[ANY] * 3,
        scratch_shapes=[pltpu.VMEM((rows, width), HALF)] * 2 + [pltpu.SemaphoreType.DMA((6,))],
        input_output_aliases={8: 1, 9: 2},
        compiler_params=pltpu.CompilerParams(vmem_limit_bytes=24 * 2**20),
        cost_estimate=pl.CostEstimate(flops=unit // 2, bytes_accessed=2**22, transcendentals=0),
    )(
        where,
        back_kept,
        back_came,
        back_kept_next,
        back_came_next,
        right_turned,
        low,
        top_next,
        left_new,
        right_new,
    )
    left_new, right_new = call(
        next_side_kernel,
        [side, side],
        (where, low_next, left_new, right_new),
        [SMEM] + [ANY] * 3,
        [pltpu.SemaphoreType.DMA((1,))],
        moved=2**21,
        space=ANY,
        aliases={2: 0, 3: 1},
    )
    return (update, second_new, left_new, right_new)


def make_plain_body(n_dp, n_shard):
    def swap(value, axis, distance):
        size = n_dp if axis == "dp" else n_shard
        return lax.ppermute(value, axis, [(i, i ^ distance) for i in range(size)])

    dp_bits = []
    bit = 1
    while bit < n_dp:
        dp_bits.append(bit)
        bit *= 2

    def ordered(first_is_low, own, other, dim):
        return jnp.where(
            first_is_low,
            jnp.concatenate([own, other], dim),
            jnp.concatenate([other, own], dim),
        )

    def body(group_grads, moment, second, stat_left, stat_right, basis_left, basis_right):
        position = lax.axis_index("shard")
        member = lax.axis_index("dp")
        rows, width = moment.shape
        core = member & 1
        half = rows // 2

        def near_columns(value):
            blocks = [
                lax.dynamic_slice_in_dim(value, (position ^ k) * rows, rows, 1)
                for k in range(n_shard)
            ]
            return jnp.concatenate(blocks, 1)

        def fetch(value, distance):
            size = value.shape[0] // 2
            part = lax.dynamic_slice_in_dim(value, core * size, size, 0)
            part = swap(part, "shard", distance)
            other = swap(part, "dp", 1)
            return ordered(core == 0, part, other, 0)

        left_own = basis_left.astype(jnp.bfloat16)
        right_own = basis_right.astype(jnp.bfloat16)
        left_rot = jnp.concatenate([left_own] + [fetch(left_own, k) for k in range(1, n_shard)], 0)
        right_rot = jnp.concatenate(
            [right_own] + [fetch(right_own, k) for k in range(1, n_shard)], 0
        )

        def whole_stat(stat):
            own = near_columns(stat)
            blocks = [own[:, b * rows : (b + 1) * rows] for b in range(n_shard)]
            bands = [own]
            for k in range(1, n_shard):
                others = [b for b in range(n_shard) if b != k]
                sent = jnp.concatenate([blocks[b] for b in others], 1).astype(jnp.bfloat16)
                came = fetch(sent, k).astype(jnp.float32)
                band = [None] * n_shard
                band[0] = blocks[k].T
                for place, b in enumerate(others):
                    band[k ^ b] = came[:, place * rows : (place + 1) * rows]
                bands.append(jnp.concatenate(band, 1))
            return jnp.concatenate(bands, 0)

        stat_left_full = whole_stat(stat_left)
        stat_right_full = whole_stat(stat_right)

        part = group_grads[0]
        for bit in dp_bits:
            size = part.shape[0] // 2
            high = (member & bit) // bit
            kept = lax.dynamic_slice_in_dim(part, high * size, size, 0)
            sent = lax.dynamic_slice_in_dim(part, (1 - high) * size, size, 0)
            part = kept.astype(jnp.float32) + swap(sent, "dp", bit).astype(jnp.float32)
        chunk = part.astype(jnp.bfloat16)[None]
        chunk = jnp.concatenate([chunk] + [swap(chunk, "shard", k) for k in range(1, n_shard)], 0)
        for bit in reversed(dp_bits):
            chunk = ordered((member & bit) == 0, chunk, swap(chunk, "dp", bit), 1)
        gradient = near_columns(chunk.reshape(width, width))

        grad_rows = gradient[:rows].astype(jnp.float32)
        moment_half = (
            BETA_ONE * near_columns(moment) + (1.0 - BETA_ONE) * grad_rows
        ).astype(jnp.bfloat16)
        near_rot = near_columns(right_rot)
        moment_turned = matmul(moment_half, near_rot).astype(jnp.bfloat16)
        moment_block = jnp.concatenate(
            [moment_turned[:, :rows]]
            + [
                swap(moment_turned[:, k * rows : (k + 1) * rows], "shard", k)
                for k in range(1, n_shard)
            ],
            0,
        )
        grad_block = matmul(gradient, near_rot[:, :rows]).astype(jnp.bfloat16)
        grad_rot = matmul(left_rot, grad_block, 0) / width
        moment_rot = matmul(left_rot, moment_block, 0) / width
        second_new = BETA_TWO * second + (1.0 - BETA_TWO) * grad_rot * grad_rot
        scaled = (moment_rot / (jnp.sqrt(second_new) + EPSILON)).astype(jnp.bfloat16)
        turned_back = matmul(left_rot, scaled).astype(jnp.bfloat16)
        back_rows = jnp.concatenate(
            [turned_back[:rows]]
            + [
                swap(turned_back[k * rows : (k + 1) * rows], "shard", k)
                for k in range(1, n_shard)
            ],
            1,
        )
        update = (near_columns(matmul(back_rows, near_rot, 1, 1)) / width).astype(jnp.bfloat16)

        def refreshed(stat, product_of_grads, rot):
            stat_new = BETA_STAT * stat + (1.0 - BETA_STAT) * product_of_grads
            product = matmul(stat_new.astype(jnp.bfloat16), rot)
            start = product / jnp.sqrt(jnp.sum(product * product, axis=0) / width + NORM_EPS)
            current = start.astype(jnp.bfloat16)
            for iteration in range(NS_ITERS):
                kept = width if iteration + 1 < NS_ITERS else rows
                gram = (matmul(current[:kept], current, 1, 1) / width).astype(jnp.bfloat16)
                result = 1.5 * current[:kept].astype(jnp.float32) - 0.5 * matmul(gram, current)
                current = result.astype(jnp.bfloat16)
            return result

        left_new = refreshed(stat_left_full, matmul(gradient, gradient, 1, 1), left_rot)
        right_new = refreshed(stat_right_full, matmul(gradient, gradient, 0, 0), right_rot)
        return (update, second_new, left_new, right_new)

    return body


def solution(mesh):
    n_dp, n_shard = mesh.shape["dp"], mesh.shape["shard"]
    body = fast_body if (n_dp, n_shard) == (16, 2) else make_plain_body(n_dp, n_shard)
    return jax.shard_map(
        body,
        mesh=mesh,
        in_specs=(
            P("dp", "shard", None),
            P("shard", None),
            P(None, "shard"),
            P("shard", None),
            P("shard", None),
            P("shard", None),
            P("shard", None),
        ),
        out_specs=(P("shard", None), P(None, "shard"), P("shard", None), P("shard", None)),
        check_vma=False,
    )
```

```python
import jax
import jax.numpy as jnp
from jax import lax
from jax.experimental import pallas as pl
from jax.experimental.pallas import tpu as pltpu
from jax.sharding import PartitionSpec as P

NS_ITERS = 2


BETA_ONE = 0.9
BETA_TWO = 0.9
BETA_STAT = 0.95
EPSILON = 1e-08
NORM_EPS = 1e-06
HALF = jnp.bfloat16
FULL = jnp.float32
VMEM = pl.BlockSpec(memory_space=pltpu.VMEM)
ANY = pl.BlockSpec(memory_space=pl.ANY)
SMEM = pl.BlockSpec(memory_space=pltpu.SMEM)


def matmul(left_mat, right_mat, left_dim=1, right_dim=0):
    return lax.dot_general(
        left_mat,
        right_mat,
        (((left_dim,), (right_dim,)), ((), ())),
        preferred_element_type=FULL,
    )


def shaped(shape, dtype):
    return jax.ShapeDtypeStruct(shape, dtype)


def tile(index, size):
    return pl.ds(pl.multiple_of(index * size, size), size)


def call(
    kernel, outs, operands, specs, scratch=(), flops=0, moved=0, limit=24, space=VMEM, aliases=None
):
    return pl.pallas_call(
        kernel,
        out_shape=outs,
        in_specs=specs,
        out_specs=[space] * len(outs),
        scratch_shapes=list(scratch),
        input_output_aliases=aliases or {},
        compiler_params=pltpu.CompilerParams(vmem_limit_bytes=limit * 2**20),
        cost_estimate=pl.CostEstimate(flops=flops, bytes_accessed=moved, transcendentals=0),
    )(*operands)


def run_all(copies):
    for copy in copies:
        copy.start()
    for copy in copies:
        copy.wait()


TILES = 4
UPPER = [(i, j) for i in range(TILES) for j in range(i, TILES)]
SPLIT = len(UPPER) // 2


def pack(out, base, value):
    size = out.shape[1]
    across = value.shape[1] // size
    for band in range(value.shape[0] // size):
        for column in range(across):
            out[base + band * across + column] = value[
                band * size : (band + 1) * size, column * size : (column + 1) * size
            ].astype(HALF)


def diagonal(size):
    shape = (size, size)
    return lax.broadcasted_iota(jnp.int32, shape, 0) == lax.broadcasted_iota(jnp.int32, shape, 1)


def start_kernel(
    where,
    raw,
    came,
    left,
    right,
    stat_left,
    stat_right,
    state,
    kept,
    sent,
    basis_in,
    stat_in,
    sem,
):
    position, core, x, z = where[0], where[1], where[2], where[3]
    half, width = basis_in.shape[1:]
    size = state.shape[1]
    copies = [
        pltpu.make_async_copy(basis.at[tile(core, half)], basis_in.at[i], sem.at[i])
        for i, basis in enumerate((left, right))
    ]
    for copy in copies:
        copy.start()
    for side, stat in enumerate((stat_left, stat_right)):

        @pl.when(core == side)
        def _():
            pltpu.make_async_copy(stat.at[:, tile(position, size * TILES)], stat_in, sem.at[2]).start()

    rows = kept.shape[0]
    for out, there in ((kept, tile(x, rows)), (sent, tile(1 - x, rows))):
        out[...] = (raw[there].astype(FULL) + came[there].astype(FULL)).astype(out.dtype)
    count = half * width // size**2
    for i, copy in enumerate(copies):
        copy.wait()
        pack(state, i * count, basis_in.at[i])
    pltpu.make_async_copy(stat_left.at[:, : size * TILES], stat_in, sem.at[2]).wait()
    same = diagonal(size)
    base = 2 * count

    def tile_of(i, j):
        return stat_in[i * size : (i + 1) * size, j * size : (j + 1) * size]

    @pl.when(z % 2 == 0)
    def _():
        for place in range(SPLIT + 1):
            state[base + place] = tile_of(*UPPER[place]).astype(HALF)

    @pl.when(z % 2 == 1)
    def _():
        for place in range(SPLIT, len(UPPER)):
            state[base + place - SPLIT] = tile_of(*UPPER[place]).astype(HALF)
        for i in range(TILES):
            value = tile_of(i, i)
            low = jnp.where(same, value - value.astype(HALF).astype(FULL), 0.0)
            line = jnp.sum(low, axis=0, keepdims=True)
            state[base + SPLIT, i * 16 : (i + 1) * 16] = jnp.broadcast_to(line, (16, size)).astype(
                HALF
            )


def second_sum_kernel(where, kept, came, own, *sent):
    size = own.shape[0]
    z = where[3]
    for k, out in enumerate((own, *sent)):
        there = tile(z ^ k, size)
        out[...] = (kept[there] + came[there].astype(FULL)).astype(out.dtype)


def third_sum_kernel(own, one, two, three, out):
    out[...] = (
        (own[...] + one[...].astype(FULL)) + (two[...].astype(FULL) + three[...].astype(FULL))
    ).astype(HALF)


def joined_kernel(where, *refs):
    out = refs[-1]
    z = where[3]
    size = refs[0].shape[0]
    for k, part in enumerate(refs[:-1]):
        out[tile(z ^ k, size)] = part[...]


def place_basis(where, out, own, mine, theirs, side):
    rows, width = own.shape
    half = rows // 2
    size = mine.shape[1]
    position, core = where[0], where[1]
    across = width // size
    base = side * half * width // size**2
    out[tile(position, rows)] = own[...].astype(HALF)
    other = (1 - position) * 2
    for part, block in ((mine, other + core), (theirs, other + 1 - core)):
        for band in range(half // size):
            here = tile(block * (half // size) + band, size)
            for column in range(across):
                out[here, column * size : (column + 1) * size] = part[base + band * across + column]


def state_kernel(
    where, left, right, mine, theirs, relayed, stat_left, stat_right, bases, turned, back, full, sem
):
    rows, width = left.shape
    size = rows // TILES
    position, core = where[0], where[1]
    here, there = tile(position, rows), tile(1 - position, rows)
    for side, stat in enumerate((stat_left, stat_right)):

        @pl.when(core == side)
        def _():
            pltpu.make_async_copy(stat, full.at[here], sem).start()

    place_basis(where, bases.at[core], left, mine, theirs, 0)
    place_basis(where, bases.at[1 - core], right, mine, theirs, 1)
    turned[...] = bases[core].T
    back[...] = bases[1 - core].T
    base = (1 - position) * TILES
    first = rows * width // size**2
    same = diagonal(size)
    even = where[3] % 2 == 0
    for number, (i, j) in enumerate(UPPER):
        if number < SPLIT:
            pair = mine[first + number], relayed[number]
        elif number == SPLIT:
            pair = mine[first + SPLIT], mine[first]
        else:
            pair = relayed[number - SPLIT], mine[first + number - SPLIT]
        value = jnp.where(even, pair[0].astype(FULL), pair[1].astype(FULL))
        if i == j:
            lines = slice(i * 16, (i + 1) * 16)
            line = jnp.where(
                even,
                relayed[SPLIT, lines].astype(FULL),
                mine[first + SPLIT, lines].astype(FULL),
            )[:1]
            value = value + jnp.where(same, line, 0.0)
        full[tile(base + i, size), tile(base + j, size)] = value
        if i != j:
            full[tile(base + j, size), tile(base + i, size)] = value.T
    pltpu.make_async_copy(stat_left, full.at[here], sem).wait()
    full[there, here] = full[here, there].T


def moment_kernel(where, moment, bases, own, over_x, next_own, next_over_x, ours, others, half):
    position, core, x = where[0], where[1], where[2]
    size = own.shape[0]
    step = ours.shape[1]
    for place, part in enumerate((own, over_x, next_own, next_over_x)):
        here = tile((core ^ (place // 2)) * 2 + (x ^ (place % 2)), size)
        half[here] = (
            BETA_ONE * moment[here] + (1.0 - BETA_ONE) * part[...].astype(FULL)
        ).astype(HALF)
    there, here = tile((1 - position) * 2 + core, step), tile(position * 2 + core, step)
    others[...] = matmul(half[...], bases[1 - core, :, there]).astype(HALF)
    ours[...] = matmul(half[...], bases[1 - core, :, here]).astype(HALF)


def place_symmetric(out, here, value):
    out[: here.stop, here] = value
    if here.start:
        out[here, : here.start] = value[: here.start].T


def statistic_kernel(where, bases, turned, stat, second, *refs):
    parts, (start, start_turned, new, pair, half, sem) = refs[:-6], refs[-6:]
    position, core, x = where[0], where[1], where[2]
    width = half.shape[0]
    step = new.shape[1]
    gradient = pair.at[core]
    copies = []
    for place, part in enumerate(parts):
        size = part.shape[0]
        block = (
            (position ^ (place // 4)) * 4 + (core ^ (place // 2 % 2)) * 2 + (x ^ (place % 2))
        )
        copies.append(pltpu.make_async_copy(part, gradient.at[tile(block, size)], sem.at[place]))
    run_all(copies)
    for here in quarters(width):
        pair[1 - core, :, here] = gradient[here].T
    block = matmul(gradient[...], bases[1 - core, :, tile(position * 2 + core, step)])
    for here in reversed(quarters(width)):
        above = slice(0, here.stop)
        grads = matmul(pair[0, above], pair[1, :, here])
        value = (BETA_STAT * stat[above, here] + (1.0 - BETA_STAT) * grads).astype(HALF)
        place_symmetric(half, here, value)
    grad_rot = matmul(turned[...], block.astype(HALF)) * (1.0 / width)
    new[...] = BETA_TWO * second[:, tile(core, step)] + (1.0 - BETA_TWO) * grad_rot * grad_rot
    for here in quarters(width):
        product = matmul(half[...], bases[0, :, here])
        square = jnp.sum(product * product, axis=0, keepdims=True) * (1.0 / width)
        value = (product * lax.rsqrt(square + NORM_EPS)).astype(HALF)
        start[:, here] = value
        start_turned[here] = value.T


def adam_kernel(where, bases, turned, mine, came, new, kept, sent):
    width = new.shape[0]
    rows = mine.shape[0]
    position, core = where[0], where[1]
    here, there = tile(position, rows), tile(1 - position, rows)
    moment_rot = (
        matmul(turned[:, here], mine[...]) + matmul(turned[:, there], came[...])
    ) * (1.0 / width)
    scaled = (moment_rot / (jnp.sqrt(new[...]) + EPSILON)).astype(HALF)
    sent[...] = matmul(bases[core, there], scaled).astype(HALF)
    kept[...] = matmul(bases[core, here], scaled).astype(HALF)


def write_part(core, side, block, part, left, right, sem):
    size = part.shape[0]
    here = slice(block * size, (block + 1) * size)
    for place, out in enumerate((left, right)):

        @pl.when((core ^ side) == place)
        def _():
            pltpu.make_async_copy(part, out.at[here], sem).start()

    return pltpu.make_async_copy(part, left.at[here], sem)


def update_kernel(
    where,
    kept,
    came,
    kept_next,
    came_next,
    back,
    low,
    top_next,
    left_in,
    right_in,
    out,
    left,
    right,
    rows_back,
    product,
    sem,
):
    rows, width = out.shape
    step = kept.shape[1]
    position, core = where[0], where[1]
    copies = [
        write_part(core, 0, 1, low, left, right, sem.at[0]),
        write_part(core, 1, 0, top_next, left, right, sem.at[1]),
    ]
    for value, place in (
        (kept, position * 2 + core),
        (came, (1 - position) * 2 + core),
        (kept_next, position * 2 + 1 - core),
        (came_next, (1 - position) * 2 + 1 - core),
    ):
        rows_back[:, tile(place, step)] = value[...]
    for i, here in enumerate(quarters(width)):
        product[:, here] = (matmul(rows_back[...], back[:, here]) * (1.0 / width)).astype(HALF)
        copies.append(pltpu.make_async_copy(product.at[:, here], out.at[:, here], sem.at[2 + i]))
        copies[-1].start()
    for copy in copies:
        copy.wait()


def next_side_kernel(where, low, left_in, right_in, left, right, sem):
    write_part(where[1], 1, 1, low, left, right, sem.at[0]).wait()


def quarters(width):
    step = width // 4
    return [slice(i * step, (i + 1) * step) for i in range(4)]


def improved(current, turned, kept, gram, result, result_turned):
    size, width = result.shape
    if size == width:
        for here in reversed(quarters(width)):
            product = matmul(current[: here.stop], turned[:, here]) * (1.0 / width)
            place_symmetric(gram, here, product.astype(HALF))
    else:
        for here in quarters(width):
            product = matmul(current[kept], turned[:, here]) * (1.0 / width)
            gram[:size, here] = product.astype(HALF)
    for here in quarters(width):
        value = (
            1.5 * current[kept, here].astype(FULL) - 0.5 * matmul(gram[:size], current[:, here])
        ).astype(result.dtype)
        result[:, here] = value
        if result_turned is not None:
            result_turned[here] = value.T


def refresh_kernel(
    where, start, start_turned, new, current, turned, out, second_new, gram, *scratch
):
    width = start.shape[0]
    rows = width // 2
    between, sem = scratch[:-1], scratch[-1]
    copy = pltpu.make_async_copy(new, second_new.at[:, tile(where[1], new.shape[1])], sem)
    copy.start()
    source, source_turned = start, start_turned
    for iteration in range(NS_ITERS - 1):
        if iteration + 2 == NS_ITERS:
            result, result_turned = current, turned
        else:
            result, result_turned = between[0].at[iteration % 2], between[1].at[iteration % 2]
        improved(source, source_turned, slice(0, width), gram, result, result_turned)
        source, source_turned = result, result_turned
    improved(current, turned, tile(where[0] * 2, rows // 2), gram, out, None)
    copy.wait()


def last_kernel(
    where, current, turned, top, new_next, second_in, out, left, right, second_new, gram, sem
):
    core = where[1]
    copies = [
        write_part(core, 0, 0, top, left, right, sem.at[0]),
        pltpu.make_async_copy(
            new_next, second_new.at[:, tile(1 - core, new_next.shape[1])], sem.at[1]
        ),
    ]
    copies[1].start()
    improved(current, turned, tile(where[0] * 2 + 1, out.shape[0]), gram, out, None)
    for copy in copies:
        copy.wait()


def fast_body(group_grads, moment, second, stat_left, stat_right, basis_left, basis_right):
    position = lax.axis_index("shard")
    member = lax.axis_index("dp")
    rows, width = moment.shape
    half = rows // 2
    quarter = rows // 4
    chunk = rows // 16
    core, x, z = member & 1, (member >> 1) & 1, member >> 2
    where = jnp.stack([position, core, x, z]).astype(jnp.int32)
    unit = 2 * width**3

    def dp_swap(value, distance):
        return lax.ppermute(value, "dp", [(i, i ^ distance) for i in range(16)])

    def shard_swap(value):
        return lax.ppermute(value, "shard", [(0, 1), (1, 0)])

    def cross_swap(value):
        pairs = [(i, i ^ 5) for i in range(32)]
        return lax.ppermute(value, ("dp", "shard"), pairs)

    raw = lax.dynamic_slice_in_dim(group_grads[0], (1 - core) * half, half, 0)
    came = dp_swap(raw, 1)
    raw = lax.dynamic_slice_in_dim(group_grads[0], core * half, half, 0)
    tiles = rows * width // quarter**2
    count = tiles + SPLIT + 1
    state_sent, kept, sent = call(
        start_kernel,
        [
            shaped((count, quarter, quarter), HALF),
            shaped((quarter, width), FULL),
            shaped((quarter, width), HALF),
        ],
        (where, raw, came, basis_left, basis_right, stat_left, stat_right),
        [SMEM] + [VMEM] * 2 + [ANY] * 4,
        [
            pltpu.VMEM((2, half, width), FULL),
            pltpu.VMEM((rows, rows), FULL),
            pltpu.SemaphoreType.DMA((3,)),
        ],
        moved=2**22,
        limit=50,
    )
    came = dp_swap(sent, 2)
    state_mine = shard_swap(state_sent)
    own, *sent = call(
        second_sum_kernel,
        [shaped((chunk, width), FULL)] + [shaped((chunk, width), HALF)] * 3,
        (where, kept, came),
        [SMEM] + [VMEM] * 2,
        moved=2**20,
    )
    pieces = [dp_swap(value, 4 * (k + 1)) for k, value in enumerate(sent)]
    (piece,) = call(
        third_sum_kernel,
        [shaped((chunk, width), HALF)],
        (own, *pieces),
        [VMEM] * 4,
        moved=2**19,
    )
    pieces = [piece] + [dp_swap(piece, 4 * k) for k in (1, 2, 3)]
    (part,) = call(
        joined_kernel,
        [shaped((quarter, width), HALF)],
        (where, *pieces),
        [SMEM] + [VMEM] * 4,
        moved=2**19,
    )
    part, state_mine = lax.optimization_barrier((part, state_mine))
    parts = [part, dp_swap(part, 2), shard_swap(part), cross_swap(part)]
    state_theirs = dp_swap(state_mine, 1)
    state_relayed = dp_swap(state_mine[tiles:], 4)
    square = shaped((width, width), HALF)
    bases, left_turned, right_turned, stat = call(
        state_kernel,
        [shaped((2, width, width), HALF), square, square, shaped((width, width), FULL)],
        (
            where,
            basis_left,
            basis_right,
            state_mine,
            state_theirs,
            state_relayed,
            stat_left,
            stat_right,
        ),
        [SMEM] + [VMEM] * 5 + [ANY] * 2,
        [pltpu.SemaphoreType.DMA(())],
        moved=2**24,
    )
    near = parts[:2] + [dp_swap(value, 1) for value in parts[:2]]
    moment_mine, moment_sent = call(
        moment_kernel,
        [shaped((rows, half), HALF)] * 2,
        (where, moment, bases, *near),
        [SMEM] + [VMEM] * 6,
        [pltpu.VMEM((rows, width), HALF)],
        flops=unit // 4,
        moved=2**22,
    )
    moment_came = shard_swap(moment_sent)
    far = list(lax.optimization_barrier((parts[2], parts[3], bases)))[:2]
    far += [dp_swap(value, 1) for value in far]
    start, start_turned, new = call(
        statistic_kernel,
        [square, square, shaped((width, half), FULL)],
        (where, bases, left_turned, stat, second, *near, *far),
        [SMEM] + [VMEM] * 4 + [ANY] * 8,
        [
            pltpu.VMEM((2, width, width), HALF),
            pltpu.VMEM((width, width), HALF),
            pltpu.SemaphoreType.DMA((8,)),
        ],
        flops=3 * unit // 2,
        moved=2**23,
    )
    new_next = dp_swap(new, 1)
    start, moment_came = lax.optimization_barrier((start, moment_came))
    back_kept, back_sent = call(
        adam_kernel,
        [shaped((rows, half), HALF)] * 2,
        (where, bases, left_turned, moment_mine, moment_came, new),
        [SMEM] + [VMEM] * 5,
        flops=unit // 2,
        moved=2**22,
    )
    start, back_sent = lax.optimization_barrier((start, back_sent))
    back_came = shard_swap(back_sent)
    back_kept_next = dp_swap(back_kept, 1)
    current, current_turned, top, second_new = pl.pallas_call(
        refresh_kernel,
        out_shape=[square, square, shaped((half, width), FULL), shaped((width, rows), FULL)],
        in_specs=[SMEM] + [VMEM] * 2 + [ANY],
        out_specs=[VMEM] * 3 + [ANY],
        scratch_shapes=[pltpu.VMEM((width, width), HALF)]
        + [pltpu.VMEM((2, width, width), HALF)] * (2 if NS_ITERS > 2 else 0)
        + [pltpu.SemaphoreType.DMA(())],
        compiler_params=pltpu.CompilerParams(vmem_limit_bytes=24 * 2**20),
        cost_estimate=pl.CostEstimate(
            flops=6 * unit, bytes_accessed=2**23, transcendentals=0
        ),
    )(where, start, start_turned, new)
    top_next = dp_swap(top, 1)
    current, back_came, back_kept_next, new_next = lax.optimization_barrier(
        (current, back_came, back_kept_next, new_next)
    )
    back_came_next = dp_swap(back_came, 1)
    side = shaped((rows, width), FULL)
    low, left_new, right_new, second_new = pl.pallas_call(
        last_kernel,
        out_shape=[shaped((half, width), FULL), side, side, shaped((width, rows), FULL)],
        in_specs=[SMEM] + [VMEM] * 2 + [ANY] * 3,
        out_specs=[VMEM] + [ANY] * 3,
        scratch_shapes=[pltpu.VMEM((half, width), HALF), pltpu.SemaphoreType.DMA((2,))],
        input_output_aliases={5: 3},
        compiler_params=pltpu.CompilerParams(vmem_limit_bytes=24 * 2**20),
        cost_estimate=pl.CostEstimate(flops=unit // 2, bytes_accessed=2**22, transcendentals=0),
    )(where, current, current_turned, top, new_next, second_new)
    low, back_came_next = lax.optimization_barrier((low, back_came_next))
    low_next = dp_swap(low, 1)
    update, left_new, right_new = pl.pallas_call(
        update_kernel,
        out_shape=[shaped((rows, width), HALF), side, side],
        in_specs=[SMEM] + [VMEM] * 5 + [ANY] * 4,
        out_specs=[ANY] * 3,
        scratch_shapes=[pltpu.VMEM((rows, width), HALF)] * 2 + [pltpu.SemaphoreType.DMA((6,))],
        input_output_aliases={8: 1, 9: 2},
        compiler_params=pltpu.CompilerParams(vmem_limit_bytes=24 * 2**20),
        cost_estimate=pl.CostEstimate(flops=unit // 2, bytes_accessed=2**22, transcendentals=0),
    )(
        where,
        back_kept,
        back_came,
        back_kept_next,
        back_came_next,
        right_turned,
        low,
        top_next,
        left_new,
        right_new,
    )
    left_new, right_new = call(
        next_side_kernel,
        [side, side],
        (where, low_next, left_new, right_new),
        [SMEM] + [ANY] * 3,
        [pltpu.SemaphoreType.DMA((1,))],
        moved=2**21,
        space=ANY,
        aliases={2: 0, 3: 1},
    )
    return (update, second_new, left_new, right_new)


def make_plain_body(n_dp, n_shard):
    def swap(value, axis, distance):
        size = n_dp if axis == "dp" else n_shard
        return lax.ppermute(value, axis, [(i, i ^ distance) for i in range(size)])

    dp_bits = []
    bit = 1
    while bit < n_dp:
        dp_bits.append(bit)
        bit *= 2

    def ordered(first_is_low, own, other, dim):
        return jnp.where(
            first_is_low,
            jnp.concatenate([own, other], dim),
            jnp.concatenate([other, own], dim),
        )

    def body(group_grads, moment, second, stat_left, stat_right, basis_left, basis_right):
        position = lax.axis_index("shard")
        member = lax.axis_index("dp")
        rows, width = moment.shape
        core = member & 1
        half = rows // 2

        def near_columns(value):
            blocks = [
                lax.dynamic_slice_in_dim(value, (position ^ k) * rows, rows, 1)
                for k in range(n_shard)
            ]
            return jnp.concatenate(blocks, 1)

        def fetch(value, distance):
            size = value.shape[0] // 2
            part = lax.dynamic_slice_in_dim(value, core * size, size, 0)
            part = swap(part, "shard", distance)
            other = swap(part, "dp", 1)
            return ordered(core == 0, part, other, 0)

        left_own = basis_left.astype(jnp.bfloat16)
        right_own = basis_right.astype(jnp.bfloat16)
        left_rot = jnp.concatenate([left_own] + [fetch(left_own, k) for k in range(1, n_shard)], 0)
        right_rot = jnp.concatenate(
            [right_own] + [fetch(right_own, k) for k in range(1, n_shard)], 0
        )

        def whole_stat(stat):
            own = near_columns(stat)
            blocks = [own[:, b * rows : (b + 1) * rows] for b in range(n_shard)]
            bands = [own]
            for k in range(1, n_shard):
                others = [b for b in range(n_shard) if b != k]
                sent = jnp.concatenate([blocks[b] for b in others], 1).astype(jnp.bfloat16)
                came = fetch(sent, k).astype(jnp.float32)
                band = [None] * n_shard
                band[0] = blocks[k].T
                for place, b in enumerate(others):
                    band[k ^ b] = came[:, place * rows : (place + 1) * rows]
                bands.append(jnp.concatenate(band, 1))
            return jnp.concatenate(bands, 0)

        stat_left_full = whole_stat(stat_left)
        stat_right_full = whole_stat(stat_right)

        part = group_grads[0]
        for bit in dp_bits:
            size = part.shape[0] // 2
            high = (member & bit) // bit
            kept = lax.dynamic_slice_in_dim(part, high * size, size, 0)
            sent = lax.dynamic_slice_in_dim(part, (1 - high) * size, size, 0)
            part = kept.astype(jnp.float32) + swap(sent, "dp", bit).astype(jnp.float32)
        chunk = part.astype(jnp.bfloat16)[None]
        chunk = jnp.concatenate([chunk] + [swap(chunk, "shard", k) for k in range(1, n_shard)], 0)
        for bit in reversed(dp_bits):
            chunk = ordered((member & bit) == 0, chunk, swap(chunk, "dp", bit), 1)
        gradient = near_columns(chunk.reshape(width, width))

        grad_rows = gradient[:rows].astype(jnp.float32)
        moment_half = (
            BETA_ONE * near_columns(moment) + (1.0 - BETA_ONE) * grad_rows
        ).astype(jnp.bfloat16)
        near_rot = near_columns(right_rot)
        moment_turned = matmul(moment_half, near_rot).astype(jnp.bfloat16)
        moment_block = jnp.concatenate(
            [moment_turned[:, :rows]]
            + [
                swap(moment_turned[:, k * rows : (k + 1) * rows], "shard", k)
                for k in range(1, n_shard)
            ],
            0,
        )
        grad_block = matmul(gradient, near_rot[:, :rows]).astype(jnp.bfloat16)
        grad_rot = matmul(left_rot, grad_block, 0) / width
        moment_rot = matmul(left_rot, moment_block, 0) / width
        second_new = BETA_TWO * second + (1.0 - BETA_TWO) * grad_rot * grad_rot
        scaled = (moment_rot / (jnp.sqrt(second_new) + EPSILON)).astype(jnp.bfloat16)
        turned_back = matmul(left_rot, scaled).astype(jnp.bfloat16)
        back_rows = jnp.concatenate(
            [turned_back[:rows]]
            + [
                swap(turned_back[k * rows : (k + 1) * rows], "shard", k)
                for k in range(1, n_shard)
            ],
            1,
        )
        update = (near_columns(matmul(back_rows, near_rot, 1, 1)) / width).astype(jnp.bfloat16)

        def refreshed(stat, product_of_grads, rot):
            stat_new = BETA_STAT * stat + (1.0 - BETA_STAT) * product_of_grads
            product = matmul(stat_new.astype(jnp.bfloat16), rot)
            start = product / jnp.sqrt(jnp.sum(product * product, axis=0) / width + NORM_EPS)
            current = start.astype(jnp.bfloat16)
            for iteration in range(NS_ITERS):
                kept = width if iteration + 1 < NS_ITERS else rows
                gram = (matmul(current[:kept], current, 1, 1) / width).astype(jnp.bfloat16)
                result = 1.5 * current[:kept].astype(jnp.float32) - 0.5 * matmul(gram, current)
                current = result.astype(jnp.bfloat16)
            return result

        left_new = refreshed(stat_left_full, matmul(gradient, gradient, 1, 1), left_rot)
        right_new = refreshed(stat_right_full, matmul(gradient, gradient, 0, 0), right_rot)
        return (update, second_new, left_new, right_new)

    return body


def solution(mesh):
    n_dp, n_shard = mesh.shape["dp"], mesh.shape["shard"]
    body = fast_body if (n_dp, n_shard) == (16, 2) else make_plain_body(n_dp, n_shard)
    return jax.shard_map(
        body,
        mesh=mesh,
        in_specs=(
            P("dp", "shard", None),
            P("shard", None),
            P(None, "shard"),
            P("shard", None),
            P("shard", None),
            P("shard", None),
            P("shard", None),
        ),
        out_specs=(P("shard", None), P(None, "shard"), P("shard", None), P("shard", None)),
        check_vma=False,
    )
```

```python
import jax
import jax.numpy as jnp
from jax import lax
from jax.experimental import pallas as pl
from jax.experimental.pallas import tpu as pltpu
from jax.sharding import PartitionSpec as P

NS_ITERS = 2


BETA_ONE = 0.9
BETA_TWO = 0.9
BETA_STAT = 0.95
EPSILON = 1e-08
NORM_EPS = 1e-06
HALF = jnp.bfloat16
FULL = jnp.float32
VMEM = pl.BlockSpec(memory_space=pltpu.VMEM)
ANY = pl.BlockSpec(memory_space=pl.ANY)
SMEM = pl.BlockSpec(memory_space=pltpu.SMEM)


def matmul(left_mat, right_mat, left_dim=1, right_dim=0):
    return lax.dot_general(
        left_mat,
        right_mat,
        (((left_dim,), (right_dim,)), ((), ())),
        preferred_element_type=FULL,
    )


def shaped(shape, dtype):
    return jax.ShapeDtypeStruct(shape, dtype)


def tile(index, size):
    return pl.ds(pl.multiple_of(index * size, size), size)


def call(
    kernel, outs, operands, specs, scratch=(), flops=0, moved=0, limit=24, space=VMEM, aliases=None
):
    return pl.pallas_call(
        kernel,
        out_shape=outs,
        in_specs=specs,
        out_specs=[space] * len(outs),
        scratch_shapes=list(scratch),
        input_output_aliases=aliases or {},
        compiler_params=pltpu.CompilerParams(vmem_limit_bytes=limit * 2**20),
        cost_estimate=pl.CostEstimate(flops=flops, bytes_accessed=moved, transcendentals=0),
    )(*operands)


def run_all(copies):
    for copy in copies:
        copy.start()
    for copy in copies:
        copy.wait()


TILES = 4
UPPER = [(i, j) for i in range(TILES) for j in range(i, TILES)]
SPLIT = len(UPPER) // 2


def pack(out, base, value):
    size = out.shape[1]
    across = value.shape[1] // size
    for band in range(value.shape[0] // size):
        for column in range(across):
            out[base + band * across + column] = value[
                band * size : (band + 1) * size, column * size : (column + 1) * size
            ].astype(HALF)


def diagonal(size):
    shape = (size, size)
    return lax.broadcasted_iota(jnp.int32, shape, 0) == lax.broadcasted_iota(jnp.int32, shape, 1)


def start_kernel(
    where,
    raw,
    came,
    left,
    right,
    stat_left,
    stat_right,
    state,
    kept,
    sent,
    basis_in,
    stat_in,
    sem,
):
    position, core, x, z = where[0], where[1], where[2], where[3]
    half, width = basis_in.shape[1:]
    size = state.shape[1]
    copies = [
        pltpu.make_async_copy(basis.at[tile(core, half)], basis_in.at[i], sem.at[i])
        for i, basis in enumerate((left, right))
    ]
    for copy in copies:
        copy.start()
    for side, stat in enumerate((stat_left, stat_right)):

        @pl.when(core == side)
        def _():
            pltpu.make_async_copy(stat.at[:, tile(position, size * TILES)], stat_in, sem.at[2]).start()

    rows = kept.shape[0]
    for out, there in ((kept, tile(x, rows)), (sent, tile(1 - x, rows))):
        out[...] = (raw[there].astype(FULL) + came[there].astype(FULL)).astype(out.dtype)
    count = half * width // size**2
    for i, copy in enumerate(copies):
        copy.wait()
        pack(state, i * count, basis_in.at[i])
    pltpu.make_async_copy(stat_left.at[:, : size * TILES], stat_in, sem.at[2]).wait()
    same = diagonal(size)
    base = 2 * count

    def tile_of(i, j):
        return stat_in[i * size : (i + 1) * size, j * size : (j + 1) * size]

    @pl.when(z % 2 == 0)
    def _():
        for place in range(SPLIT + 1):
            state[base + place] = tile_of(*UPPER[place]).astype(HALF)

    @pl.when(z % 2 == 1)
    def _():
        for place in range(SPLIT, len(UPPER)):
            state[base + place - SPLIT] = tile_of(*UPPER[place]).astype(HALF)
        for i in range(TILES):
            value = tile_of(i, i)
            low = jnp.where(same, value - value.astype(HALF).astype(FULL), 0.0)
            line = jnp.sum(low, axis=0, keepdims=True)
            state[base + SPLIT, i * 16 : (i + 1) * 16] = jnp.broadcast_to(line, (16, size)).astype(
                HALF
            )


def second_sum_kernel(where, kept, came, own, *sent):
    size = own.shape[0]
    z = where[3]
    for k, out in enumerate((own, *sent)):
        there = tile(z ^ k, size)
        out[...] = (kept[there] + came[there].astype(FULL)).astype(out.dtype)


def third_sum_kernel(own, one, two, three, out):
    out[...] = (
        (own[...] + one[...].astype(FULL)) + (two[...].astype(FULL) + three[...].astype(FULL))
    ).astype(HALF)


def joined_kernel(where, *refs):
    out = refs[-1]
    z = where[3]
    size = refs[0].shape[0]
    for k, part in enumerate(refs[:-1]):
        out[tile(z ^ k, size)] = part[...]


def place_basis(where, out, own, mine, theirs, side):
    rows, width = own.shape
    half = rows // 2
    size = mine.shape[1]
    position, core = where[0], where[1]
    across = width // size
    base = side * half * width // size**2
    out[tile(position, rows)] = own[...].astype(HALF)
    other = (1 - position) * 2
    for part, block in ((mine, other + core), (theirs, other + 1 - core)):
        for band in range(half // size):
            here = tile(block * (half // size) + band, size)
            for column in range(across):
                out[here, column * size : (column + 1) * size] = part[base + band * across + column]


def state_kernel(
    where, left, right, mine, theirs, relayed, stat_left, stat_right, bases, turned, back, full, sem
):
    rows, width = left.shape
    size = rows // TILES
    position, core = where[0], where[1]
    here, there = tile(position, rows), tile(1 - position, rows)
    for side, stat in enumerate((stat_left, stat_right)):

        @pl.when(core == side)
        def _():
            pltpu.make_async_copy(stat, full.at[here], sem).start()

    place_basis(where, bases.at[core], left, mine, theirs, 0)
    place_basis(where, bases.at[1 - core], right, mine, theirs, 1)
    turned[...] = bases[core].T
    back[...] = bases[1 - core].T
    base = (1 - position) * TILES
    first = rows * width // size**2
    same = diagonal(size)
    even = where[3] % 2 == 0
    for number, (i, j) in enumerate(UPPER):
        if number < SPLIT:
            pair = mine[first + number], relayed[number]
        elif number == SPLIT:
            pair = mine[first + SPLIT], mine[first]
        else:
            pair = relayed[number - SPLIT], mine[first + number - SPLIT]
        value = jnp.where(even, pair[0].astype(FULL), pair[1].astype(FULL))
        if i == j:
            lines = slice(i * 16, (i + 1) * 16)
            line = jnp.where(
                even,
                relayed[SPLIT, lines].astype(FULL),
                mine[first + SPLIT, lines].astype(FULL),
            )[:1]
            value = value + jnp.where(same, line, 0.0)
        full[tile(base + i, size), tile(base + j, size)] = value
        if i != j:
            full[tile(base + j, size), tile(base + i, size)] = value.T
    pltpu.make_async_copy(stat_left, full.at[here], sem).wait()
    full[there, here] = full[here, there].T


def moment_kernel(where, moment, bases, own, over_x, next_own, next_over_x, ours, others, half):
    position, core, x = where[0], where[1], where[2]
    size = own.shape[0]
    step = ours.shape[1]
    for place, part in enumerate((own, over_x, next_own, next_over_x)):
        here = tile((core ^ (place // 2)) * 2 + (x ^ (place % 2)), size)
        half[here] = (
            BETA_ONE * moment[here] + (1.0 - BETA_ONE) * part[...].astype(FULL)
        ).astype(HALF)
    there, here = tile((1 - position) * 2 + core, step), tile(position * 2 + core, step)
    others[...] = matmul(half[...], bases[1 - core, :, there]).astype(HALF)
    ours[...] = matmul(half[...], bases[1 - core, :, here]).astype(HALF)


def place_symmetric(out, here, value):
    out[: here.stop, here] = value
    if here.start:
        out[here, : here.start] = value[: here.start].T


def statistic_kernel(where, bases, turned, stat, second, *refs):
    parts, (start, start_turned, new, pair, half, sem) = refs[:-6], refs[-6:]
    position, core, x = where[0], where[1], where[2]
    width = half.shape[0]
    step = new.shape[1]
    gradient = pair.at[core]
    copies = []
    for place, part in enumerate(parts):
        size = part.shape[0]
        block = (
            (position ^ (place // 4)) * 4 + (core ^ (place // 2 % 2)) * 2 + (x ^ (place % 2))
        )
        copies.append(pltpu.make_async_copy(part, gradient.at[tile(block, size)], sem.at[place]))
    run_all(copies)
    for here in quarters(width):
        pair[1 - core, :, here] = gradient[here].T
    block = matmul(gradient[...], bases[1 - core, :, tile(position * 2 + core, step)])
    for here in reversed(quarters(width)):
        above = slice(0, here.stop)
        grads = matmul(pair[0, above], pair[1, :, here])
        value = (BETA_STAT * stat[above, here] + (1.0 - BETA_STAT) * grads).astype(HALF)
        place_symmetric(half, here, value)
    grad_rot = matmul(turned[...], block.astype(HALF)) * (1.0 / width)
    new[...] = BETA_TWO * second[:, tile(core, step)] + (1.0 - BETA_TWO) * grad_rot * grad_rot
    for here in quarters(width):
        product = matmul(half[...], bases[0, :, here])
        square = jnp.sum(product * product, axis=0, keepdims=True) * (1.0 / width)
        value = (product * lax.rsqrt(square + NORM_EPS)).astype(HALF)
        start[:, here] = value
        start_turned[here] = value.T


def adam_kernel(where, bases, turned, mine, came, new, kept, sent):
    width = new.shape[0]
    rows = mine.shape[0]
    position, core = where[0], where[1]
    here, there = tile(position, rows), tile(1 - position, rows)
    moment_rot = (
        matmul(turned[:, here], mine[...]) + matmul(turned[:, there], came[...])
    ) * (1.0 / width)
    scaled = (moment_rot / (jnp.sqrt(new[...]) + EPSILON)).astype(HALF)
    sent[...] = matmul(bases[core, there], scaled).astype(HALF)
    kept[...] = matmul(bases[core, here], scaled).astype(HALF)


def write_part(core, side, block, part, left, right, sem):
    size = part.shape[0]
    here = slice(block * size, (block + 1) * size)
    for place, out in enumerate((left, right)):

        @pl.when((core ^ side) == place)
        def _():
            pltpu.make_async_copy(part, out.at[here], sem).start()

    return pltpu.make_async_copy(part, left.at[here], sem)


def update_kernel(
    where,
    kept,
    came,
    kept_next,
    came_next,
    back,
    low,
    top_next,
    left_in,
    right_in,
    out,
    left,
    right,
    rows_back,
    product,
    sem,
):
    rows, width = out.shape
    step = kept.shape[1]
    position, core = where[0], where[1]
    copies = [
        write_part(core, 0, 1, low, left, right, sem.at[0]),
        write_part(core, 1, 0, top_next, left, right, sem.at[1]),
    ]
    for value, place in (
        (kept, position * 2 + core),
        (came, (1 - position) * 2 + core),
        (kept_next, position * 2 + 1 - core),
        (came_next, (1 - position) * 2 + 1 - core),
    ):
        rows_back[:, tile(place, step)] = value[...]
    for i, here in enumerate(quarters(width)):
        product[:, here] = (matmul(rows_back[...], back[:, here]) * (1.0 / width)).astype(HALF)
        copies.append(pltpu.make_async_copy(product.at[:, here], out.at[:, here], sem.at[2 + i]))
        copies[-1].start()
    for copy in copies:
        copy.wait()


def next_side_kernel(where, low, left_in, right_in, left, right, sem):
    write_part(where[1], 1, 1, low, left, right, sem.at[0]).wait()


def quarters(width):
    step = width // 4
    return [slice(i * step, (i + 1) * step) for i in range(4)]


def improved(current, turned, kept, gram, result, result_turned):
    size, width = result.shape
    if size == width:
        for here in reversed(quarters(width)):
            product = matmul(current[: here.stop], turned[:, here]) * (1.0 / width)
            place_symmetric(gram, here, product.astype(HALF))
    else:
        for here in quarters(width):
            product = matmul(current[kept], turned[:, here]) * (1.0 / width)
            gram[:size, here] = product.astype(HALF)
    for here in quarters(width):
        value = (
            1.5 * current[kept, here].astype(FULL) - 0.5 * matmul(gram[:size], current[:, here])
        ).astype(result.dtype)
        result[:, here] = value
        if result_turned is not None:
            result_turned[here] = value.T


def refresh_kernel(
    where, start, start_turned, new, current, turned, out, second_new, gram, *scratch
):
    width = start.shape[0]
    rows = width // 2
    between, sem = scratch[:-1], scratch[-1]
    copy = pltpu.make_async_copy(new, second_new.at[:, tile(where[1], new.shape[1])], sem)
    copy.start()
    source, source_turned = start, start_turned
    for iteration in range(NS_ITERS - 1):
        if iteration + 2 == NS_ITERS:
            result, result_turned = current, turned
        else:
            result, result_turned = between[0].at[iteration % 2], between[1].at[iteration % 2]
        improved(source, source_turned, slice(0, width), gram, result, result_turned)
        source, source_turned = result, result_turned
    improved(current, turned, tile(where[0] * 2, rows // 2), gram, out, None)
    copy.wait()


def last_kernel(
    where, current, turned, top, new_next, second_in, out, left, right, second_new, gram, sem
):
    core = where[1]
    copies = [
        write_part(core, 0, 0, top, left, right, sem.at[0]),
        pltpu.make_async_copy(
            new_next, second_new.at[:, tile(1 - core, new_next.shape[1])], sem.at[1]
        ),
    ]
    copies[1].start()
    improved(current, turned, tile(where[0] * 2 + 1, out.shape[0]), gram, out, None)
    for copy in copies:
        copy.wait()


def fast_body(group_grads, moment, second, stat_left, stat_right, basis_left, basis_right):
    position = lax.axis_index("shard")
    member = lax.axis_index("dp")
    rows, width = moment.shape
    half = rows // 2
    quarter = rows // 4
    chunk = rows // 16
    core, x, z = member & 1, (member >> 1) & 1, member >> 2
    where = jnp.stack([position, core, x, z]).astype(jnp.int32)
    unit = 2 * width**3

    def dp_swap(value, distance):
        return lax.ppermute(value, "dp", [(i, i ^ distance) for i in range(16)])

    def shard_swap(value):
        return lax.ppermute(value, "shard", [(0, 1), (1, 0)])

    def cross_swap(value):
        pairs = [(i, i ^ 5) for i in range(32)]
        return lax.ppermute(value, ("dp", "shard"), pairs)

    raw = lax.dynamic_slice_in_dim(group_grads[0], (1 - core) * half, half, 0)
    came = dp_swap(raw, 1)
    raw = lax.dynamic_slice_in_dim(group_grads[0], core * half, half, 0)
    tiles = rows * width // quarter**2
    count = tiles + SPLIT + 1
    state_sent, kept, sent = call(
        start_kernel,
        [
            shaped((count, quarter, quarter), HALF),
            shaped((quarter, width), FULL),
            shaped((quarter, width), HALF),
        ],
        (where, raw, came, basis_left, basis_right, stat_left, stat_right),
        [SMEM] + [VMEM] * 2 + [ANY] * 4,
        [
            pltpu.VMEM((2, half, width), FULL),
            pltpu.VMEM((rows, rows), FULL),
            pltpu.SemaphoreType.DMA((3,)),
        ],
        moved=2**22,
        limit=50,
    )
    came = dp_swap(sent, 2)
    state_mine = shard_swap(state_sent)
    own, *sent = call(
        second_sum_kernel,
        [shaped((chunk, width), FULL)] + [shaped((chunk, width), HALF)] * 3,
        (where, kept, came),
        [SMEM] + [VMEM] * 2,
        moved=2**20,
    )
    pieces = [dp_swap(sent[k], 4 * (k + 1)) for k in reversed(range(3))]
    (piece,) = call(
        third_sum_kernel,
        [shaped((chunk, width), HALF)],
        (own, *pieces),
        [VMEM] * 4,
        moved=2**19,
    )
    pieces = [piece] + [dp_swap(piece, 4 * k) for k in (1, 2, 3)]
    (part,) = call(
        joined_kernel,
        [shaped((quarter, width), HALF)],
        (where, *pieces),
        [SMEM] + [VMEM] * 4,
        moved=2**19,
    )
    part, state_mine = lax.optimization_barrier((part, state_mine))
    parts = [part, dp_swap(part, 2), shard_swap(part), cross_swap(part)]
    state_theirs = dp_swap(state_mine, 1)
    state_relayed = dp_swap(state_mine[tiles:], 4)
    square = shaped((width, width), HALF)
    bases, left_turned, right_turned, stat = call(
        state_kernel,
        [shaped((2, width, width), HALF), square, square, shaped((width, width), FULL)],
        (
            where,
            basis_left,
            basis_right,
            state_mine,
            state_theirs,
            state_relayed,
            stat_left,
            stat_right,
        ),
        [SMEM] + [VMEM] * 5 + [ANY] * 2,
        [pltpu.SemaphoreType.DMA(())],
        moved=2**24,
    )
    near = parts[:2] + [dp_swap(value, 1) for value in parts[:2]]
    moment_mine, moment_sent = call(
        moment_kernel,
        [shaped((rows, half), HALF)] * 2,
        (where, moment, bases, *near),
        [SMEM] + [VMEM] * 6,
        [pltpu.VMEM((rows, width), HALF)],
        flops=unit // 4,
        moved=2**22,
    )
    moment_came = shard_swap(moment_sent)
    far = list(lax.optimization_barrier((parts[2], parts[3], bases)))[:2]
    far += [dp_swap(value, 1) for value in far]
    start, start_turned, new = call(
        statistic_kernel,
        [square, square, shaped((width, half), FULL)],
        (where, bases, left_turned, stat, second, *near, *far),
        [SMEM] + [VMEM] * 4 + [ANY] * 8,
        [
            pltpu.VMEM((2, width, width), HALF),
            pltpu.VMEM((width, width), HALF),
            pltpu.SemaphoreType.DMA((8,)),
        ],
        flops=3 * unit // 2,
        moved=2**23,
    )
    new_next = dp_swap(new, 1)
    start, moment_came = lax.optimization_barrier((start, moment_came))
    back_kept, back_sent = call(
        adam_kernel,
        [shaped((rows, half), HALF)] * 2,
        (where, bases, left_turned, moment_mine, moment_came, new),
        [SMEM] + [VMEM] * 5,
        flops=unit // 2,
        moved=2**22,
    )
    start, back_sent = lax.optimization_barrier((start, back_sent))
    back_came = shard_swap(back_sent)
    back_kept_next = dp_swap(back_kept, 1)
    current, current_turned, top, second_new = pl.pallas_call(
        refresh_kernel,
        out_shape=[square, square, shaped((half, width), FULL), shaped((width, rows), FULL)],
        in_specs=[SMEM] + [VMEM] * 2 + [ANY],
        out_specs=[VMEM] * 3 + [ANY],
        scratch_shapes=[pltpu.VMEM((width, width), HALF)]
        + [pltpu.VMEM((2, width, width), HALF)] * (2 if NS_ITERS > 2 else 0)
        + [pltpu.SemaphoreType.DMA(())],
        compiler_params=pltpu.CompilerParams(vmem_limit_bytes=24 * 2**20),
        cost_estimate=pl.CostEstimate(
            flops=6 * unit, bytes_accessed=2**23, transcendentals=0
        ),
    )(where, start, start_turned, new)
    top_next = dp_swap(top, 1)
    current, back_came, back_kept_next, new_next = lax.optimization_barrier(
        (current, back_came, back_kept_next, new_next)
    )
    back_came_next = dp_swap(back_came, 1)
    side = shaped((rows, width), FULL)
    low, left_new, right_new, second_new = pl.pallas_call(
        last_kernel,
        out_shape=[shaped((half, width), FULL), side, side, shaped((width, rows), FULL)],
        in_specs=[SMEM] + [VMEM] * 2 + [ANY] * 3,
        out_specs=[VMEM] + [ANY] * 3,
        scratch_shapes=[pltpu.VMEM((half, width), HALF), pltpu.SemaphoreType.DMA((2,))],
        input_output_aliases={5: 3},
        compiler_params=pltpu.CompilerParams(vmem_limit_bytes=24 * 2**20),
        cost_estimate=pl.CostEstimate(flops=unit // 2, bytes_accessed=2**22, transcendentals=0),
    )(where, current, current_turned, top, new_next, second_new)
    low, back_came_next = lax.optimization_barrier((low, back_came_next))
    low_next = dp_swap(low, 1)
    update, left_new, right_new = pl.pallas_call(
        update_kernel,
        out_shape=[shaped((rows, width), HALF), side, side],
        in_specs=[SMEM] + [VMEM] * 5 + [ANY] * 4,
        out_specs=[ANY] * 3,
        scratch_shapes=[pltpu.VMEM((rows, width), HALF)] * 2 + [pltpu.SemaphoreType.DMA((6,))],
        input_output_aliases={8: 1, 9: 2},
        compiler_params=pltpu.CompilerParams(vmem_limit_bytes=24 * 2**20),
        cost_estimate=pl.CostEstimate(flops=unit // 2, bytes_accessed=2**22, transcendentals=0),
    )(
        where,
        back_kept,
        back_came,
        back_kept_next,
        back_came_next,
        right_turned,
        low,
        top_next,
        left_new,
        right_new,
    )
    left_new, right_new = call(
        next_side_kernel,
        [side, side],
        (where, low_next, left_new, right_new),
        [SMEM] + [ANY] * 3,
        [pltpu.SemaphoreType.DMA((1,))],
        moved=2**21,
        space=ANY,
        aliases={2: 0, 3: 1},
    )
    return (update, second_new, left_new, right_new)


def make_plain_body(n_dp, n_shard):
    def swap(value, axis, distance):
        size = n_dp if axis == "dp" else n_shard
        return lax.ppermute(value, axis, [(i, i ^ distance) for i in range(size)])

    dp_bits = []
    bit = 1
    while bit < n_dp:
        dp_bits.append(bit)
        bit *= 2

    def ordered(first_is_low, own, other, dim):
        return jnp.where(
            first_is_low,
            jnp.concatenate([own, other], dim),
            jnp.concatenate([other, own], dim),
        )

    def body(group_grads, moment, second, stat_left, stat_right, basis_left, basis_right):
        position = lax.axis_index("shard")
        member = lax.axis_index("dp")
        rows, width = moment.shape
        core = member & 1
        half = rows // 2

        def near_columns(value):
            blocks = [
                lax.dynamic_slice_in_dim(value, (position ^ k) * rows, rows, 1)
                for k in range(n_shard)
            ]
            return jnp.concatenate(blocks, 1)

        def fetch(value, distance):
            size = value.shape[0] // 2
            part = lax.dynamic_slice_in_dim(value, core * size, size, 0)
            part = swap(part, "shard", distance)
            other = swap(part, "dp", 1)
            return ordered(core == 0, part, other, 0)

        left_own = basis_left.astype(jnp.bfloat16)
        right_own = basis_right.astype(jnp.bfloat16)
        left_rot = jnp.concatenate([left_own] + [fetch(left_own, k) for k in range(1, n_shard)], 0)
        right_rot = jnp.concatenate(
            [right_own] + [fetch(right_own, k) for k in range(1, n_shard)], 0
        )

        def whole_stat(stat):
            own = near_columns(stat)
            blocks = [own[:, b * rows : (b + 1) * rows] for b in range(n_shard)]
            bands = [own]
            for k in range(1, n_shard):
                others = [b for b in range(n_shard) if b != k]
                sent = jnp.concatenate([blocks[b] for b in others], 1).astype(jnp.bfloat16)
                came = fetch(sent, k).astype(jnp.float32)
                band = [None] * n_shard
                band[0] = blocks[k].T
                for place, b in enumerate(others):
                    band[k ^ b] = came[:, place * rows : (place + 1) * rows]
                bands.append(jnp.concatenate(band, 1))
            return jnp.concatenate(bands, 0)

        stat_left_full = whole_stat(stat_left)
        stat_right_full = whole_stat(stat_right)

        part = group_grads[0]
        for bit in dp_bits:
            size = part.shape[0] // 2
            high = (member & bit) // bit
            kept = lax.dynamic_slice_in_dim(part, high * size, size, 0)
            sent = lax.dynamic_slice_in_dim(part, (1 - high) * size, size, 0)
            part = kept.astype(jnp.float32) + swap(sent, "dp", bit).astype(jnp.float32)
        chunk = part.astype(jnp.bfloat16)[None]
        chunk = jnp.concatenate([chunk] + [swap(chunk, "shard", k) for k in range(1, n_shard)], 0)
        for bit in reversed(dp_bits):
            chunk = ordered((member & bit) == 0, chunk, swap(chunk, "dp", bit), 1)
        gradient = near_columns(chunk.reshape(width, width))

        grad_rows = gradient[:rows].astype(jnp.float32)
        moment_half = (
            BETA_ONE * near_columns(moment) + (1.0 - BETA_ONE) * grad_rows
        ).astype(jnp.bfloat16)
        near_rot = near_columns(right_rot)
        moment_turned = matmul(moment_half, near_rot).astype(jnp.bfloat16)
        moment_block = jnp.concatenate(
            [moment_turned[:, :rows]]
            + [
                swap(moment_turned[:, k * rows : (k + 1) * rows], "shard", k)
                for k in range(1, n_shard)
            ],
            0,
        )
        grad_block = matmul(gradient, near_rot[:, :rows]).astype(jnp.bfloat16)
        grad_rot = matmul(left_rot, grad_block, 0) / width
        moment_rot = matmul(left_rot, moment_block, 0) / width
        second_new = BETA_TWO * second + (1.0 - BETA_TWO) * grad_rot * grad_rot
        scaled = (moment_rot / (jnp.sqrt(second_new) + EPSILON)).astype(jnp.bfloat16)
        turned_back = matmul(left_rot, scaled).astype(jnp.bfloat16)
        back_rows = jnp.concatenate(
            [turned_back[:rows]]
            + [
                swap(turned_back[k * rows : (k + 1) * rows], "shard", k)
                for k in range(1, n_shard)
            ],
            1,
        )
        update = (near_columns(matmul(back_rows, near_rot, 1, 1)) / width).astype(jnp.bfloat16)

        def refreshed(stat, product_of_grads, rot):
            stat_new = BETA_STAT * stat + (1.0 - BETA_STAT) * product_of_grads
            product = matmul(stat_new.astype(jnp.bfloat16), rot)
            start = product / jnp.sqrt(jnp.sum(product * product, axis=0) / width + NORM_EPS)
            current = start.astype(jnp.bfloat16)
            for iteration in range(NS_ITERS):
                kept = width if iteration + 1 < NS_ITERS else rows
                gram = (matmul(current[:kept], current, 1, 1) / width).astype(jnp.bfloat16)
                result = 1.5 * current[:kept].astype(jnp.float32) - 0.5 * matmul(gram, current)
                current = result.astype(jnp.bfloat16)
            return result

        left_new = refreshed(stat_left_full, matmul(gradient, gradient, 1, 1), left_rot)
        right_new = refreshed(stat_right_full, matmul(gradient, gradient, 0, 0), right_rot)
        return (update, second_new, left_new, right_new)

    return body


def solution(mesh):
    n_dp, n_shard = mesh.shape["dp"], mesh.shape["shard"]
    body = fast_body if (n_dp, n_shard) == (16, 2) else make_plain_body(n_dp, n_shard)
    return jax.shard_map(
        body,
        mesh=mesh,
        in_specs=(
            P("dp", "shard", None),
            P("shard", None),
            P(None, "shard"),
            P("shard", None),
            P("shard", None),
            P("shard", None),
            P("shard", None),
        ),
        out_specs=(P("shard", None), P(None, "shard"), P("shard", None), P("shard", None)),
        check_vma=False,
    )
```

```python
import jax
import jax.numpy as jnp
from jax import lax
from jax.experimental import pallas as pl
from jax.experimental.pallas import tpu as pltpu
from jax.sharding import PartitionSpec as P

NS_ITERS = 2


BETA_ONE = 0.9
BETA_TWO = 0.9
BETA_STAT = 0.95
EPSILON = 1e-08
NORM_EPS = 1e-06
HALF = jnp.bfloat16
FULL = jnp.float32
VMEM = pl.BlockSpec(memory_space=pltpu.VMEM)
ANY = pl.BlockSpec(memory_space=pl.ANY)
SMEM = pl.BlockSpec(memory_space=pltpu.SMEM)


def matmul(left_mat, right_mat, left_dim=1, right_dim=0):
    return lax.dot_general(
        left_mat,
        right_mat,
        (((left_dim,), (right_dim,)), ((), ())),
        preferred_element_type=FULL,
    )


def shaped(shape, dtype):
    return jax.ShapeDtypeStruct(shape, dtype)


def tile(index, size):
    return pl.ds(pl.multiple_of(index * size, size), size)


def call(
    kernel, outs, operands, specs, scratch=(), flops=0, moved=0, limit=24, space=VMEM, aliases=None
):
    return pl.pallas_call(
        kernel,
        out_shape=outs,
        in_specs=specs,
        out_specs=[space] * len(outs),
        scratch_shapes=list(scratch),
        input_output_aliases=aliases or {},
        compiler_params=pltpu.CompilerParams(vmem_limit_bytes=limit * 2**20),
        cost_estimate=pl.CostEstimate(flops=flops, bytes_accessed=moved, transcendentals=0),
    )(*operands)


def run_all(copies):
    for copy in copies:
        copy.start()
    for copy in copies:
        copy.wait()


TILES = 4
UPPER = [(i, j) for i in range(TILES) for j in range(i, TILES)]
SPLIT = len(UPPER) // 2


def pack(out, base, value):
    size = out.shape[1]
    across = value.shape[1] // size
    for band in range(value.shape[0] // size):
        for column in range(across):
            out[base + band * across + column] = value[
                band * size : (band + 1) * size, column * size : (column + 1) * size
            ].astype(HALF)


def diagonal(size):
    shape = (size, size)
    return lax.broadcasted_iota(jnp.int32, shape, 0) == lax.broadcasted_iota(jnp.int32, shape, 1)


def start_kernel(
    where,
    raw,
    came,
    left,
    right,
    stat_left,
    stat_right,
    state,
    kept,
    sent,
    basis_in,
    stat_in,
    sem,
):
    position, core, x, z = where[0], where[1], where[2], where[3]
    half, width = basis_in.shape[1:]
    size = state.shape[1]
    copies = [
        pltpu.make_async_copy(basis.at[tile(core, half)], basis_in.at[i], sem.at[i])
        for i, basis in enumerate((left, right))
    ]
    for copy in copies:
        copy.start()
    for side, stat in enumerate((stat_left, stat_right)):

        @pl.when(core == side)
        def _():
            pltpu.make_async_copy(stat.at[:, tile(position, size * TILES)], stat_in, sem.at[2]).start()

    rows = kept.shape[0]
    for out, there in ((kept, tile(x, rows)), (sent, tile(1 - x, rows))):
        out[...] = (raw[there].astype(FULL) + came[there].astype(FULL)).astype(out.dtype)
    count = half * width // size**2
    for i, copy in enumerate(copies):
        copy.wait()
        pack(state, i * count, basis_in.at[i])
    pltpu.make_async_copy(stat_left.at[:, : size * TILES], stat_in, sem.at[2]).wait()
    same = diagonal(size)
    base = 2 * count

    def tile_of(i, j):
        return stat_in[i * size : (i + 1) * size, j * size : (j + 1) * size]

    @pl.when(z % 2 == 0)
    def _():
        for place in range(SPLIT + 1):
            state[base + place] = tile_of(*UPPER[place]).astype(HALF)

    @pl.when(z % 2 == 1)
    def _():
        for place in range(SPLIT, len(UPPER)):
            state[base + place - SPLIT] = tile_of(*UPPER[place]).astype(HALF)
        for i in range(TILES):
            value = tile_of(i, i)
            low = jnp.where(same, value - value.astype(HALF).astype(FULL), 0.0)
            line = jnp.sum(low, axis=0, keepdims=True)
            state[base + SPLIT, i * 16 : (i + 1) * 16] = jnp.broadcast_to(line, (16, size)).astype(
                HALF
            )


def second_sum_kernel(where, kept, came, own, *sent):
    size = own.shape[0]
    z = where[3]
    for k, out in enumerate((own, *sent)):
        there = tile(z ^ k, size)
        out[...] = (kept[there] + came[there].astype(FULL)).astype(out.dtype)


def third_sum_kernel(own, one, two, three, out):
    out[...] = (
        (own[...] + one[...].astype(FULL)) + (two[...].astype(FULL) + three[...].astype(FULL))
    ).astype(HALF)


def joined_kernel(where, *refs):
    out = refs[-1]
    z = where[3]
    size = refs[0].shape[0]
    for k, part in enumerate(refs[:-1]):
        out[tile(z ^ k, size)] = part[...]


def place_basis(where, out, own, mine, theirs, side):
    rows, width = own.shape
    half = rows // 2
    size = mine.shape[1]
    position, core = where[0], where[1]
    across = width // size
    base = side * half * width // size**2
    out[tile(position, rows)] = own[...].astype(HALF)
    other = (1 - position) * 2
    for part, block in ((mine, other + core), (theirs, other + 1 - core)):
        for band in range(half // size):
            here = tile(block * (half // size) + band, size)
            for column in range(across):
                out[here, column * size : (column + 1) * size] = part[base + band * across + column]


def state_kernel(
    where, left, right, mine, theirs, relayed, stat_left, stat_right, bases, turned, back, full, sem
):
    rows, width = left.shape
    size = rows // TILES
    position, core = where[0], where[1]
    here, there = tile(position, rows), tile(1 - position, rows)
    for side, stat in enumerate((stat_left, stat_right)):

        @pl.when(core == side)
        def _():
            pltpu.make_async_copy(stat, full.at[here], sem).start()

    place_basis(where, bases.at[core], left, mine, theirs, 0)
    place_basis(where, bases.at[1 - core], right, mine, theirs, 1)
    turned[...] = bases[core].T
    back[...] = bases[1 - core].T
    base = (1 - position) * TILES
    first = rows * width // size**2
    same = diagonal(size)
    even = where[3] % 2 == 0
    for number, (i, j) in enumerate(UPPER):
        if number < SPLIT:
            pair = mine[first + number], relayed[number]
        elif number == SPLIT:
            pair = mine[first + SPLIT], mine[first]
        else:
            pair = relayed[number - SPLIT], mine[first + number - SPLIT]
        value = jnp.where(even, pair[0].astype(FULL), pair[1].astype(FULL))
        if i == j:
            lines = slice(i * 16, (i + 1) * 16)
            line = jnp.where(
                even,
                relayed[SPLIT, lines].astype(FULL),
                mine[first + SPLIT, lines].astype(FULL),
            )[:1]
            value = value + jnp.where(same, line, 0.0)
        full[tile(base + i, size), tile(base + j, size)] = value
        if i != j:
            full[tile(base + j, size), tile(base + i, size)] = value.T
    pltpu.make_async_copy(stat_left, full.at[here], sem).wait()
    full[there, here] = full[here, there].T


def moment_kernel(where, moment, bases, own, over_x, next_own, next_over_x, ours, others, half):
    position, core, x = where[0], where[1], where[2]
    size = own.shape[0]
    step = ours.shape[1]
    for place, part in enumerate((own, over_x, next_own, next_over_x)):
        here = tile((core ^ (place // 2)) * 2 + (x ^ (place % 2)), size)
        half[here] = (
            BETA_ONE * moment[here] + (1.0 - BETA_ONE) * part[...].astype(FULL)
        ).astype(HALF)
    there, here = tile((1 - position) * 2 + core, step), tile(position * 2 + core, step)
    others[...] = matmul(half[...], bases[1 - core, :, there]).astype(HALF)
    ours[...] = matmul(half[...], bases[1 - core, :, here]).astype(HALF)


def place_symmetric(out, here, value):
    out[: here.stop, here] = value
    if here.start:
        out[here, : here.start] = value[: here.start].T


def statistic_kernel(where, bases, turned, stat, second, *refs):
    parts, (start, start_turned, new, pair, half, sem) = refs[:-6], refs[-6:]
    position, core, x = where[0], where[1], where[2]
    width = half.shape[0]
    step = new.shape[1]
    gradient = pair.at[core]
    copies = []
    for place, part in enumerate(parts):
        size = part.shape[0]
        block = (
            (position ^ (place // 4)) * 4 + (core ^ (place // 2 % 2)) * 2 + (x ^ (place % 2))
        )
        copies.append(pltpu.make_async_copy(part, gradient.at[tile(block, size)], sem.at[place]))
    run_all(copies)
    for here in quarters(width):
        pair[1 - core, :, here] = gradient[here].T
    block = matmul(gradient[...], bases[1 - core, :, tile(position * 2 + core, step)])
    for here in reversed(quarters(width)):
        above = slice(0, here.stop)
        grads = matmul(pair[0, above], pair[1, :, here])
        value = (BETA_STAT * stat[above, here] + (1.0 - BETA_STAT) * grads).astype(HALF)
        place_symmetric(half, here, value)
    grad_rot = matmul(turned[...], block.astype(HALF)) * (1.0 / width)
    new[...] = BETA_TWO * second[:, tile(core, step)] + (1.0 - BETA_TWO) * grad_rot * grad_rot
    for here in quarters(width):
        product = matmul(half[...], bases[0, :, here])
        square = jnp.sum(product * product, axis=0, keepdims=True) * (1.0 / width)
        value = (product * lax.rsqrt(square + NORM_EPS)).astype(HALF)
        start[:, here] = value
        start_turned[here] = value.T


def adam_kernel(where, bases, turned, mine, came, new, kept, sent):
    width = new.shape[0]
    rows = mine.shape[0]
    position, core = where[0], where[1]
    here, there = tile(position, rows), tile(1 - position, rows)
    moment_rot = (
        matmul(turned[:, here], mine[...]) + matmul(turned[:, there], came[...])
    ) * (1.0 / width)
    scaled = (moment_rot / (jnp.sqrt(new[...]) + EPSILON)).astype(HALF)
    sent[...] = matmul(bases[core, there], scaled).astype(HALF)
    kept[...] = matmul(bases[core, here], scaled).astype(HALF)


def write_part(core, side, block, part, left, right, sem):
    size = part.shape[0]
    here = slice(block * size, (block + 1) * size)
    for place, out in enumerate((left, right)):

        @pl.when((core ^ side) == place)
        def _():
            pltpu.make_async_copy(part, out.at[here], sem).start()

    return pltpu.make_async_copy(part, left.at[here], sem)


def update_kernel(
    where,
    kept,
    came,
    kept_next,
    came_next,
    back,
    low,
    top_next,
    left_in,
    right_in,
    out,
    left,
    right,
    rows_back,
    product,
    sem,
):
    rows, width = out.shape
    step = kept.shape[1]
    position, core = where[0], where[1]
    copies = [
        write_part(core, 0, 1, low, left, right, sem.at[0]),
        write_part(core, 1, 0, top_next, left, right, sem.at[1]),
    ]
    for value, place in (
        (kept, position * 2 + core),
        (came, (1 - position) * 2 + core),
        (kept_next, position * 2 + 1 - core),
        (came_next, (1 - position) * 2 + 1 - core),
    ):
        rows_back[:, tile(place, step)] = value[...]
    for i, here in enumerate(quarters(width)):
        product[:, here] = (matmul(rows_back[...], back[:, here]) * (1.0 / width)).astype(HALF)
        copies.append(pltpu.make_async_copy(product.at[:, here], out.at[:, here], sem.at[2 + i]))
        copies[-1].start()
    for copy in copies:
        copy.wait()


def next_side_kernel(where, low, left_in, right_in, left, right, sem):
    write_part(where[1], 1, 1, low, left, right, sem.at[0]).wait()


def quarters(width):
    step = width // 4
    return [slice(i * step, (i + 1) * step) for i in range(4)]


def improved(current, turned, kept, gram, result, result_turned):
    size, width = result.shape
    if size == width:
        for here in reversed(quarters(width)):
            product = matmul(current[: here.stop], turned[:, here]) * (1.0 / width)
            place_symmetric(gram, here, product.astype(HALF))
    else:
        for here in quarters(width):
            product = matmul(current[kept], turned[:, here]) * (1.0 / width)
            gram[:size, here] = product.astype(HALF)
    for here in quarters(width):
        value = (
            1.5 * current[kept, here].astype(FULL) - 0.5 * matmul(gram[:size], current[:, here])
        ).astype(result.dtype)
        result[:, here] = value
        if result_turned is not None:
            result_turned[here] = value.T


def refresh_kernel(
    where, start, start_turned, new, new_next, current, turned, out, second_new, gram, *scratch
):
    width = start.shape[0]
    rows = width // 2
    between, sem = scratch[:-1], scratch[-1]
    copies = [
        pltpu.make_async_copy(value, second_new.at[:, tile(place, new.shape[1])], sem.at[i])
        for i, (value, place) in enumerate(((new, where[1]), (new_next, 1 - where[1])))
    ]
    for copy in copies:
        copy.start()
    source, source_turned = start, start_turned
    for iteration in range(NS_ITERS - 1):
        if iteration + 2 == NS_ITERS:
            result, result_turned = current, turned
        else:
            result, result_turned = between[0].at[iteration % 2], between[1].at[iteration % 2]
        improved(source, source_turned, slice(0, width), gram, result, result_turned)
        source, source_turned = result, result_turned
    improved(current, turned, tile(where[0] * 2, rows // 2), gram, out, None)
    for copy in copies:
        copy.wait()


def last_kernel(where, current, turned, top, out, left, right, gram, sem):
    copy = write_part(where[1], 0, 0, top, left, right, sem.at[0])
    improved(current, turned, tile(where[0] * 2 + 1, out.shape[0]), gram, out, None)
    copy.wait()


def fast_body(group_grads, moment, second, stat_left, stat_right, basis_left, basis_right):
    position = lax.axis_index("shard")
    member = lax.axis_index("dp")
    rows, width = moment.shape
    half = rows // 2
    quarter = rows // 4
    chunk = rows // 16
    core, x, z = member & 1, (member >> 1) & 1, member >> 2
    where = jnp.stack([position, core, x, z]).astype(jnp.int32)
    unit = 2 * width**3

    def dp_swap(value, distance):
        return lax.ppermute(value, "dp", [(i, i ^ distance) for i in range(16)])

    def shard_swap(value):
        return lax.ppermute(value, "shard", [(0, 1), (1, 0)])

    def cross_swap(value):
        pairs = [(i, i ^ 5) for i in range(32)]
        return lax.ppermute(value, ("dp", "shard"), pairs)

    raw = lax.dynamic_slice_in_dim(group_grads[0], (1 - core) * half, half, 0)
    came = dp_swap(raw, 1)
    raw = lax.dynamic_slice_in_dim(group_grads[0], core * half, half, 0)
    tiles = rows * width // quarter**2
    count = tiles + SPLIT + 1
    state_sent, kept, sent = call(
        start_kernel,
        [
            shaped((count, quarter, quarter), HALF),
            shaped((quarter, width), FULL),
            shaped((quarter, width), HALF),
        ],
        (where, raw, came, basis_left, basis_right, stat_left, stat_right),
        [SMEM] + [VMEM] * 2 + [ANY] * 4,
        [
            pltpu.VMEM((2, half, width), FULL),
            pltpu.VMEM((rows, rows), FULL),
            pltpu.SemaphoreType.DMA((3,)),
        ],
        moved=2**22,
        limit=50,
    )
    came = dp_swap(sent, 2)
    state_mine = shard_swap(state_sent)
    own, *sent = call(
        second_sum_kernel,
        [shaped((chunk, width), FULL)] + [shaped((chunk, width), HALF)] * 3,
        (where, kept, came),
        [SMEM] + [VMEM] * 2,
        moved=2**20,
    )
    pieces = [dp_swap(value, 4 * (k + 1)) for k, value in enumerate(sent)]
    (piece,) = call(
        third_sum_kernel,
        [shaped((chunk, width), HALF)],
        (own, *pieces),
        [VMEM] * 4,
        moved=2**19,
    )
    pieces = [piece] + [dp_swap(piece, 4 * k) for k in (1, 2, 3)]
    (part,) = call(
        joined_kernel,
        [shaped((quarter, width), HALF)],
        (where, *pieces),
        [SMEM] + [VMEM] * 4,
        moved=2**19,
    )
    part, state_mine = lax.optimization_barrier((part, state_mine))
    parts = [part, dp_swap(part, 2), shard_swap(part), cross_swap(part)]
    state_theirs = dp_swap(state_mine, 1)
    state_relayed = dp_swap(state_mine[tiles:], 4)
    square = shaped((width, width), HALF)
    bases, left_turned, right_turned, stat = call(
        state_kernel,
        [shaped((2, width, width), HALF), square, square, shaped((width, width), FULL)],
        (
            where,
            basis_left,
            basis_right,
            state_mine,
            state_theirs,
            state_relayed,
            stat_left,
            stat_right,
        ),
        [SMEM] + [VMEM] * 5 + [ANY] * 2,
        [pltpu.SemaphoreType.DMA(())],
        moved=2**24,
    )
    near = parts[:2] + [dp_swap(value, 1) for value in parts[:2]]
    moment_mine, moment_sent = call(
        moment_kernel,
        [shaped((rows, half), HALF)] * 2,
        (where, moment, bases, *near),
        [SMEM] + [VMEM] * 6,
        [pltpu.VMEM((rows, width), HALF)],
        flops=unit // 4,
        moved=2**22,
    )
    moment_came = shard_swap(moment_sent)
    far = list(lax.optimization_barrier((parts[2], parts[3], bases)))[:2]
    far += [dp_swap(value, 1) for value in far]
    start, start_turned, new = call(
        statistic_kernel,
        [square, square, shaped((width, half), FULL)],
        (where, bases, left_turned, stat, second, *near, *far),
        [SMEM] + [VMEM] * 4 + [ANY] * 8,
        [
            pltpu.VMEM((2, width, width), HALF),
            pltpu.VMEM((width, width), HALF),
            pltpu.SemaphoreType.DMA((8,)),
        ],
        flops=3 * unit // 2,
        moved=2**23,
    )
    new_next = dp_swap(new, 1)
    start, moment_came = lax.optimization_barrier((start, moment_came))
    back_kept, back_sent = call(
        adam_kernel,
        [shaped((rows, half), HALF)] * 2,
        (where, bases, left_turned, moment_mine, moment_came, new),
        [SMEM] + [VMEM] * 5,
        flops=6 * unit,
        moved=2**22,
    )
    start, back_sent, new_next = lax.optimization_barrier((start, back_sent, new_next))
    back_came = shard_swap(back_sent)
    back_kept_next = dp_swap(back_kept, 1)
    current, current_turned, top, second_new = pl.pallas_call(
        refresh_kernel,
        out_shape=[square, square, shaped((half, width), FULL), shaped((width, rows), FULL)],
        in_specs=[SMEM] + [VMEM] * 2 + [ANY] * 2,
        out_specs=[VMEM] * 3 + [ANY],
        scratch_shapes=[pltpu.VMEM((width, width), HALF)]
        + [pltpu.VMEM((2, width, width), HALF)] * (2 if NS_ITERS > 2 else 0)
        + [pltpu.SemaphoreType.DMA((2,))],
        compiler_params=pltpu.CompilerParams(vmem_limit_bytes=24 * 2**20),
        cost_estimate=pl.CostEstimate(
            flops=6 * unit, bytes_accessed=2**23, transcendentals=0
        ),
    )(where, start, start_turned, new, new_next)
    top_next = dp_swap(top, 1)
    current, back_came, back_kept_next = lax.optimization_barrier(
        (current, back_came, back_kept_next)
    )
    back_came_next = dp_swap(back_came, 1)
    side = shaped((rows, width), FULL)
    low, left_new, right_new = pl.pallas_call(
        last_kernel,
        out_shape=[shaped((half, width), FULL), side, side],
        in_specs=[SMEM] + [VMEM] * 2 + [ANY],
        out_specs=[VMEM] + [ANY] * 2,
        scratch_shapes=[pltpu.VMEM((half, width), HALF), pltpu.SemaphoreType.DMA((1,))],
        compiler_params=pltpu.CompilerParams(vmem_limit_bytes=24 * 2**20),
        cost_estimate=pl.CostEstimate(flops=unit // 2, bytes_accessed=2**22, transcendentals=0),
    )(where, current, current_turned, top)
    low, back_came_next = lax.optimization_barrier((low, back_came_next))
    low_next = dp_swap(low, 1)
    update, left_new, right_new = pl.pallas_call(
        update_kernel,
        out_shape=[shaped((rows, width), HALF), side, side],
        in_specs=[SMEM] + [VMEM] * 5 + [ANY] * 4,
        out_specs=[ANY] * 3,
        scratch_shapes=[pltpu.VMEM((rows, width), HALF)] * 2 + [pltpu.SemaphoreType.DMA((6,))],
        input_output_aliases={8: 1, 9: 2},
        compiler_params=pltpu.CompilerParams(vmem_limit_bytes=24 * 2**20),
        cost_estimate=pl.CostEstimate(flops=unit // 2, bytes_accessed=2**22, transcendentals=0),
    )(
        where,
        back_kept,
        back_came,
        back_kept_next,
        back_came_next,
        right_turned,
        low,
        top_next,
        left_new,
        right_new,
    )
    left_new, right_new = call(
        next_side_kernel,
        [side, side],
        (where, low_next, left_new, right_new),
        [SMEM] + [ANY] * 3,
        [pltpu.SemaphoreType.DMA((1,))],
        moved=2**21,
        space=ANY,
        aliases={2: 0, 3: 1},
    )
    return (update, second_new, left_new, right_new)


def make_plain_body(n_dp, n_shard):
    def swap(value, axis, distance):
        size = n_dp if axis == "dp" else n_shard
        return lax.ppermute(value, axis, [(i, i ^ distance) for i in range(size)])

    dp_bits = []
    bit = 1
    while bit < n_dp:
        dp_bits.append(bit)
        bit *= 2

    def ordered(first_is_low, own, other, dim):
        return jnp.where(
            first_is_low,
            jnp.concatenate([own, other], dim),
            jnp.concatenate([other, own], dim),
        )

    def body(group_grads, moment, second, stat_left, stat_right, basis_left, basis_right):
        position = lax.axis_index("shard")
        member = lax.axis_index("dp")
        rows, width = moment.shape
        core = member & 1
        half = rows // 2

        def near_columns(value):
            blocks = [
                lax.dynamic_slice_in_dim(value, (position ^ k) * rows, rows, 1)
                for k in range(n_shard)
            ]
            return jnp.concatenate(blocks, 1)

        def fetch(value, distance):
            size = value.shape[0] // 2
            part = lax.dynamic_slice_in_dim(value, core * size, size, 0)
            part = swap(part, "shard", distance)
            other = swap(part, "dp", 1)
            return ordered(core == 0, part, other, 0)

        left_own = basis_left.astype(jnp.bfloat16)
        right_own = basis_right.astype(jnp.bfloat16)
        left_rot = jnp.concatenate([left_own] + [fetch(left_own, k) for k in range(1, n_shard)], 0)
        right_rot = jnp.concatenate(
            [right_own] + [fetch(right_own, k) for k in range(1, n_shard)], 0
        )

        def whole_stat(stat):
            own = near_columns(stat)
            blocks = [own[:, b * rows : (b + 1) * rows] for b in range(n_shard)]
            bands = [own]
            for k in range(1, n_shard):
                others = [b for b in range(n_shard) if b != k]
                sent = jnp.concatenate([blocks[b] for b in others], 1).astype(jnp.bfloat16)
                came = fetch(sent, k).astype(jnp.float32)
                band = [None] * n_shard
                band[0] = blocks[k].T
                for place, b in enumerate(others):
                    band[k ^ b] = came[:, place * rows : (place + 1) * rows]
                bands.append(jnp.concatenate(band, 1))
            return jnp.concatenate(bands, 0)

        stat_left_full = whole_stat(stat_left)
        stat_right_full = whole_stat(stat_right)

        part = group_grads[0]
        for bit in dp_bits:
            size = part.shape[0] // 2
            high = (member & bit) // bit
            kept = lax.dynamic_slice_in_dim(part, high * size, size, 0)
            sent = lax.dynamic_slice_in_dim(part, (1 - high) * size, size, 0)
            part = kept.astype(jnp.float32) + swap(sent, "dp", bit).astype(jnp.float32)
        chunk = part.astype(jnp.bfloat16)[None]
        chunk = jnp.concatenate([chunk] + [swap(chunk, "shard", k) for k in range(1, n_shard)], 0)
        for bit in reversed(dp_bits):
            chunk = ordered((member & bit) == 0, chunk, swap(chunk, "dp", bit), 1)
        gradient = near_columns(chunk.reshape(width, width))

        grad_rows = gradient[:rows].astype(jnp.float32)
        moment_half = (
            BETA_ONE * near_columns(moment) + (1.0 - BETA_ONE) * grad_rows
        ).astype(jnp.bfloat16)
        near_rot = near_columns(right_rot)
        moment_turned = matmul(moment_half, near_rot).astype(jnp.bfloat16)
        moment_block = jnp.concatenate(
            [moment_turned[:, :rows]]
            + [
                swap(moment_turned[:, k * rows : (k + 1) * rows], "shard", k)
                for k in range(1, n_shard)
            ],
            0,
        )
        grad_block = matmul(gradient, near_rot[:, :rows]).astype(jnp.bfloat16)
        grad_rot = matmul(left_rot, grad_block, 0) / width
        moment_rot = matmul(left_rot, moment_block, 0) / width
        second_new = BETA_TWO * second + (1.0 - BETA_TWO) * grad_rot * grad_rot
        scaled = (moment_rot / (jnp.sqrt(second_new) + EPSILON)).astype(jnp.bfloat16)
        turned_back = matmul(left_rot, scaled).astype(jnp.bfloat16)
        back_rows = jnp.concatenate(
            [turned_back[:rows]]
            + [
                swap(turned_back[k * rows : (k + 1) * rows], "shard", k)
                for k in range(1, n_shard)
            ],
            1,
        )
        update = (near_columns(matmul(back_rows, near_rot, 1, 1)) / width).astype(jnp.bfloat16)

        def refreshed(stat, product_of_grads, rot):
            stat_new = BETA_STAT * stat + (1.0 - BETA_STAT) * product_of_grads
            product = matmul(stat_new.astype(jnp.bfloat16), rot)
            start = product / jnp.sqrt(jnp.sum(product * product, axis=0) / width + NORM_EPS)
            current = start.astype(jnp.bfloat16)
            for iteration in range(NS_ITERS):
                kept = width if iteration + 1 < NS_ITERS else rows
                gram = (matmul(current[:kept], current, 1, 1) / width).astype(jnp.bfloat16)
                result = 1.5 * current[:kept].astype(jnp.float32) - 0.5 * matmul(gram, current)
                current = result.astype(jnp.bfloat16)
            return result

        left_new = refreshed(stat_left_full, matmul(gradient, gradient, 1, 1), left_rot)
        right_new = refreshed(stat_right_full, matmul(gradient, gradient, 0, 0), right_rot)
        return (update, second_new, left_new, right_new)

    return body


def solution(mesh):
    n_dp, n_shard = mesh.shape["dp"], mesh.shape["shard"]
    body = fast_body if (n_dp, n_shard) == (16, 2) else make_plain_body(n_dp, n_shard)
    return jax.shard_map(
        body,
        mesh=mesh,
        in_specs=(
            P("dp", "shard", None),
            P("shard", None),
            P(None, "shard"),
            P("shard", None),
            P("shard", None),
            P("shard", None),
            P("shard", None),
        ),
        out_specs=(P("shard", None), P(None, "shard"), P("shard", None), P("shard", None)),
        check_vma=False,
    )
```
